32 devices in a mesh: shell: 4 (over x, core), blk: 8 (over z, y).
Axes of the slice: x: 2, y: 2, z: 4, core: 2. Of those that a mesh axis runs over, the one named last changes fastest.
Arguments:
- strain_spec: bfloat16 [6, 4, 1024, 2, 1024], P(None, 'shell', 'blk'), may hold values from -6 to 6
- order_map: int32 [1024], replicated, may hold values from 0 to 1023, as said below
- viscosity: float32 [4, 1024, 2048], P('shell', 'blk'), may hold values from 0.2 to 5
- radial_weight: float32 [4], P('shell'), may hold values from 0.3 to 3
Outputs:
- stress_spec: bfloat16 [6, 4, 1024, 2, 1024], P(None, 'shell', 'blk')
- integrated: float32 [6, 1024, 2, 1024], P(None, 'blk', None, 'shell')
The draws below stay inside these ranges and needn't reach their ends.
Inputs may be any that keep to these rules, and one draw needn't show every extreme that they name: order_map is a permutation of the orders 0 to 1023; the entries 2i and 2i + 1 hold two orders m and 1023 - m, in either order, so each device's 128 slots hold 64 such pairs.
All inputs are finite; a program needn't handle non-finite values.
Results may differ from the reference program's by a relative error of at most 0.014.
Values may be sent and summed in bfloat16 or wider, within the bound.
No kernel may reach another device: no remote copies, remote signals or barrier semaphores. Data moves between devices by JAX's collectives and lax.ppermute only.
A program may use at most 256 MiB of HBM per device.

```python
import math
import jax
import jax.numpy as jnp
from jax import lax

DEGREES = 1024
CYCLES = 1024
POINTS = 2048
COMPS = 6
SHELLS = 4


def draw_order_map(key, part):
    pair_key = jax.random.fold_in(key, 11)
    flip_key = jax.random.fold_in(key, 23)
    lower_order = jax.random.permutation(pair_key, DEGREES // 2).astype(jnp.int32)
    upper_order = DEGREES - 1 - lower_order
    flipped = jax.random.randint(flip_key, (DEGREES // 2,), 0, 2).astype(jnp.int32)
    first_slot = jnp.where(flipped == 1, upper_order, lower_order)
    second_slot = jnp.where(flipped == 1, lower_order, upper_order)
    return jnp.stack([first_slot, second_slot], axis=1).reshape(DEGREES).astype(jnp.int32)


def levels(rng, extent, shards, smallest, largest):
    factor_of = 1.0
    for dim, blocks in shards:
        draws = jax.random.uniform(jax.random.fold_in(jax.random.fold_in(rng, 6), dim), (blocks,), jnp.float32, smallest / len(shards), largest / len(shards))
        factor_of = factor_of * jnp.repeat(jnp.exp(draws), extent[dim] // blocks).reshape((-1,) + (1,) * (len(extent) - 1 - dim))
    return factor_of


def centred(own_key, dims, deviation, limit, split=(), held_as=jnp.bfloat16):
    values = deviation * jax.random.normal(own_key, dims, jnp.float32)
    if split:
        values = values * levels(own_key, dims, split, -0.22, 0.18)
    return jnp.clip(values, -limit, limit).astype(held_as)


def setup_inputs(seed: int = 0) -> dict:
    arg_keys = jax.random.split(jax.random.key(seed), 5)
    return {
        "strain_spec": centred(arg_keys[0], (COMPS, SHELLS, DEGREES, 2, DEGREES), 1.0, 6.0, ((1, 4), (2, 8))),
        "order_map": draw_order_map(jax.random.fold_in(arg_keys[4], 71), 0),
        "viscosity": jnp.clip(jnp.exp(math.log(5.0) - 3.218876 * jax.random.uniform(arg_keys[2], (SHELLS, CYCLES, POINTS), jnp.float32) ** levels(arg_keys[2], (SHELLS, CYCLES, POINTS), ((0, 4), (1, 8)), -0.2, 0.2)), 0.2, 5.0),
        "radial_weight": jnp.clip(jnp.exp(math.log(3.0) - 2.3025851 * jax.random.uniform(arg_keys[3], (SHELLS,), jnp.float32) ** levels(arg_keys[3], (SHELLS,), ((0, 4),), -0.2, 0.2)), 0.3, 3.0),
    }


two_power = 1099511627776.0
inverse_power = 1.0 / 1099511627776.0
log_jump = 40.0 * math.log(2.0)

def cycle_geometry(cycle_count):
    cycle_index = jnp.arange(cycle_count // 2, dtype=jnp.float32)
    colatitude = math.pi * (2.0 * cycle_index + 1.0) / (2.0 * cycle_count)
    return (jnp.cos(colatitude), jnp.log(jnp.sin(colatitude)))

def fejer_weights(cycle_count):
    half_count = cycle_count // 2
    cycle_index = jnp.arange(half_count, dtype=jnp.int32)
    wave_number = jnp.arange(1, half_count + 1, dtype=jnp.int32)
    phase_index = wave_number[:, None] * (2 * cycle_index[None, :] + 1) % (2 * cycle_count)
    angles = phase_index.astype(jnp.float32) * (math.pi / cycle_count)
    wave_float = wave_number.astype(jnp.float32)
    divisor = 4.0 * wave_float * wave_float - 1.0
    series = lax.optimization_barrier(jnp.sum(jnp.cos(angles) / divisor[:, None], axis=0))
    return 2.0 / cycle_count * (1.0 - 2.0 * series)

def legendre_tables(orders, cycle_count, degree_count):
    cosine, log_sine = cycle_geometry(cycle_count)
    order_int = orders.astype(jnp.int32)[:, None]
    order_float = orders.astype(jnp.float32)[:, None]
    counter = jnp.arange(1, degree_count, dtype=jnp.int32)
    counter_float = counter.astype(jnp.float32)
    factors = jnp.where(counter[None, :] <= order_int, jnp.log(1.0 - 0.5 / counter_float)[None, :], 0.0)
    log_start = 0.5 * jnp.log((2.0 * order_float + 1.0) / (4.0 * math.pi)) + 0.5 * lax.optimization_barrier(jnp.sum(factors, axis=1, keepdims=True)) + order_float * log_sine[None, :]
    even_first = order_int % 2 == 0

    def advance(carry_state, degree):
        previous, latest, log_scale = carry_state
        degree_float = degree.astype(jnp.float32)
        below_float = degree_float - 1.0
        coef_first = jnp.sqrt(jnp.maximum(4.0 * degree_float * degree_float - 1.0, 0.0) / jnp.maximum(degree_float * degree_float - order_float * order_float, 1.0))
        coef_second = jnp.sqrt(jnp.maximum(below_float * below_float - order_float * order_float, 0.0) / jnp.maximum(4.0 * below_float * below_float - 1.0, 1.0))
        current = coef_first * (cosine[None, :] * latest - coef_second * previous)
        current = jnp.where(degree == order_int + 1, jnp.sqrt(2.0 * order_float + 3.0) * cosine[None, :] * latest, current)
        current = jnp.where(degree == order_int, 1.0, current)
        current = jnp.where(degree < order_int, 0.0, current)
        result = current * jnp.exp(log_scale)
        too_large = jnp.abs(current) > two_power
        factor = jnp.where(too_large, inverse_power, 1.0)
        next_state = (latest * factor, current * factor, log_scale + jnp.where(too_large, log_jump, 0.0))
        return (next_state, result)

    def pair_step(carry_state, half_degree):
        carry_state, lower_row = advance(carry_state, 2 * half_degree)
        carry_state, upper_row = advance(carry_state, 2 * half_degree + 1)
        even_row = jnp.where(even_first, lower_row, upper_row).astype(jnp.bfloat16)
        odd_row = jnp.where(even_first, upper_row, lower_row).astype(jnp.bfloat16)
        return (carry_state, (even_row, odd_row))
    zero_rows = jnp.zeros((orders.shape[0], cycle_count // 2), jnp.float32)
    initial = (zero_rows, zero_rows, log_start + zero_rows)
    final_state, tables = lax.scan(pair_step, initial, jnp.arange(degree_count // 2, dtype=jnp.int32), unroll=32)
    return tables

def fourier_table(orders_all, point_count):
    longitudes = jnp.arange(point_count, dtype=jnp.int32)
    phase_index = orders_all.astype(jnp.int32)[:, None] * longitudes[None, :] % point_count
    angles = phase_index.astype(jnp.float32) * (2.0 * math.pi / point_count)
    return jnp.stack([jnp.cos(angles), -jnp.sin(angles)], axis=1).astype(jnp.bfloat16)

def synthesize(spectra, tables, orders):
    even_first = (orders % 2 == 0)[None, None, :, None, None]
    paired = spectra.reshape(spectra.shape[:-1] + (spectra.shape[-1] // 2, 2))
    even_part = jnp.where(even_first, paired[..., 0], paired[..., 1]).astype(jnp.float32)
    odd_part = jnp.where(even_first, paired[..., 1], paired[..., 0]).astype(jnp.float32)
    symmetric = jnp.einsum('csmri,imj->csmrj', even_part, tables[0].astype(jnp.float32))
    antisymmetric = jnp.einsum('csmri,imj->csmrj', odd_part, tables[1].astype(jnp.float32))
    north_side = symmetric + antisymmetric
    south_side = symmetric - antisymmetric
    return jnp.concatenate([north_side, jnp.flip(south_side, axis=-1)], axis=-1).astype(jnp.bfloat16)

def analyze(gridded, tables, orders, weights):
    half_count = gridded.shape[-1] // 2
    north_side = gridded[..., :half_count].astype(jnp.float32)
    south_side = jnp.flip(gridded[..., half_count:], axis=-1).astype(jnp.float32)
    even_side = (weights * (north_side + south_side)).astype(jnp.bfloat16).astype(jnp.float32)
    odd_side = (weights * (north_side - south_side)).astype(jnp.bfloat16).astype(jnp.float32)
    even_part = jnp.einsum('csmrj,imj->csmri', even_side, tables[0].astype(jnp.float32))
    odd_part = jnp.einsum('csmrj,imj->csmri', odd_side, tables[1].astype(jnp.float32))
    even_first = (orders % 2 == 0)[None, None, :, None, None]
    low_side = jnp.where(even_first, even_part, odd_part)
    high_side = jnp.where(even_first, odd_part, even_part)
    stacked = jnp.stack([low_side, high_side], axis=-1)
    return stacked.reshape(stacked.shape[:-2] + (2 * stacked.shape[-2],))

def reference(strain_spec, order_map, viscosity, radial_weight):
    component_count, shell_count, slot_count, complex_parts, degree_count = strain_spec.shape
    block_size = math.gcd(DEGREES, 64)
    block_count = slot_count // block_size
    orders_blocked = order_map.reshape(block_count, block_size)
    weights = fejer_weights(CYCLES)
    wave_table = fourier_table(order_map, POINTS).astype(jnp.float32)
    doubling = jnp.where(order_map == 0, 1.0, 2.0).astype(jnp.bfloat16)
    norm_factor = 2.0 * math.pi / POINTS
    blocked = strain_spec.reshape(component_count, shell_count, block_count, block_size, 2, degree_count)
    blocked = blocked.transpose(2, 0, 1, 3, 4, 5)

    def synth_block(packed):
        slot_piece, orders = packed
        return synthesize(slot_piece, legendre_tables(orders, CYCLES, DEGREES), orders)
    fourier = lax.map(synth_block, (blocked, orders_blocked))
    fourier = fourier.transpose(2, 1, 0, 3, 4, 5).reshape(shell_count, component_count, slot_count, 2, CYCLES)

    def cycle_shell(packed):
        gridded, shell_viscosity = packed
        scaled = (gridded * doubling[None, :, None, None]).astype(jnp.float32)
        grid_field = jnp.einsum('cmrj,mrk->cjk', scaled, wave_table)
        stress = (shell_viscosity[None] * grid_field).astype(jnp.bfloat16).astype(jnp.float32)
        spectra = jnp.einsum('cjk,mrk->cmrj', stress, wave_table)
        return (spectra * norm_factor).astype(jnp.bfloat16)
    spectrum = lax.map(cycle_shell, (fourier, viscosity))
    spectrum = spectrum.reshape(shell_count, component_count, block_count, block_size, 2, CYCLES)
    spectrum = spectrum.transpose(2, 1, 0, 3, 4, 5)

    def analysis_block(packed):
        slot_piece, orders = packed
        return analyze(slot_piece, legendre_tables(orders, CYCLES, DEGREES), orders, weights)
    coefficient = lax.map(analysis_block, (spectrum, orders_blocked))
    coefficient = coefficient.transpose(1, 2, 0, 3, 4, 5).reshape(component_count, shell_count, slot_count, 2, degree_count)
    stress_spec = coefficient.astype(jnp.bfloat16)
    integrated = lax.optimization_barrier(jnp.sum(coefficient * radial_weight[None, :, None, None, None], axis=1))
    return (stress_spec, integrated)
```

```python
import functools
import math

import jax
import jax.numpy as jnp
from jax import lax
from jax.experimental import pallas as pl
from jax.experimental.pallas import tpu as pltpu
from jax.sharding import PartitionSpec as P

two_power = 1099511627776.0
inverse_power = 1.0 / 1099511627776.0
log_jump = 40.0 * math.log(2.0)

ORD = 8
CHUNK = 64
BLOCK = 16
LANES = 128
VMEM_LIMIT = 56 * 1024 * 1024


def fejer_weights(cycle_count):
    half_count = cycle_count // 2
    cycle_index = jnp.arange(half_count, dtype=jnp.int32)
    wave_number = jnp.arange(1, half_count + 1, dtype=jnp.int32)
    phase_index = wave_number[:, None] * (2 * cycle_index[None, :] + 1) % (2 * cycle_count)
    angles = phase_index.astype(jnp.float32) * (math.pi / cycle_count)
    wave_float = wave_number.astype(jnp.float32)
    divisor = 4.0 * wave_float * wave_float - 1.0
    series = jnp.sum(jnp.cos(angles) / divisor[:, None], axis=0)
    return 2.0 / cycle_count * (1.0 - 2.0 * series)


def rank_orders(orders):
    top = orders.shape[-1]
    key = orders + (orders % 2) * (1 << 20)
    return jnp.sum((key[..., None, :] < key[..., :, None]).astype(jnp.int32), axis=-1)


def apply_rank(values, rank):
    count = rank.shape[-1]
    place = jnp.arange(count, dtype=jnp.int32)
    hit = rank[..., :, None] == place
    return jnp.sum(jnp.where(hit, values[..., :, None], 0), axis=-2)


def recursion_coefficients(sorted_orders, degree_count):
    groups = sorted_orders.shape[0] // ORD
    chunks = degree_count // CHUNK
    order = sorted_orders.astype(jnp.float32).reshape(groups, ORD, 1)
    degree = jnp.arange(degree_count, dtype=jnp.float32)[None, None, :]
    below = degree - 1.0
    coef = 4.0 * (below * below - order * order) / (4.0 * below * below - 1.0)
    coef = coef.reshape(groups, ORD, chunks, CHUNK).transpose(0, 2, 1, 3)
    gap = jnp.maximum(degree * degree - order * order, 1.0)
    ratio = jnp.where(degree > order, jnp.sqrt((degree * degree - 0.25) / gap), 1.0)
    kappa = ratio.reshape(groups, ORD, degree_count // BLOCK, BLOCK)
    step = 1
    while step < BLOCK:
        shifted = jnp.pad(kappa[..., :-step], ((0, 0),) * 3 + ((step, 0),), constant_values=1.0)
        kappa = kappa * shifted
        step *= 2
    ends = kappa[..., -1].reshape(groups, ORD, chunks, CHUNK // BLOCK).transpose(0, 2, 1, 3)
    lanes = kappa.reshape(groups, ORD, chunks, CHUNK // 2, 2).transpose(0, 2, 4, 3, 1)
    lanes = lanes.reshape(groups * chunks, CHUNK * ORD)
    counter = jnp.arange(1, degree_count, dtype=jnp.float32)
    logs = jnp.where(counter <= order, jnp.log(1.0 - 0.5 / counter), 0.0)
    start = 0.5 * jnp.log((2.0 * order + 1.0) / (4.0 * math.pi)) + 0.5 * jnp.sum(
        logs, axis=-1, keepdims=True
    )
    extra = jnp.concatenate([order, start], axis=-1)[:, None]
    extra = jnp.broadcast_to(extra, (groups, chunks, ORD, 2))
    used = CHUNK + CHUNK // BLOCK + 2
    fill = jnp.zeros((groups, chunks, ORD, LANES - used), jnp.float32)
    table = jnp.concatenate([coef, ends, extra, fill], axis=-1)
    return table.reshape(groups * chunks, ORD, LANES), lanes


def work_items(sorted_orders, degree_count):
    groups = sorted_orders.shape[0] // ORD
    chunks = degree_count // CHUNK
    first = sorted_orders.reshape(groups, ORD)[:, 0] // CHUNK
    count = chunks - first
    index = jnp.arange(groups, dtype=jnp.int32)
    upto = jnp.sum(jnp.where(index[None, :] <= index[:, None], count[None, :], 0), axis=1)
    item = jnp.arange(groups * chunks, dtype=jnp.int32)
    group = jnp.sum((item[:, None] >= upto[None, :]).astype(jnp.int32), axis=1)
    group = jnp.minimum(group, groups - 1)
    hit = group[:, None] == index[None, :]
    offset = jnp.sum(jnp.where(hit, (upto - count)[None, :], 0), axis=1)
    begin = jnp.sum(jnp.where(hit, first[None, :], 0), axis=1)
    chunk = item - offset + begin
    start = (chunk == begin).astype(jnp.int32)
    return group, jnp.minimum(chunk, chunks - 1), start, upto[-1:]


def spread_matrix():
    place = jnp.arange(CHUNK * ORD, dtype=jnp.int32)
    parity = place // (CHUNK * ORD // 2)
    degree = 2 * (place % (CHUNK * ORD // 2) // ORD) + parity
    half = jnp.arange(LANES // CHUNK, dtype=jnp.int32)[:, None, None]
    row = jnp.arange(LANES, dtype=jnp.int32)[None, :, None]
    return (row - CHUNK * half == degree[None, None, :]).astype(jnp.bfloat16)


def order_mask(kappa_row):
    shape = (2 * ORD, CHUNK * ORD)
    row_order = lax.broadcasted_iota(jnp.int32, shape, 0) // 2
    lane_order = lax.broadcasted_iota(jnp.int32, shape, 1) % ORD
    return jnp.where(row_order == lane_order, kappa_row, 0.0)


def synth_kernel(
    comps,
    groups,
    chunks,
    group_ref,
    chunk_ref,
    start_ref,
    count_ref,
    spec_ref,
    place_ref,
    coef_ref,
    kappa_ref,
    spread_ref,
    geometry_ref,
    out_ref,
    table_ref,
    sorted_ref,
    even_ref,
    odd_ref,
    prev_ref,
    last_ref,
    log_ref,
    buffer_ref,
    sems,
):
    rows = 2 * ORD
    half = CHUNK * ORD // 2
    lane_blocks = geometry_ref.shape[1] // LANES
    for c in range(comps):
        moved = jnp.dot(place_ref[...], spec_ref[c], preferred_element_type=jnp.float32)
        sorted_ref[c] = moved.astype(jnp.bfloat16)
    count = count_ref[0]

    def table_copy(item, slot):
        return pltpu.make_async_copy(buffer_ref.at[slot], table_ref.at[item], sems.at[slot])

    def body(item, carry):
        group = group_ref[item]
        chunk = chunk_ref[item]
        slot = lax.rem(item, 2)
        place = group * chunks + chunk

        @pl.when(start_ref[item] == 1)
        def _():
            even_ref[...] = jnp.zeros_like(even_ref)
            odd_ref[...] = jnp.zeros_like(odd_ref)
            prev_ref[...] = jnp.zeros_like(prev_ref)
            last_ref[...] = jnp.zeros_like(last_ref)
            head = coef_ref[place]
            order = head[:, CHUNK + CHUNK // BLOCK : CHUNK + CHUNK // BLOCK + 1]
            start = head[:, CHUNK + CHUNK // BLOCK + 1 : CHUNK + CHUNK // BLOCK + 2]
            log_ref[...] = start + order * geometry_ref[1:2, :]

        @pl.when(item >= 2)
        def _():
            table_copy(item - 2, slot).wait()

        coefs = coef_ref[place]
        order_at = CHUNK + CHUNK // BLOCK
        order = coefs[:, order_at : order_at + 1]
        seed_at = order - (chunk * CHUNK).astype(jnp.float32)
        twice = geometry_ref[0:1, :]
        prev = prev_ref[...]
        last = last_ref[...]
        logs = log_ref[...]
        for b in range(CHUNK // BLOCK):
            scale = jnp.exp(logs)
            held = []
            for i in range(BLOCK):
                step = b * BLOCK + i
                now = twice * last - coefs[:, step : step + 1] * prev
                now = jnp.where(seed_at == float(step), 1.0, now)
                held.append(now * scale)
                prev, last = last, now
            for p in range(2):
                for i in range(p, BLOCK, 4):
                    pair = jnp.concatenate([held[i], held[i + 2]], axis=0).astype(jnp.bfloat16)
                    at = (b * BLOCK + i - p) // 2 * ORD
                    buffer_ref[slot, p, at : at + 2 * ORD, :] = pair
            end = coefs[:, CHUNK + b : CHUNK + b + 1]
            last = last * end
            prev = prev * end
            large = jnp.abs(last) > two_power
            factor = jnp.where(large, inverse_power, 1.0)
            last = last * factor
            prev = prev * factor
            logs = logs + jnp.where(large, log_jump, 0.0)
        prev_ref[...] = prev
        last_ref[...] = last
        log_ref[...] = logs
        table_copy(item, slot).start()

        at = pl.multiple_of(group * rows, rows)
        lane = pl.multiple_of(chunk // (LANES // CHUNK) * LANES, LANES)
        piece = jnp.concatenate(
            [sorted_ref[c, pl.ds(at, rows), pl.ds(lane, LANES)] for c in range(comps)], axis=0
        )
        spread = spread_ref[lax.rem(chunk, LANES // CHUNK)]
        wide = jnp.dot(piece, spread, preferred_element_type=jnp.float32)
        mask = order_mask(kappa_ref[pl.ds(place, 1), :])
        wide = jnp.concatenate(
            [wide[c * rows : (c + 1) * rows] * mask for c in range(comps)], axis=0
        ).astype(jnp.bfloat16)
        even_ref[...] += jnp.dot(
            wide[:, :half], buffer_ref[slot, 0], preferred_element_type=jnp.float32
        )
        odd_ref[...] += jnp.dot(
            wide[:, half:], buffer_ref[slot, 1], preferred_element_type=jnp.float32
        )

        @pl.when(chunk == chunks - 1)
        def _():
            sign = jnp.where(group < groups // 2, 1.0, -1.0)
            for c in range(comps):
                even = even_ref[c * rows : (c + 1) * rows, :]
                odd = odd_ref[c * rows : (c + 1) * rows, :]
                north = (even + odd).astype(jnp.bfloat16)
                south = (sign * (even - odd)).astype(jnp.bfloat16)
                for b in range(lane_blocks):
                    lanes = slice(b * LANES, (b + 1) * LANES)
                    out_ref[b, c, group] = north[:, lanes]
                    out_ref[2 * lane_blocks - 1 - b, c, group] = south[:, lanes]

        return carry

    lax.fori_loop(0, count, body, 0)
    for back in (2, 1):
        item = count - back
        table_copy(item, lax.rem(item, 2)).wait()


def analysis_kernel(
    comps,
    groups,
    chunks,
    group_ref,
    chunk_ref,
    start_ref,
    count_ref,
    grid_ref,
    table_ref,
    place_ref,
    kappa_ref,
    spread_ref,
    weight_ref,
    out_ref,
    sorted_ref,
    even_ref,
    odd_ref,
    buffer_ref,
    sems,
):
    rows = 2 * ORD
    half = CHUNK * ORD // 2
    lane_blocks = weight_ref.shape[1] // LANES
    count = count_ref[0]
    sorted_ref[...] = jnp.zeros_like(sorted_ref)

    def table_copy(item, slot):
        return pltpu.make_async_copy(table_ref.at[item], buffer_ref.at[slot], sems.at[slot])

    table_copy(0, 0).start()

    def body(item, carry):
        group = group_ref[item]
        chunk = chunk_ref[item]
        slot = lax.rem(item, 2)
        place = group * chunks + chunk

        @pl.when(item + 1 < count)
        def _():
            table_copy(item + 1, 1 - slot).start()

        @pl.when(start_ref[item] == 1)
        def _():
            sign = jnp.where(group < groups // 2, 1.0, -1.0)
            for b in range(lane_blocks):
                lanes = slice(b * LANES, (b + 1) * LANES)
                weight = weight_ref[:, lanes]
                for c in range(comps):
                    north = grid_ref[b, c, group].astype(jnp.float32)
                    south = sign * grid_ref[2 * lane_blocks - 1 - b, c, group].astype(jnp.float32)
                    at = slice(c * rows, (c + 1) * rows)
                    even_ref[at, lanes] = (weight * (north + south)).astype(jnp.bfloat16)
                    odd_ref[at, lanes] = (weight * (north - south)).astype(jnp.bfloat16)

        table_copy(item, slot).wait()
        contract = (((1,), (1,)), ((), ()))
        wide_even = lax.dot_general(
            even_ref[...], buffer_ref[slot, 0], contract, preferred_element_type=jnp.float32
        )
        wide_odd = lax.dot_general(
            odd_ref[...], buffer_ref[slot, 1], contract, preferred_element_type=jnp.float32
        )
        mask = order_mask(kappa_ref[pl.ds(place, 1), :])
        wide = jnp.concatenate(
            [
                jnp.concatenate(
                    [
                        wide_even[c * rows : (c + 1) * rows] * mask[:, :half],
                        wide_odd[c * rows : (c + 1) * rows] * mask[:, half:],
                    ],
                    axis=1,
                )
                for c in range(comps)
            ],
            axis=0,
        ).astype(jnp.bfloat16)
        spread = spread_ref[lax.rem(chunk, LANES // CHUNK)]
        narrow = lax.dot_general(wide, spread, contract, preferred_element_type=jnp.float32)
        narrow = narrow.astype(jnp.bfloat16)
        at = pl.multiple_of(group * rows, rows)
        lane = pl.multiple_of(chunk // (LANES // CHUNK) * LANES, LANES)
        for c in range(comps):
            where = (c, pl.ds(at, rows), pl.ds(lane, LANES))
            sorted_ref[where] = sorted_ref[where] + narrow[c * rows : (c + 1) * rows]
        return carry

    lax.fori_loop(0, count, body, 0)
    for c in range(comps):
        moved = jnp.dot(place_ref[...], sorted_ref[c], preferred_element_type=jnp.float32)
        out_ref[c] = moved.astype(jnp.bfloat16)


def grid_kernel(
    norm, packs, grid_ref, forward_ref, backward_ref, viscosity_ref, out_ref, field_ref, stress_ref
):
    blocks, _, groups, rows, lanes = grid_ref.shape
    half_groups = groups // 2
    depth = blocks * half_groups * rows
    points = forward_ref.shape[1]
    tile = 256
    width = packs * lanes
    for w in range(packs):
        for p in range(2):
            for d in range(blocks):
                piece = grid_ref[d, w, p * half_groups : (p + 1) * half_groups]
                field_ref[
                    p,
                    d * half_groups * rows : (d + 1) * half_groups * rows,
                    w * lanes : (w + 1) * lanes,
                ] = piece.reshape(half_groups * rows, lanes)

    def points_step(i, carry):
        at = pl.multiple_of(i * tile, tile)
        even = jnp.dot(
            forward_ref[0, pl.ds(at, tile), :], field_ref[0], preferred_element_type=jnp.float32
        )
        odd = jnp.dot(
            forward_ref[1, pl.ds(at, tile), :], field_ref[1], preferred_element_type=jnp.float32
        )
        near = viscosity_ref[pl.ds(at, tile), :]
        far = viscosity_ref[pl.ds(points + at, tile), :]
        if packs > 1:
            near = jnp.concatenate([near] * packs, axis=1)
            far = jnp.concatenate([far] * packs, axis=1)
        near = (near * (even + odd)).astype(jnp.bfloat16).astype(jnp.float32)
        far = (far * (even - odd)).astype(jnp.bfloat16).astype(jnp.float32)
        stress_ref[0, pl.ds(at, tile), :] = (near + far).astype(jnp.bfloat16)
        stress_ref[1, pl.ds(at, tile), :] = (near - far).astype(jnp.bfloat16)
        return carry

    lax.fori_loop(0, points // tile, points_step, 0)
    step_rows = half_groups * rows

    def orders_step(d, carry):
        at = pl.multiple_of(d * step_rows, step_rows)
        for p in range(2):
            found = jnp.dot(
                backward_ref[p, pl.ds(at, step_rows), :],
                stress_ref[p],
                preferred_element_type=jnp.float32,
            )
            found = (found * norm).astype(jnp.bfloat16)
            for w in range(packs):
                out_ref[d, w, p * half_groups : (p + 1) * half_groups] = found[
                    :, w * lanes : (w + 1) * lanes
                ].reshape(half_groups, rows, lanes)
        return carry

    lax.fori_loop(0, blocks, orders_step, 0)


def whole(shape):
    return pl.BlockSpec(shape, lambda *_: (0,) * len(shape))


def run_synth(items, spectra, place, coefs, kappa, spread, geometry, groups, chunks):
    comps, slots, degrees = spectra.shape
    half_cycles = geometry.shape[1]
    blocks = 2 * half_cycles // LANES
    rows = 2 * ORD
    half = CHUNK * ORD // 2
    smem = pl.BlockSpec(memory_space=pltpu.SMEM)
    vmem = pl.BlockSpec(memory_space=pltpu.VMEM)
    return pl.pallas_call(
        functools.partial(synth_kernel, comps, groups, chunks),
        out_shape=(
            jax.ShapeDtypeStruct((blocks, comps, groups, rows, LANES), jnp.bfloat16),
            jax.ShapeDtypeStruct((groups * chunks, 2, half, half_cycles), jnp.bfloat16),
        ),
        in_specs=[smem] * 4 + [vmem] * 6,
        out_specs=(vmem, pl.BlockSpec(memory_space=pl.ANY)),
        scratch_shapes=[
            pltpu.VMEM((comps, slots, degrees), jnp.bfloat16),
            pltpu.VMEM((comps * rows, half_cycles), jnp.float32),
            pltpu.VMEM((comps * rows, half_cycles), jnp.float32),
            pltpu.VMEM((ORD, half_cycles), jnp.float32),
            pltpu.VMEM((ORD, half_cycles), jnp.float32),
            pltpu.VMEM((ORD, half_cycles), jnp.float32),
            pltpu.VMEM((2, 2, half, half_cycles), jnp.bfloat16),
            pltpu.SemaphoreType.DMA((2,)),
        ],
        compiler_params=pltpu.CompilerParams(vmem_limit_bytes=VMEM_LIMIT),
        name="synthesis",
    )(*items, spectra, place, coefs, kappa, spread, geometry)


def run_analysis(items, gridded, table, place, kappa, spread, weights, degrees, groups, chunks):
    blocks, comps, _, rows, _ = gridded.shape
    half_cycles = weights.shape[1]
    half = CHUNK * ORD // 2
    slots = place.shape[0]
    smem = pl.BlockSpec(memory_space=pltpu.SMEM)
    vmem = pl.BlockSpec(memory_space=pltpu.VMEM)
    return pl.pallas_call(
        functools.partial(analysis_kernel, comps, groups, chunks),
        out_shape=jax.ShapeDtypeStruct((comps, slots, degrees), jnp.bfloat16),
        in_specs=[smem] * 4 + [vmem, pl.BlockSpec(memory_space=pl.ANY)] + [vmem] * 4,
        out_specs=vmem,
        scratch_shapes=[
            pltpu.VMEM((comps, slots, degrees), jnp.bfloat16),
            pltpu.VMEM((comps * rows, half_cycles), jnp.bfloat16),
            pltpu.VMEM((comps * rows, half_cycles), jnp.bfloat16),
            pltpu.VMEM((2, 2, half, half_cycles), jnp.bfloat16),
            pltpu.SemaphoreType.DMA((2,)),
        ],
        compiler_params=pltpu.CompilerParams(vmem_limit_bytes=VMEM_LIMIT),
        name="analysis",
    )(*items, gridded, table, place, kappa, spread, weights)


def run_grid(received, forward, backward, viscosity, norm):
    blocks, comps, groups, rows, lanes = received.shape
    packs = 2 if comps % 2 == 0 else 1
    depth = blocks * groups // 2 * rows
    half_points = forward.shape[1]
    part = pl.BlockSpec((blocks, packs, groups, rows, lanes), lambda i: (0, i, 0, 0, 0))
    return pl.pallas_call(
        functools.partial(grid_kernel, norm, packs),
        out_shape=jax.ShapeDtypeStruct(received.shape, jnp.bfloat16),
        grid=(comps // packs,),
        in_specs=[part, whole(forward.shape), whole(backward.shape), whole(viscosity.shape)],
        out_specs=part,
        scratch_shapes=[
            pltpu.VMEM((2, depth, packs * lanes), jnp.bfloat16),
            pltpu.VMEM((2, half_points, packs * lanes), jnp.bfloat16),
        ],
        compiler_params=pltpu.CompilerParams(vmem_limit_bytes=VMEM_LIMIT),
        name="grid_transforms",
    )(received, forward, backward, viscosity)


def wave_tables(sorted_all, point_count, groups):
    blocks = sorted_all.shape[0]
    orders = sorted_all.reshape(blocks, 2, groups // 2, ORD).transpose(1, 0, 2, 3).reshape(2, -1)
    shift = jnp.arange(2, dtype=jnp.int32) * (point_count // 4)
    longitudes = jnp.arange(point_count // 2, dtype=jnp.int32)

    def values(phase):
        angles = (phase % point_count).astype(jnp.float32) * (2.0 * math.pi / point_count)
        return jnp.cos(angles).astype(jnp.bfloat16)

    rows = (2, orders.shape[1] * 2)
    order_rows = jnp.broadcast_to(orders[:, :, None], orders.shape + (2,)).reshape(rows)
    shift_rows = jnp.broadcast_to(shift, orders.shape + (2,)).reshape(rows)
    backward = values(order_rows[:, :, None] * longitudes + shift_rows[:, :, None])
    forward = values(order_rows[:, None, :] * longitudes[:, None] + shift_rows[:, None, :])
    return forward, backward


def to_blocks(gridded, cycle_local):
    blocks, comps, groups, rows, _ = gridded.shape
    share = LANES // cycle_local
    if share == 1:
        return gridded
    cut = gridded.reshape(2, blocks // 2, comps, groups, rows, share, cycle_local)
    cut = cut.transpose(0, 1, 5, 2, 3, 4, 6)
    cut = jnp.stack([cut[0], jnp.flip(cut[1], axis=1)])
    return cut.reshape(blocks * share, comps, groups, rows, cycle_local)


def from_blocks(gridded, cycle_local):
    blocks, comps, groups, rows, _ = gridded.shape
    share = LANES // cycle_local
    if share == 1:
        return gridded
    cut = gridded.reshape(2, blocks // share // 2, share, comps, groups, rows, cycle_local)
    cut = jnp.stack([cut[0], jnp.flip(cut[1], axis=1)])
    cut = cut.transpose(0, 1, 3, 4, 5, 2, 6)
    return cut.reshape(blocks // share, comps, groups, rows, LANES)


def pack_comps(gridded):
    blocks, comps, groups, rows, cycle_local = gridded.shape
    if cycle_local == LANES:
        return gridded
    side = gridded.transpose(0, 2, 3, 1, 4).reshape(blocks, 1, groups, rows, comps * cycle_local)
    extra = -(comps * cycle_local) % LANES
    return jnp.pad(side, ((0, 0),) * 4 + ((0, extra),))


def unpack_comps(gridded, comps, cycle_local):
    if cycle_local == LANES:
        return gridded
    blocks, _, groups, rows, _ = gridded.shape
    side = gridded[..., : comps * cycle_local]
    side = side.reshape(blocks, groups, rows, comps, cycle_local)
    return side.transpose(0, 3, 1, 2, 4)


def shards(strain_spec, order_map, viscosity, radial_weight):
    comps, shells, slots, parts, degrees = strain_spec.shape
    block_count = lax.axis_size("blk")
    block = lax.axis_index("blk")
    cycle_local = viscosity.shape[1]
    cycle_count = cycle_local * block_count
    half_cycles = cycle_count // 2
    points = viscosity.shape[2]
    groups = slots // ORD
    chunks = degrees // CHUNK

    rank_all = rank_orders(order_map.reshape(block_count, slots))
    sorted_all = apply_rank(order_map.reshape(block_count, slots), rank_all)
    rank = lax.dynamic_index_in_dim(rank_all, block, 0, keepdims=False)
    sorted_orders = lax.dynamic_index_in_dim(sorted_all, block, 0, keepdims=False)
    items = work_items(sorted_orders, degrees)
    coefs, kappa = recursion_coefficients(sorted_orders, degrees)
    spread = spread_matrix()

    cycle_index = jnp.arange(half_cycles, dtype=jnp.float32)
    colatitude = math.pi * (2.0 * cycle_index + 1.0) / (2.0 * cycle_count)
    geometry = jnp.stack([2.0 * jnp.cos(colatitude), jnp.log(jnp.sin(colatitude))])

    row_rank = (rank[:, None] * 2 + jnp.arange(2, dtype=jnp.int32)).reshape(-1)
    place = jnp.arange(slots * 2, dtype=jnp.int32)
    hit = row_rank[None, :] == place[:, None]
    my_orders = lax.dynamic_index_in_dim(
        order_map.reshape(block_count, slots), block, 0, keepdims=False
    )
    doubling = jnp.repeat(jnp.where(my_orders == 0, 1.0, 2.0), 2)
    place_in = jnp.where(hit, doubling[None, :], 0.0).astype(jnp.bfloat16)
    place_out = hit.T.astype(jnp.bfloat16)

    spectra = strain_spec.reshape(comps, slots * parts, degrees)
    gridded, table = run_synth(
        items, spectra, place_in, coefs, kappa, spread, geometry, groups, chunks
    )
    received = lax.all_to_all(to_blocks(gridded, cycle_local), "blk", 0, 0, tiled=True)

    forward, backward = wave_tables(sorted_all, points, groups)
    weights = fejer_weights(cycle_count)[None, :]
    mirror = jnp.arange(cycle_local, dtype=jnp.int32)
    mirror = jnp.where(block * 2 < block_count, mirror, cycle_local - 1 - mirror)
    turn = (mirror[None, :] == jnp.arange(cycle_local, dtype=jnp.int32)[:, None]).astype(jnp.float32)
    local = jnp.einsum("jk,ji->ki", viscosity[0], turn, precision=lax.Precision.HIGHEST)
    if cycle_local < LANES:
        local = jnp.concatenate([local] * comps, axis=1)
        local = jnp.pad(local, ((0, 0), (0, -local.shape[1] % LANES)))
    spectrum = run_grid(pack_comps(received), forward, backward, local, 2.0 * math.pi / points)
    spectrum = unpack_comps(spectrum, comps, cycle_local)
    returned = lax.all_to_all(spectrum, "blk", 0, 0, tiled=True)

    stress = run_analysis(
        items,
        from_blocks(returned, cycle_local),
        table,
        place_out,
        kappa,
        spread,
        weights,
        degrees,
        groups,
        chunks,
    )
    shell_count = lax.axis_size("shell")
    all_weights = lax.all_gather(radial_weight, "shell").reshape(shell_count)
    cut = stress.reshape(comps, slots * parts, shell_count, degrees // shell_count)
    shared = lax.all_to_all(cut.transpose(2, 0, 1, 3), "shell", 0, 0, tiled=True)
    integrated = jnp.sum(shared.astype(jnp.float32) * all_weights[:, None, None, None], axis=0)
    stress_spec = stress.reshape(strain_spec.shape)
    return (stress_spec, integrated.reshape(comps, slots, parts, degrees // shell_count))


def solution(mesh):
    return jax.shard_map(
        shards,
        mesh=mesh,
        in_specs=(P(None, "shell", "blk", None, None), P(), P("shell", "blk", None), P("shell")),
        out_specs=(P(None, "shell", "blk", None, None), P(None, "blk", None, "shell")),
        check_vma=False,
    )
```

```python
import functools
import math

import jax
import jax.numpy as jnp
from jax import lax
from jax.experimental import pallas as pl
from jax.experimental.pallas import tpu as pltpu
from jax.sharding import PartitionSpec as P

two_power = 1099511627776.0
inverse_power = 1.0 / 1099511627776.0
log_jump = 40.0 * math.log(2.0)

ORD = 8
CHUNK = 64
BLOCK = 16
LANES = 128
SLOTS = 4
PARTS = 2
VMEM_LIMIT = 56 * 1024 * 1024


def fejer_weights(cycle_count):
    half_count = cycle_count // 2
    cycle_index = jnp.arange(half_count, dtype=jnp.int32)
    wave_number = jnp.arange(1, half_count + 1, dtype=jnp.int32)
    phase_index = wave_number[:, None] * (2 * cycle_index[None, :] + 1) % (2 * cycle_count)
    angles = phase_index.astype(jnp.float32) * (math.pi / cycle_count)
    wave_float = wave_number.astype(jnp.float32)
    divisor = 4.0 * wave_float * wave_float - 1.0
    series = jnp.sum(jnp.cos(angles) / divisor[:, None], axis=0)
    return 2.0 / cycle_count * (1.0 - 2.0 * series)


def rank_orders(orders):
    top = orders.shape[-1]
    key = orders + (orders % 2) * (1 << 20)
    return jnp.sum((key[..., None, :] < key[..., :, None]).astype(jnp.int32), axis=-1)


def apply_rank(values, rank):
    count = rank.shape[-1]
    place = jnp.arange(count, dtype=jnp.int32)
    hit = rank[..., :, None] == place
    return jnp.sum(jnp.where(hit, values[..., :, None], 0), axis=-2)


def lane_fill(values):
    return jnp.broadcast_to(values.reshape(-1, ORD, 1), (values.shape[0] // ORD, ORD, LANES))


def spread_matrix():
    place = jnp.arange(CHUNK * ORD, dtype=jnp.int32)
    parity = place // (CHUNK * ORD // 2)
    degree = 2 * (place % (CHUNK * ORD // 2) // ORD) + parity
    half = jnp.arange(LANES // CHUNK, dtype=jnp.int32)[:, None, None]
    row = jnp.arange(LANES, dtype=jnp.int32)[None, :, None]
    return (row - CHUNK * half == degree[None, None, :]).astype(jnp.bfloat16)


def gather_matrix():
    return spread_matrix()[0, :CHUNK, :]


def degree_rows(degree_count):
    below = jnp.arange(degree_count, dtype=jnp.float32) - 1.0
    bottom = 4.0 * below * below - 1.0
    rows = jnp.stack([4.0 * below * below / bottom, 4.0 / bottom])
    return jnp.broadcast_to(rows[:, :, None], (2, degree_count, LANES))


def kappa_lanes(order):
    lane = lax.broadcasted_iota(jnp.int32, order.shape, 1)
    degree = lane.astype(jnp.float32)
    square = degree * degree
    gap = jnp.maximum(square - order * order, 1.0)
    kappa = jnp.where(degree > order, jnp.sqrt((square - 0.25) / gap), 1.0)
    step = 1
    while step < BLOCK:
        moved = pltpu.roll(kappa, step, 1)
        kappa = kappa * jnp.where(lane % BLOCK >= step, moved, 1.0)
        step *= 2
    return kappa


def synth_kernel(
    comps,
    groups,
    chunks,
    sign,
    first_ref,
    last_ref,
    spec_ref,
    place_ref,
    order_ref,
    start_ref,
    degree_ref,
    spread_ref,
    geometry_ref,
    out_ref,
    table_ref,
    kappa_ref,
    sorted_ref,
    even_ref,
    odd_ref,
    prev_ref,
    last_row_ref,
    log_ref,
    end_ref,
    wide_ref,
    buffer_ref,
    sems,
):
    rows = 2 * ORD
    half = CHUNK * ORD // 2
    lane_blocks = geometry_ref.shape[1] // LANES
    for c in range(comps):
        moved = jnp.dot(place_ref[...], spec_ref[c], preferred_element_type=jnp.float32)
        sorted_ref[c] = moved.astype(jnp.bfloat16)
    degrees = chunks * CHUNK
    batch = math.gcd(groups, 4)

    def fill_kappa(i, carry):
        order = order_ref[pl.ds(i * batch, batch)].reshape(batch * ORD, LANES)
        kappa = kappa_lanes(jnp.concatenate([order] * (degrees // LANES), axis=1))
        kappa = kappa.reshape(batch, ORD, degrees)
        kappa_ref[pl.ds(i * batch, batch)] = kappa
        for b in range(degrees // BLOCK):
            end = kappa[:, :, (b + 1) * BLOCK - 1 : (b + 1) * BLOCK]
            end_ref[pl.ds(i * batch, batch), b] = jnp.broadcast_to(end, (batch, ORD, LANES))
        return carry

    lax.fori_loop(0, groups // batch, fill_kappa, 0)
    shape = (rows, CHUNK * ORD)
    row_order = lax.broadcasted_iota(jnp.int32, shape, 0) % ORD
    lane_order = lax.broadcasted_iota(jnp.int32, shape, 1) % ORD
    mask = jnp.where(row_order == lane_order, 1.0, 0.0)
    count = lax.fori_loop(0, groups, lambda g, n: n + chunks - first_ref[g], jnp.int32(0))
    even_ref[...] = jnp.zeros_like(even_ref)
    odd_ref[...] = jnp.zeros_like(odd_ref)
    wide_ref[...] = jnp.zeros_like(wide_ref)
    buffer_ref[SLOTS - 1] = jnp.zeros_like(buffer_ref[SLOTS - 1])

    def table_copies(item, slot):
        return [
            pltpu.make_async_copy(
                buffer_ref.at[slot, p], table_ref.at[item, p], sems.at[slot, p]
            )
            for p in range(2)
        ]

    def products(slot):
        even_ref[...] += jnp.dot(
            wide_ref[:, :half], buffer_ref[slot, 0], preferred_element_type=jnp.float32
        )
        odd_ref[...] += jnp.dot(
            wide_ref[:, half:], buffer_ref[slot, 1], preferred_element_type=jnp.float32
        )

    def recursion(seeded, group, chunk, slot):
        order = order_ref[group]
        begin = chunk * CHUNK
        odd_chunk = lax.rem(chunk, LANES // CHUNK)
        lane = pl.multiple_of((chunk - odd_chunk) * CHUNK, LANES)
        kappa = kappa_ref[group, :, pl.ds(lane, LANES)]
        square = order * order
        seed_at = jnp.concatenate([order - begin.astype(jnp.float32)] * lane_blocks, axis=1)
        twice = geometry_ref[0:1, :]
        prev = prev_ref[...]
        last = last_row_ref[...]
        logs = log_ref[...]
        for b in range(CHUNK // BLOCK):
            scale = jnp.exp(logs)
            held = []
            for i in range(BLOCK):
                step = b * BLOCK + i
                one = degree_ref[0, pl.ds(begin + step, 1), :]
                two = degree_ref[1, pl.ds(begin + step, 1), :]
                coef = jnp.concatenate([one - two * square] * lane_blocks, axis=1)
                now = twice * last - coef * prev
                if seeded:
                    now = jnp.where(seed_at == float(step), 1.0, now)
                held.append(now * scale)
                prev, last = last, now
            for p in range(2):
                for i in range(p, BLOCK, 4):
                    pair = jnp.concatenate([held[i], held[i + 2]], axis=0).astype(jnp.bfloat16)
                    at = (b * BLOCK + i - p) // 2 * ORD
                    buffer_ref[slot, p, at : at + 2 * ORD, :] = pair
            end = end_ref[group, chunk * (CHUNK // BLOCK) + b]
            end = jnp.concatenate([end] * lane_blocks, axis=1)
            last = last * end
            prev = prev * end
            large = jnp.abs(last) > two_power
            factor = jnp.where(large, inverse_power, 1.0)
            last = last * factor
            prev = prev * factor
            logs = logs + jnp.where(large, log_jump, 0.0)
        prev_ref[...] = prev
        last_row_ref[...] = last
        log_ref[...] = logs
        at = pl.multiple_of(group * rows, rows)
        factors = jnp.concatenate([kappa, kappa], axis=0)
        piece = jnp.concatenate(
            [
                (sorted_ref[c, pl.ds(at, rows), pl.ds(lane, LANES)] * factors).astype(jnp.bfloat16)
                for c in range(comps)
            ],
            axis=0,
        )
        wide = jnp.dot(piece, spread_ref[odd_chunk], preferred_element_type=jnp.float32)
        for c in range(comps):
            at = slice(c * rows, (c + 1) * rows)
            wide_ref[at, :] = (wide[at] * mask).astype(jnp.bfloat16)

    def finish(group):
        for c in range(comps):
            even = even_ref[c * rows : (c + 1) * rows, :]
            odd = odd_ref[c * rows : (c + 1) * rows, :]
            north = (even + odd).astype(jnp.bfloat16)
            south = (sign * (even - odd)).astype(jnp.bfloat16)
            for b in range(lane_blocks):
                lanes = slice(b * LANES, (b + 1) * LANES)
                out_ref[b, c, group] = north[:, lanes]
                out_ref[2 * lane_blocks - 1 - b, c, group] = south[:, lanes]
        even_ref[...] = jnp.zeros_like(even_ref)
        odd_ref[...] = jnp.zeros_like(odd_ref)

    def body(item, carry):
        before_group, before_chunk, group, chunk = carry
        slot = lax.rem(item, SLOTS)
        before = lax.rem(item + SLOTS - 1, SLOTS)

        @pl.when(item >= SLOTS)
        def _():
            for copy in table_copies(item - SLOTS, slot):
                copy.wait()

        @pl.when(chunk == first_ref[group])
        def _():
            prev_ref[...] = jnp.zeros_like(prev_ref)
            last_row_ref[...] = jnp.zeros_like(last_row_ref)
            wide_order = jnp.concatenate([order_ref[group]] * lane_blocks, axis=1)
            wide_start = jnp.concatenate([start_ref[group]] * lane_blocks, axis=1)
            log_ref[...] = wide_start + wide_order * geometry_ref[1:2, :]

        @pl.when(chunk <= last_ref[group])
        def _():
            products(before)
            recursion(True, group, chunk, slot)

        @pl.when(chunk > last_ref[group])
        def _():
            products(before)
            recursion(False, group, chunk, slot)

        for copy in table_copies(item, slot):
            copy.start()

        @pl.when(jnp.logical_and(before_chunk == chunks - 1, item > 0))
        def _():
            finish(before_group)

        done = chunk == chunks - 1
        next_group = jnp.minimum(group + done.astype(jnp.int32), groups - 1)
        next_chunk = jnp.where(done, first_ref[next_group], chunk + 1)
        return group, chunk, next_group, next_chunk

    zero = jnp.int32(0)
    lax.fori_loop(0, count, body, (zero, zero, zero, first_ref[0]))
    products(lax.rem(count - 1, SLOTS))
    finish(jnp.int32(groups - 1))
    for back in range(SLOTS, 0, -1):

        @pl.when(count >= back)
        def _():
            for copy in table_copies(count - back, lax.rem(count - back, SLOTS)):
                copy.wait()


def analysis_kernel(
    comps,
    groups,
    chunks,
    sign,
    first_ref,
    radial_ref,
    grid_ref,
    table_ref,
    kappa_ref,
    gather_ref,
    weight_ref,
    sorted_ref,
    shared_ref,
    side_ref,
    wide_ref,
    found_ref,
    buffer_ref,
    sems,
):
    rows = 2 * ORD
    half = CHUNK * ORD // 2
    half_cycles = weight_ref.shape[1]
    degrees = chunks * CHUNK
    lane_blocks = half_cycles // LANES
    width = found_ref.shape[1]
    count = lax.fori_loop(0, groups, lambda g, n: n + chunks - first_ref[g], jnp.int32(0))
    shape = (ORD, width)
    lane = lax.broadcasted_iota(jnp.int32, shape, 1)
    own = lax.broadcasted_iota(jnp.int32, shape, 0) == lane % ORD
    mask = jnp.where(own, 1.0, 0.0)
    mask = jnp.concatenate([mask] * (half // ORD), axis=0)
    unit = (
        lax.broadcasted_iota(jnp.int32, (width, width), 0)
        == lax.broadcasted_iota(jnp.int32, (width, width), 1)
    ).astype(jnp.bfloat16)
    contract = (((1,), (1,)), ((), ()))
    wide_ref[...] = jnp.zeros_like(wide_ref)
    radial = radial_ref[0]
    shells, share = shared_ref.shape[0], shared_ref.shape[3]

    def table_copies(item, slot):
        return [
            pltpu.make_async_copy(
                table_ref.at[item, p], buffer_ref.at[slot, p], sems.at[slot, p]
            )
            for p in range(2)
        ]

    for ahead in range(SLOTS - 1):

        @pl.when(ahead < count)
        def _():
            for copy in table_copies(ahead, ahead):
                copy.start()

    def narrow(chunk):
        found = jnp.dot(gather_ref[...], wide_ref[...], preferred_element_type=jnp.float32)
        found_ref[pl.ds(pl.multiple_of(chunk * CHUNK, CHUNK), CHUNK), :] = found.astype(
            jnp.bfloat16
        )

    def advance(group, chunk, carry):
        item, before = carry
        slot = lax.rem(item, SLOTS)
        ahead = item + SLOTS - 1

        @pl.when(ahead < count)
        def _():
            for copy in table_copies(ahead, lax.rem(ahead, SLOTS)):
                copy.start()

        for copy in table_copies(item, slot):
            copy.wait()
        narrow(before)
        for p in range(2):
            wide = jnp.dot(buffer_ref[slot, p], side_ref[p], preferred_element_type=jnp.float32)
            wide_ref[p * half : (p + 1) * half, :] = (wide * mask).astype(jnp.bfloat16)
        return item + 1, chunk

    def group_body(group, item):
        for b in range(lane_blocks):
            lanes = slice(b * LANES, (b + 1) * LANES)
            weight = weight_ref[:, lanes]
            norths, souths = [], []
            for c in range(comps):
                norths.append(grid_ref[b, c, group].astype(jnp.float32))
                souths.append(sign * grid_ref[2 * lane_blocks - 1 - b, c, group].astype(jnp.float32))
            fill = jnp.zeros((width - comps * rows, LANES), jnp.float32)
            north = jnp.concatenate(norths + [fill], axis=0)
            south = jnp.concatenate(souths + [fill], axis=0)
            side_ref[0, lanes, :] = (weight * (north + south)).T.astype(jnp.bfloat16)
            side_ref[1, lanes, :] = (weight * (north - south)).T.astype(jnp.bfloat16)
        found_ref[...] = jnp.zeros_like(found_ref)
        item, before = lax.fori_loop(
            first_ref[group], chunks, functools.partial(advance, group), (item, jnp.int32(chunks))
        )
        narrow(before)
        turned = lax.dot_general(
            unit, found_ref[:degrees], contract, preferred_element_type=jnp.float32
        )
        kappa = kappa_ref[group]
        at = pl.multiple_of(group * rows, rows)
        factors = jnp.concatenate([kappa, kappa], axis=0)
        for c in range(comps):
            piece = turned[c * rows : (c + 1) * rows] * factors
            sorted_ref[c, pl.ds(at, rows), :] = piece.astype(jnp.bfloat16)
            piece = (piece * radial).astype(jnp.bfloat16)
            for n in range(shells):
                shared_ref[n, c, pl.ds(at, rows), :] = piece[:, n * share : (n + 1) * share]
        return item

    lax.fori_loop(0, groups, group_body, jnp.int32(0))


def unsort_kernel(counts, place_ref, *refs):
    out_ref = refs[-1]
    for c in range(out_ref.shape[0]):
        found = 0.0
        for part, ref in enumerate(refs[:-1]):
            lanes = slice(part * counts, (part + 1) * counts)
            found += jnp.dot(place_ref[:, lanes], ref[c], preferred_element_type=jnp.float32)
        out_ref[c] = found.astype(jnp.bfloat16)


def shell_sum_kernel(counts, place_ref, *refs):
    out_ref = refs[-1]
    for c in range(out_ref.shape[0]):
        found = 0.0
        for part, ref in enumerate(refs[:-1]):
            lanes = slice(part * counts, (part + 1) * counts)
            for n in range(ref.shape[0]):
                found += jnp.dot(place_ref[:, lanes], ref[n, c], preferred_element_type=jnp.float32)
        out_ref[c] = found


def wave_kernel(forward_base, forward_turn, backward_base, backward_turn, forward_ref, backward_ref):
    points = forward_ref.shape[1]
    step = 512
    per = forward_ref.shape[2] // step

    def forward_lanes(i, carry):
        p, block = i // per, i % per
        at = pl.multiple_of(block * step, step)
        turn_cos = forward_turn[0, p, :, pl.ds(at, step)]
        turn_sin = forward_turn[1, p, :, pl.ds(at, step)]

        def turn(n, state):
            cos, sin = state
            later_cos = cos * turn_cos - sin * turn_sin
            later_sin = sin * turn_cos + cos * turn_sin
            rows = pl.ds(pl.multiple_of(n * 2 * ORD, 2 * ORD), 2 * ORD)
            forward_ref[p, rows, pl.ds(at, step)] = jnp.concatenate(
                [cos, later_cos], axis=0
            ).astype(jnp.bfloat16)
            cos = later_cos * turn_cos - later_sin * turn_sin
            sin = later_sin * turn_cos + later_cos * turn_sin
            return cos, sin

        state = (forward_base[0, p, :, pl.ds(at, step)], forward_base[1, p, :, pl.ds(at, step)])
        lax.fori_loop(0, points // (2 * ORD), turn, state)
        return carry

    lax.fori_loop(0, 2 * per, forward_lanes, 0)
    count = backward_base.shape[2]

    def backward_rows(i, carry):
        p, q = i // count, i % count
        real, imaginary = backward_base[0, p, q], backward_base[1, p, q]
        turn_cos, turn_sin = backward_turn[0, p, q], backward_turn[1, p, q]
        rows = pl.ds(pl.multiple_of(q * 2 * ORD, 2 * ORD), 2 * ORD)
        for a in range(points // LANES):
            backward_ref[p, rows, a * LANES : (a + 1) * LANES] = jnp.concatenate(
                [real, imaginary], axis=0
            ).astype(jnp.bfloat16)
            real, imaginary = (
                real * turn_cos + imaginary * turn_sin,
                imaginary * turn_cos - real * turn_sin,
            )
        return carry

    lax.fori_loop(0, 2 * count, backward_rows, 0)


def grid_kernel(norm, packs, parts, *refs):
    grid_refs, out_refs = refs[:parts], refs[parts + 3 : 2 * parts + 3]
    forward_ref, backward_ref, viscosity_ref = refs[parts : parts + 3]
    field_ref, stress_ref = refs[2 * parts + 3 :]
    blocks, _, groups, rows, lanes = grid_refs[0].shape
    halves = parts // 2
    step_rows = halves * groups * rows
    points = forward_ref.shape[1]
    tile = 256
    for part, grid_ref in enumerate(grid_refs):
        p, offset = part // halves, part % halves * groups * rows
        for w in range(packs):
            for d in range(blocks):
                at = d * step_rows + offset
                field_ref[p, at : at + groups * rows, w * lanes : (w + 1) * lanes] = grid_ref[
                    d, w
                ].reshape(groups * rows, lanes)

    def points_step(i, carry):
        at = pl.multiple_of(i * tile, tile)
        even = jnp.dot(
            forward_ref[0, pl.ds(at, tile), :], field_ref[0], preferred_element_type=jnp.float32
        )
        odd = jnp.dot(
            forward_ref[1, pl.ds(at, tile), :], field_ref[1], preferred_element_type=jnp.float32
        )
        near = viscosity_ref[pl.ds(at, tile), :]
        far = viscosity_ref[pl.ds(points + at, tile), :]
        if packs > 1:
            near = jnp.concatenate([near] * packs, axis=1)
            far = jnp.concatenate([far] * packs, axis=1)
        near = (near * (even + odd)).astype(jnp.bfloat16).astype(jnp.float32)
        far = (far * (even - odd)).astype(jnp.bfloat16).astype(jnp.float32)
        stress_ref[0, pl.ds(at, tile), :] = (near + far).astype(jnp.bfloat16)
        stress_ref[1, pl.ds(at, tile), :] = (near - far).astype(jnp.bfloat16)
        return carry

    lax.fori_loop(0, points // tile, points_step, 0)
    def orders_step(d, carry):
        for p in range(2):
            at = pl.multiple_of(d * step_rows, step_rows)
            found = jnp.dot(
                backward_ref[p, pl.ds(at, step_rows), :],
                stress_ref[p],
                preferred_element_type=jnp.float32,
            )
            found = (found * norm).astype(jnp.bfloat16)
            for h in range(halves):
                piece = found[h * groups * rows : (h + 1) * groups * rows]
                for w in range(packs):
                    out_refs[p * halves + h][d, w] = piece[:, w * lanes : (w + 1) * lanes].reshape(
                        groups, rows, lanes
                    )
        return carry

    lax.fori_loop(0, blocks, orders_step, 0)


def whole(shape):
    return pl.BlockSpec(shape, lambda *_: (0,) * len(shape))


def params(flops, nbytes):
    return dict(
        compiler_params=pltpu.CompilerParams(vmem_limit_bytes=VMEM_LIMIT),
        cost_estimate=pl.CostEstimate(flops=flops, bytes_accessed=nbytes, transcendentals=0),
    )


def run_synth(bounds, spectra, place, orders, starts, degree_table, spread, geometry, chunks, sign):
    comps, slots, degrees = spectra.shape
    groups = orders.shape[0]
    half_cycles = geometry.shape[1]
    blocks = 2 * half_cycles // LANES
    rows = 2 * ORD
    half = CHUNK * ORD // 2
    smem = pl.BlockSpec(memory_space=pltpu.SMEM)
    vmem = pl.BlockSpec(memory_space=pltpu.VMEM)
    return pl.pallas_call(
        functools.partial(synth_kernel, comps, groups, chunks, sign),
        out_shape=(
            jax.ShapeDtypeStruct((blocks, comps, groups, rows, LANES), jnp.bfloat16),
            jax.ShapeDtypeStruct((groups * chunks, 2, half, half_cycles), jnp.bfloat16),
            jax.ShapeDtypeStruct((groups, ORD, degrees), jnp.float32),
        ),
        in_specs=[smem] * 2 + [vmem] * 7,
        out_specs=(vmem, pl.BlockSpec(memory_space=pl.ANY), vmem),
        scratch_shapes=[
            pltpu.VMEM((comps, groups * rows, degrees), jnp.bfloat16),
            pltpu.VMEM((comps * rows, half_cycles), jnp.float32),
            pltpu.VMEM((comps * rows, half_cycles), jnp.float32),
            pltpu.VMEM((ORD, half_cycles), jnp.float32),
            pltpu.VMEM((ORD, half_cycles), jnp.float32),
            pltpu.VMEM((ORD, half_cycles), jnp.float32),
            pltpu.VMEM((groups, degrees // BLOCK, ORD, LANES), jnp.float32),
            pltpu.VMEM((comps * rows, CHUNK * ORD), jnp.bfloat16),
            pltpu.VMEM((SLOTS, 2, half, half_cycles), jnp.bfloat16),
            pltpu.SemaphoreType.DMA((SLOTS, 2)),
        ],
        name="synthesis",
        **params(groups * chunks * 2 * comps * rows * 2 * half * half_cycles, 40 << 20),
    )(*bounds, spectra, place, orders, starts, degree_table, spread, geometry)


def run_analysis(first, radial_weight, gridded, table, kappa, gather, weights, shells, sign):
    blocks, comps, groups, rows, _ = gridded.shape
    half_cycles = weights.shape[1]
    half = CHUNK * ORD // 2
    degrees = kappa.shape[2]
    chunks = degrees // CHUNK
    width = -(-comps * rows // LANES) * LANES
    smem = pl.BlockSpec(memory_space=pltpu.SMEM)
    vmem = pl.BlockSpec(memory_space=pltpu.VMEM)
    return pl.pallas_call(
        functools.partial(analysis_kernel, comps, groups, chunks, sign),
        out_shape=(
            jax.ShapeDtypeStruct((comps, groups * rows, degrees), jnp.bfloat16),
            jax.ShapeDtypeStruct((shells, comps, groups * rows, degrees // shells), jnp.bfloat16),
        ),
        in_specs=[smem, smem, vmem, pl.BlockSpec(memory_space=pl.ANY)] + [vmem] * 3,
        out_specs=(vmem, vmem),
        scratch_shapes=[
            pltpu.VMEM((2, half_cycles, width), jnp.bfloat16),
            pltpu.VMEM((2 * half, width), jnp.bfloat16),
            pltpu.VMEM((degrees + CHUNK, width), jnp.bfloat16),
            pltpu.VMEM((SLOTS, 2, half, half_cycles), jnp.bfloat16),
            pltpu.SemaphoreType.DMA((SLOTS, 2)),
        ],
        name="analysis",
        **params(groups * chunks * 2 * comps * rows * 2 * half * half_cycles, 40 << 20),
    )(first, radial_weight, gridded, table, kappa, gather, weights)


def run_grid(received, forward, backward, viscosity, norm):
    blocks, comps, groups, rows, lanes = received[0].shape
    parts = len(received)
    packs = 2 if comps % 2 == 0 else 1
    depth = forward.shape[2]
    half_points = forward.shape[1]
    part = pl.BlockSpec((blocks, packs, groups, rows, lanes), lambda i: (0, i, 0, 0, 0))
    return pl.pallas_call(
        functools.partial(grid_kernel, norm, packs, parts),
        out_shape=[jax.ShapeDtypeStruct(received[0].shape, jnp.bfloat16)] * parts,
        grid=(comps // packs,),
        in_specs=[part] * parts
        + [whole(forward.shape), whole(backward.shape), whole(viscosity.shape)],
        out_specs=[part] * parts,
        scratch_shapes=[
            pltpu.VMEM((2, depth, packs * lanes), jnp.bfloat16),
            pltpu.VMEM((2, half_points, packs * lanes), jnp.bfloat16),
        ],
        name="grid_transforms",
        **params(8 * comps * lanes * depth * half_points, 16 << 20),
    )(*received, forward, backward, viscosity)


def run_place(kernel, place, pieces, out_shape, counts):
    vmem = pl.BlockSpec(memory_space=pltpu.VMEM)
    return pl.pallas_call(
        functools.partial(kernel, counts),
        out_shape=out_shape,
        in_specs=[vmem] * (1 + len(pieces)),
        out_specs=vmem,
        name="natural_order",
        **params(2 * place.shape[1] * math.prod(out_shape.shape), 8 << 20),
    )(place, *pieces)


def wave_tables(sorted_all, point_count, groups):
    blocks = sorted_all.shape[0]
    half_points = point_count // 2
    orders = sorted_all.reshape(blocks, 2, groups // 2, 1, ORD).transpose(1, 0, 2, 3, 4)
    shape = (2, blocks, groups // 2, 2, ORD)
    depth = math.prod(shape[1:])
    shift = jnp.arange(2, dtype=jnp.int32)[:, None] * (point_count // 4)
    lane_orders = jnp.broadcast_to(orders, shape).reshape(2, 1, depth)
    lane_shift = jnp.broadcast_to(shift, shape).reshape(2, 1, depth)

    def angle(phase):
        return (phase % point_count).astype(jnp.float32) * (2.0 * math.pi / point_count)

    def both(phase):
        return jnp.stack([jnp.cos(angle(phase)), jnp.sin(angle(phase))])

    rows = jnp.arange(ORD, dtype=jnp.int32)[None, :, None]
    forward_base = both(lane_orders * rows + lane_shift)
    forward_turn = both(lane_orders * ORD)
    row_orders = orders.reshape(2, depth // (2 * ORD), ORD, 1)
    longitudes = jnp.arange(LANES, dtype=jnp.int32)
    angles = angle(row_orders * longitudes)
    backward_base = jnp.stack([jnp.cos(angles), -jnp.sin(angles)])
    turn_shape = (2, 2, depth // (2 * ORD), ORD, LANES)
    backward_turn = jnp.broadcast_to(both(row_orders * LANES), turn_shape)
    vmem = pl.BlockSpec(memory_space=pltpu.VMEM)
    return pl.pallas_call(
        wave_kernel,
        out_shape=(
            jax.ShapeDtypeStruct((2, half_points, depth), jnp.bfloat16),
            jax.ShapeDtypeStruct((2, depth, half_points), jnp.bfloat16),
        ),
        in_specs=[vmem] * 4,
        out_specs=(vmem, vmem),
        name="waves",
        **params(8 * depth * half_points, 12 << 20),
    )(forward_base, forward_turn, backward_base, backward_turn)


def to_blocks(gridded, cycle_local):
    blocks, comps, groups, rows, _ = gridded.shape
    share = LANES // cycle_local
    if share == 1:
        return gridded
    cut = gridded.reshape(2, blocks // 2, comps, groups, rows, share, cycle_local)
    cut = cut.transpose(0, 1, 5, 2, 3, 4, 6)
    cut = jnp.stack([cut[0], jnp.flip(cut[1], axis=1)])
    return cut.reshape(blocks * share, comps, groups, rows, cycle_local)


def from_blocks(gridded, cycle_local):
    blocks, comps, groups, rows, _ = gridded.shape
    share = LANES // cycle_local
    if share == 1:
        return gridded
    cut = gridded.reshape(2, blocks // share // 2, share, comps, groups, rows, cycle_local)
    cut = jnp.stack([cut[0], jnp.flip(cut[1], axis=1)])
    cut = cut.transpose(0, 1, 3, 4, 5, 2, 6)
    return cut.reshape(blocks // share, comps, groups, rows, LANES)


def pack_comps(gridded):
    blocks, comps, groups, rows, cycle_local = gridded.shape
    if cycle_local == LANES:
        return gridded
    side = gridded.transpose(0, 2, 3, 1, 4).reshape(blocks, 1, groups, rows, comps * cycle_local)
    extra = -(comps * cycle_local) % LANES
    return jnp.pad(side, ((0, 0),) * 4 + ((0, extra),))


def unpack_comps(gridded, comps, cycle_local):
    if cycle_local == LANES:
        return gridded
    blocks, _, groups, rows, _ = gridded.shape
    side = gridded[..., : comps * cycle_local]
    side = side.reshape(blocks, groups, rows, comps, cycle_local)
    return side.transpose(0, 3, 1, 2, 4)


def shards(strain_spec, order_map, viscosity, radial_weight):
    comps, shells, slots, parts, degrees = strain_spec.shape
    block_count = lax.axis_size("blk")
    block = lax.axis_index("blk")
    cycle_local = viscosity.shape[1]
    cycle_count = cycle_local * block_count
    half_cycles = cycle_count // 2
    points = viscosity.shape[2]
    groups = slots // ORD
    chunks = degrees // CHUNK

    rank_all = rank_orders(order_map.reshape(block_count, slots))
    sorted_all = apply_rank(order_map.reshape(block_count, slots), rank_all)
    rank = lax.dynamic_index_in_dim(rank_all, block, 0, keepdims=False)
    sorted_orders = lax.dynamic_index_in_dim(sorted_all, block, 0, keepdims=False)
    by_group = sorted_orders.reshape(groups, ORD)
    first, last = by_group[:, 0] // CHUNK, by_group[:, -1] // CHUNK
    order = sorted_orders.astype(jnp.float32)
    counter = jnp.arange(1, degrees, dtype=jnp.float32)
    logs = jnp.where(counter <= order[:, None], jnp.log(1.0 - 0.5 / counter), 0.0)
    starts = 0.5 * jnp.log((2.0 * order + 1.0) / (4.0 * math.pi)) + 0.5 * jnp.sum(logs, axis=1)
    order_lanes = lane_fill(order)

    cycle_index = jnp.arange(half_cycles, dtype=jnp.float32)
    colatitude = math.pi * (2.0 * cycle_index + 1.0) / (2.0 * cycle_count)
    geometry = jnp.stack([2.0 * jnp.cos(colatitude), jnp.log(jnp.sin(colatitude))])

    row_rank = rank // ORD * (2 * ORD) + rank % ORD
    row_rank = (row_rank[:, None] + ORD * jnp.arange(2, dtype=jnp.int32)).reshape(-1)
    place = jnp.arange(slots * 2, dtype=jnp.int32)
    hit = row_rank[None, :] == place[:, None]
    my_orders = lax.dynamic_index_in_dim(
        order_map.reshape(block_count, slots), block, 0, keepdims=False
    )
    doubling = jnp.repeat(jnp.where(my_orders == 0, 1.0, 2.0), 2)
    place_in = jnp.where(hit, doubling[None, :], 0.0).astype(jnp.bfloat16)
    place_out = hit.T.astype(jnp.bfloat16)

    spectra = strain_spec.reshape(comps, slots * parts, degrees)
    part_count = min(PARTS, groups)
    part_groups = groups // part_count
    part_rows = part_groups * 2 * ORD
    sections = [slice(i * part_groups, (i + 1) * part_groups) for i in range(part_count)]
    signs = [1.0 if i < part_count // 2 else -1.0 for i in range(part_count)]
    start_lanes, degree_table, spread = lane_fill(starts), degree_rows(degrees), spread_matrix()
    received, tables = [], []
    for i, part in enumerate(sections):
        gridded, table, kappa = run_synth(
            (first[part], last[part]),
            spectra,
            place_in[i * part_rows : (i + 1) * part_rows],
            order_lanes[part],
            start_lanes[part],
            degree_table,
            spread,
            geometry,
            chunks,
            signs[i],
        )
        tables.append((table, kappa))
        arrived = lax.all_to_all(to_blocks(gridded, cycle_local), "blk", 0, 0, tiled=True)
        received.append(pack_comps(arrived))

    forward, backward = wave_tables(sorted_all, points, groups)
    weights = fejer_weights(cycle_count)[None, :]
    mirror = jnp.arange(cycle_local, dtype=jnp.int32)
    mirror = jnp.where(block * 2 < block_count, mirror, cycle_local - 1 - mirror)
    turn = (mirror[None, :] == jnp.arange(cycle_local, dtype=jnp.int32)[:, None]).astype(jnp.float32)
    local = jnp.einsum("jk,ji->ki", viscosity[0], turn, precision=lax.Precision.HIGHEST)
    if cycle_local < LANES:
        local = jnp.concatenate([local] * comps, axis=1)
        local = jnp.pad(local, ((0, 0), (0, -local.shape[1] % LANES)))
    spectrum = run_grid(received, forward, backward, local, 2.0 * math.pi / points)
    returned = [
        lax.all_to_all(unpack_comps(piece, comps, cycle_local), "blk", 0, 0, tiled=True)
        for piece in spectrum
    ]

    shell_count = lax.axis_size("shell")
    gather = gather_matrix()
    ordered, shared = [], []
    for i, part in enumerate(sections):
        table, kappa = tables[i]
        coefs, weighted = run_analysis(
            first[part],
            radial_weight,
            from_blocks(returned[i], cycle_local),
            table,
            kappa,
            gather,
            weights,
            shell_count,
            signs[i],
        )
        ordered.append(coefs)
        shared.append(lax.all_to_all(weighted, "shell", 0, 0, tiled=True))
    stress = run_place(
        unsort_kernel,
        place_out,
        ordered,
        jax.ShapeDtypeStruct((comps, slots * parts, degrees), jnp.bfloat16),
        part_rows,
    )
    integrated = run_place(
        shell_sum_kernel,
        place_out,
        shared,
        jax.ShapeDtypeStruct((comps, slots * parts, degrees // shell_count), jnp.float32),
        part_rows,
    )
    stress_spec = stress.reshape(strain_spec.shape)
    return (stress_spec, integrated.reshape(comps, slots, parts, degrees // shell_count))


def solution(mesh):
    return jax.shard_map(
        shards,
        mesh=mesh,
        in_specs=(P(None, "shell", "blk", None, None), P(), P("shell", "blk", None), P("shell")),
        out_specs=(P(None, "shell", "blk", None, None), P(None, "blk", None, "shell")),
        check_vma=False,
    )
```

```python
import functools
import math

import jax
import jax.numpy as jnp
from jax import lax
from jax.experimental import pallas as pl
from jax.experimental.pallas import tpu as pltpu
from jax.sharding import PartitionSpec as P

two_power = 1099511627776.0
inverse_power = 1.0 / 1099511627776.0
log_jump = 40.0 * math.log(2.0)

ORD = 8
CHUNK = 128
BLOCK = 16
LANES = 128
TILE = 256
SLOTS = 4
VMEM_LIMIT = 56 * 1024 * 1024


def fejer_weights(cycle_count):
    half_count = cycle_count // 2
    cycle_index = jnp.arange(half_count, dtype=jnp.int32)
    wave_number = jnp.arange(1, half_count + 1, dtype=jnp.int32)
    phase_index = wave_number[:, None] * (2 * cycle_index[None, :] + 1) % (2 * cycle_count)
    angles = phase_index.astype(jnp.float32) * (math.pi / cycle_count)
    wave_float = wave_number.astype(jnp.float32)
    divisor = 4.0 * wave_float * wave_float - 1.0
    series = jnp.sum(jnp.cos(angles) / divisor[:, None], axis=0)
    return 2.0 / cycle_count * (1.0 - 2.0 * series)


def rank_orders(orders):
    top = orders.shape[-1]
    key = orders + (orders % 2) * (1 << 20)
    return jnp.sum((key[..., None, :] < key[..., :, None]).astype(jnp.int32), axis=-1)


def apply_rank(values, rank):
    count = rank.shape[-1]
    place = jnp.arange(count, dtype=jnp.int32)
    hit = rank[..., :, None] == place
    return jnp.sum(jnp.where(hit, values[..., :, None], 0), axis=-2)


def lane_fill(values):
    return jnp.broadcast_to(values.reshape(-1, ORD, 1), (values.shape[0] // ORD, ORD, LANES))


def gather_matrix():
    place = jnp.arange(CHUNK * ORD, dtype=jnp.int32)
    parity = place // (CHUNK * ORD // 2)
    degree = 2 * (place % (CHUNK * ORD // 2) // ORD) + parity
    row = jnp.arange(CHUNK, dtype=jnp.int32)
    return (row[:, None] == degree[None, :]).astype(jnp.bfloat16)


def degree_rows(degree_count):
    below = jnp.arange(degree_count, dtype=jnp.float32) - 1.0
    bottom = 4.0 * below * below - 1.0
    rows = jnp.stack([4.0 * below * below / bottom, 4.0 / bottom])
    return jnp.broadcast_to(rows[:, :, None], (2, degree_count, LANES))


def kappa_lanes(order):
    lane = lax.broadcasted_iota(jnp.int32, order.shape, 1)
    degree = lane.astype(jnp.float32)
    square = degree * degree
    gap = jnp.maximum(square - order * order, 1.0)
    kappa = jnp.where(degree > order, jnp.sqrt((square - 0.25) / gap), 1.0)
    step = 1
    while step < BLOCK:
        moved = pltpu.roll(kappa, step, 1)
        kappa = kappa * jnp.where(lane % BLOCK >= step, moved, 1.0)
        step *= 2
    return kappa


def synth_kernel(
    comps,
    groups,
    chunks,
    sign,
    first_ref,
    spec_ref,
    place_ref,
    order_ref,
    start_ref,
    degree_ref,
    geometry_ref,
    out_ref,
    table_ref,
    kappa_ref,
    sorted_ref,
    even_ref,
    odd_ref,
    prev_ref,
    last_row_ref,
    log_ref,
    end_ref,
    wide_ref,
    buffer_ref,
    second_ref,
    sems,
):
    rows = 2 * ORD
    half = CHUNK * ORD // 2
    lane_blocks = geometry_ref.shape[1] // LANES
    for c in range(comps):
        moved = jnp.dot(place_ref[...], spec_ref[c], preferred_element_type=jnp.float32)
        sorted_ref[c] = moved.astype(jnp.bfloat16)
    degrees = chunks * CHUNK
    batch = math.gcd(groups, 4)

    def fill_kappa(i, carry):
        order = order_ref[pl.ds(i * batch, batch)].reshape(batch * ORD, LANES)
        kappa = kappa_lanes(jnp.concatenate([order] * (degrees // LANES), axis=1))
        kappa = kappa.reshape(batch, ORD, degrees)
        kappa_ref[pl.ds(i * batch, batch)] = kappa
        for b in range(degrees // BLOCK):
            end = kappa[:, :, (b + 1) * BLOCK - 1 : (b + 1) * BLOCK]
            end_ref[pl.ds(i * batch, batch), b] = jnp.broadcast_to(end, (batch, ORD, LANES))
        return carry

    lax.fori_loop(0, groups // batch, fill_kappa, 0)
    shape = (rows, CHUNK * ORD)
    row_order = lax.broadcasted_iota(jnp.int32, shape, 0) % ORD
    lane_order = lax.broadcasted_iota(jnp.int32, shape, 1) % ORD
    mask = jnp.where(row_order == lane_order, 1.0, 0.0)
    count = lax.fori_loop(0, groups, lambda g, n: n + chunks - first_ref[g], jnp.int32(0))
    even_ref[...] = jnp.zeros_like(even_ref)
    odd_ref[...] = jnp.zeros_like(odd_ref)
    wide_ref[...] = jnp.zeros_like(wide_ref)
    second_ref[SLOTS // 2 - 1] = jnp.zeros_like(second_ref[SLOTS // 2 - 1])

    def table_copies(item, slot, which):
        offset = 0 if which is buffer_ref else SLOTS // 2
        return [
            pltpu.make_async_copy(
                which.at[slot, p], table_ref.at[item, p], sems.at[slot + offset, p]
            )
            for p in range(2)
        ]

    def products(other, before):
        even_ref[...] += jnp.dot(
            wide_ref[:, :half], other[before, 0], preferred_element_type=jnp.float32
        )
        odd_ref[...] += jnp.dot(
            wide_ref[:, half:], other[before, 1], preferred_element_type=jnp.float32
        )

    def recursion(group, chunk, slot, mine):
        order = order_ref[group]
        begin = chunk * CHUNK
        odd_chunk = lax.rem(chunk, LANES // CHUNK)
        lane = pl.multiple_of((chunk - odd_chunk) * CHUNK, LANES)
        kappa = kappa_ref[group, :, pl.ds(lane, LANES)]
        square = order * order
        seed_at = jnp.concatenate([order - begin.astype(jnp.float32)] * lane_blocks, axis=1)
        twice = geometry_ref[0:1, :]
        prev = prev_ref[...]
        last = last_row_ref[...]
        logs = log_ref[...]
        for b in range(CHUNK // BLOCK):
            scale = jnp.exp(logs)
            held = []
            for i in range(BLOCK):
                step = b * BLOCK + i
                one = degree_ref[0, pl.ds(begin + step, 1), :]
                two = degree_ref[1, pl.ds(begin + step, 1), :]
                coef = jnp.concatenate([one - two * square] * lane_blocks, axis=1)
                now = twice * last - coef * prev
                now = jnp.where(seed_at == float(step), 1.0, now)
                held.append(now * scale)
                prev, last = last, now
            for p in range(2):
                for i in range(p, BLOCK, 4):
                    pair = jnp.concatenate([held[i], held[i + 2]], axis=0).astype(jnp.bfloat16)
                    at = (b * BLOCK + i - p) // 2 * ORD
                    mine[slot, p, at : at + 2 * ORD, :] = pair
            end = end_ref[group, chunk * (CHUNK // BLOCK) + b]
            end = jnp.concatenate([end] * lane_blocks, axis=1)
            last = last * end
            prev = prev * end
            large = jnp.abs(last) > two_power
            factor = jnp.where(large, inverse_power, 1.0)
            last = last * factor
            prev = prev * factor
            logs = logs + jnp.where(large, log_jump, 0.0)
        prev_ref[...] = prev
        last_row_ref[...] = last
        log_ref[...] = logs
        at = pl.multiple_of(group * rows, rows)
        factors = jnp.concatenate([kappa, kappa], axis=0)
        piece = jnp.concatenate(
            [
                (sorted_ref[c, pl.ds(at, rows), pl.ds(lane, LANES)] * factors).astype(jnp.bfloat16)
                for c in range(comps)
            ],
            axis=0,
        )
        lane_at = lax.broadcasted_iota(jnp.int32, (rows, LANES), 1)
        for c in range(comps):
            source = piece[c * rows : (c + 1) * rows].astype(jnp.float32)
            for q in range(CHUNK * ORD // LANES):
                p, t = q // (CHUNK * ORD // LANES // 2), q % (CHUNK * ORD // LANES // 2)
                index = 2 * (lane_at // ORD + t * (LANES // ORD)) + p + odd_chunk * CHUNK
                moved = jnp.take_along_axis(source, index, axis=1)
                lanes = slice(q * LANES, (q + 1) * LANES)
                wide_ref[c * rows : (c + 1) * rows, lanes] = (moved * mask[:, lanes]).astype(jnp.bfloat16)

    def finish(group):
        for c in range(comps):
            even = even_ref[c * rows : (c + 1) * rows, :]
            odd = odd_ref[c * rows : (c + 1) * rows, :]
            north = (even + odd).astype(jnp.bfloat16)
            south = (sign * (even - odd)).astype(jnp.bfloat16)
            for b in range(lane_blocks):
                lanes = slice(b * LANES, (b + 1) * LANES)
                out_ref[b, c, group] = north[:, lanes]
                out_ref[2 * lane_blocks - 1 - b, c, group] = south[:, lanes]
        even_ref[...] = jnp.zeros_like(even_ref)
        odd_ref[...] = jnp.zeros_like(odd_ref)

    def body(item, carry):
        before_group, before_chunk, group, chunk = carry
        for parity in range(2):

            @pl.when(jnp.logical_and(item >= SLOTS, lax.rem(item, 2) == parity))
            def _(parity=parity):
                which = second_ref if parity else buffer_ref
                for copy in table_copies(item - SLOTS, lax.rem(item // 2, SLOTS // 2), which):
                    copy.wait()

        @pl.when(chunk == first_ref[group])
        def _():
            prev_ref[...] = jnp.zeros_like(prev_ref)
            last_row_ref[...] = jnp.zeros_like(last_row_ref)
            wide_order = jnp.concatenate([order_ref[group]] * lane_blocks, axis=1)
            wide_start = jnp.concatenate([start_ref[group]] * lane_blocks, axis=1)
            log_ref[...] = wide_start + wide_order * geometry_ref[1:2, :]

        for parity in range(2):

            @pl.when(lax.rem(item, 2) == parity)
            def _(parity=parity):
                mine, other = (buffer_ref, second_ref) if parity == 0 else (second_ref, buffer_ref)
                place = lax.rem(item // 2, SLOTS // 2)
                before = lax.rem((item + SLOTS - 1) // 2, SLOTS // 2)
                products(other, before)
                recursion(group, chunk, place, mine)
                for copy in table_copies(item, place, mine):
                    copy.start()

        @pl.when(jnp.logical_and(before_chunk == chunks - 1, item > 0))
        def _():
            finish(before_group)

        done = chunk == chunks - 1
        next_group = jnp.minimum(group + done.astype(jnp.int32), groups - 1)
        next_chunk = jnp.where(done, first_ref[next_group], chunk + 1)
        return group, chunk, next_group, next_chunk

    zero = jnp.int32(0)
    lax.fori_loop(0, count, body, (zero, zero, zero, first_ref[0]))
    for parity in range(2):
        which = second_ref if parity else buffer_ref

        @pl.when(lax.rem(count - 1, 2) == parity)
        def _(which=which):
            products(which, lax.rem((count - 1) // 2, SLOTS // 2))

        for back in range(SLOTS, 0, -1):
            item = count - back

            @pl.when(jnp.logical_and(item >= 0, lax.rem(item + SLOTS, 2) == parity))
            def _(item=item, which=which):
                for copy in table_copies(item, lax.rem(item // 2, SLOTS // 2), which):
                    copy.wait()

    finish(jnp.int32(groups - 1))


def analysis_kernel(
    comps,
    groups,
    chunks,
    sign,
    first_ref,
    radial_ref,
    grid_ref,
    table_ref,
    kappa_ref,
    gather_ref,
    weight_ref,
    sorted_ref,
    shared_ref,
    side_ref,
    wide_ref,
    found_ref,
    buffer_ref,
    sems,
):
    rows = 2 * ORD
    half = CHUNK * ORD // 2
    half_cycles = weight_ref.shape[1]
    degrees = chunks * CHUNK
    lane_blocks = half_cycles // LANES
    width = found_ref.shape[1]
    count = lax.fori_loop(0, groups, lambda g, n: n + chunks - first_ref[g], jnp.int32(0))
    shape = (ORD, width)
    lane = lax.broadcasted_iota(jnp.int32, shape, 1)
    own = lax.broadcasted_iota(jnp.int32, shape, 0) == lane % ORD
    mask = jnp.where(own, 1.0, 0.0)
    mask = jnp.concatenate([mask] * (half // ORD), axis=0)
    wide_ref[...] = jnp.zeros_like(wide_ref)
    radial = radial_ref[0]
    shells, share = shared_ref.shape[0], shared_ref.shape[3]

    def table_copies(item, slot):
        return [
            pltpu.make_async_copy(
                table_ref.at[item, p], buffer_ref.at[slot, p], sems.at[slot, p]
            )
            for p in range(2)
        ]

    for ahead in range(SLOTS - 1):

        @pl.when(ahead < count)
        def _():
            for copy in table_copies(ahead, ahead):
                copy.start()

    def narrow(chunk):
        found = jnp.dot(gather_ref[...], wide_ref[...], preferred_element_type=jnp.float32)
        found_ref[pl.ds(pl.multiple_of(chunk * CHUNK, CHUNK), CHUNK), :] = found.astype(
            jnp.bfloat16
        )

    def advance(group, chunk, carry):
        item, before = carry
        slot = lax.rem(item, SLOTS)
        ahead = item + SLOTS - 1

        @pl.when(ahead < count)
        def _():
            for copy in table_copies(ahead, lax.rem(ahead, SLOTS)):
                copy.start()

        for copy in table_copies(item, slot):
            copy.wait()
        narrow(before)
        for p in range(2):
            wide = jnp.dot(buffer_ref[slot, p], side_ref[p], preferred_element_type=jnp.float32)
            wide_ref[p * half : (p + 1) * half, :] = (wide * mask).astype(jnp.bfloat16)
        return item + 1, chunk

    def group_body(group, item):
        for b in range(lane_blocks):
            lanes = slice(b * LANES, (b + 1) * LANES)
            weight = weight_ref[:, lanes]
            norths, souths = [], []
            for c in range(comps):
                norths.append(grid_ref[b, c, group].astype(jnp.float32))
                souths.append(sign * grid_ref[2 * lane_blocks - 1 - b, c, group].astype(jnp.float32))
            fill = jnp.zeros((width - comps * rows, LANES), jnp.float32)
            north = jnp.concatenate(norths + [fill], axis=0)
            south = jnp.concatenate(souths + [fill], axis=0)
            side_ref[0, lanes, :] = (weight * (north + south)).astype(jnp.bfloat16).T
            side_ref[1, lanes, :] = (weight * (north - south)).astype(jnp.bfloat16).T
        found_ref[...] = jnp.zeros_like(found_ref)
        item, before = lax.fori_loop(
            first_ref[group], chunks, functools.partial(advance, group), (item, jnp.int32(chunks))
        )
        narrow(before)
        turned = found_ref[:degrees].T.astype(jnp.float32)
        kappa = kappa_ref[group]
        at = pl.multiple_of(group * rows, rows)
        factors = jnp.concatenate([kappa, kappa], axis=0)
        for c in range(comps):
            piece = turned[c * rows : (c + 1) * rows] * factors
            sorted_ref[c, pl.ds(at, rows), :] = piece.astype(jnp.bfloat16)
            piece = (piece * radial).astype(jnp.bfloat16)
            for n in range(shells):
                shared_ref[n, c, pl.ds(at, rows), :] = piece[:, n * share : (n + 1) * share]
        return item

    lax.fori_loop(0, groups, group_body, jnp.int32(0))


def unsort_kernel(counts, place_ref, *refs):
    out_ref = refs[-1]
    for c in range(out_ref.shape[0]):
        found = 0.0
        for part, ref in enumerate(refs[:-1]):
            lanes = slice(part * counts, (part + 1) * counts)
            found += jnp.dot(place_ref[:, lanes], ref[c], preferred_element_type=jnp.float32)
        out_ref[c] = found.astype(jnp.bfloat16)


def shell_sum_kernel(counts, place_ref, *refs):
    out_ref = refs[-1]
    for c in range(out_ref.shape[0]):
        found = 0.0
        for part, ref in enumerate(refs[:-1]):
            lanes = slice(part * counts, (part + 1) * counts)
            for n in range(ref.shape[0]):
                found += jnp.dot(place_ref[:, lanes], ref[n, c], preferred_element_type=jnp.float32)
        out_ref[c] = found


def wave_kernel(forward_base, forward_turn, backward_base, backward_turn, forward_ref, backward_ref):
    points = forward_ref.shape[1]
    step = 512
    per = forward_ref.shape[2] // step

    def forward_lanes(i, carry):
        p, block = i // per, i % per
        at = pl.multiple_of(block * step, step)
        turn_cos = forward_turn[0, p, :, pl.ds(at, step)]
        turn_sin = forward_turn[1, p, :, pl.ds(at, step)]

        def turn(n, state):
            cos, sin = state
            later_cos = cos * turn_cos - sin * turn_sin
            later_sin = sin * turn_cos + cos * turn_sin
            rows = pl.ds(pl.multiple_of(n * 2 * ORD, 2 * ORD), 2 * ORD)
            forward_ref[p, rows, pl.ds(at, step)] = jnp.concatenate(
                [cos, later_cos], axis=0
            ).astype(jnp.bfloat16)
            cos = later_cos * turn_cos - later_sin * turn_sin
            sin = later_sin * turn_cos + later_cos * turn_sin
            return cos, sin

        state = (forward_base[0, p, :, pl.ds(at, step)], forward_base[1, p, :, pl.ds(at, step)])
        lax.fori_loop(0, points // (2 * ORD), turn, state)
        return carry

    lax.fori_loop(0, 2 * per, forward_lanes, 0)
    count = backward_base.shape[2]

    def backward_rows(i, carry):
        p, q = i // count, i % count
        real, imaginary = backward_base[0, p, q], backward_base[1, p, q]
        turn_cos, turn_sin = backward_turn[0, p, q], backward_turn[1, p, q]
        rows = pl.ds(pl.multiple_of(q * 2 * ORD, 2 * ORD), 2 * ORD)
        for a in range(points // LANES):
            backward_ref[p, rows, a * LANES : (a + 1) * LANES] = jnp.concatenate(
                [real, imaginary], axis=0
            ).astype(jnp.bfloat16)
            real, imaginary = (
                real * turn_cos + imaginary * turn_sin,
                imaginary * turn_cos - real * turn_sin,
            )
        return carry

    lax.fori_loop(0, 2 * count, backward_rows, 0)


def lay_field(grid_ref, field_ref):
    blocks, packs, groups, rows, lanes = grid_ref.shape
    for w in range(packs):
        for d in range(blocks):
            at = d * groups * rows
            field_ref[at : at + groups * rows, w * lanes : (w + 1) * lanes] = grid_ref[
                d, w
            ].reshape(groups * rows, lanes)


def even_field_kernel(grid_ref, forward_ref, even_ref, field_ref):
    lay_field(grid_ref, field_ref)

    def step(i, carry):
        at = pl.multiple_of(i * TILE, TILE)
        even_ref[0, pl.ds(at, TILE), :] = jnp.dot(
            forward_ref[pl.ds(at, TILE), :], field_ref[...], preferred_element_type=jnp.float32
        )
        return carry

    lax.fori_loop(0, forward_ref.shape[0] // TILE, step, 0)


def lay_spectrum(norm, wave_ref, stress, out_ref):
    blocks, packs, groups, rows, lanes = out_ref.shape
    count = groups * rows

    def step(d, carry):
        at = pl.multiple_of(d * count, count)
        found = jnp.dot(
            wave_ref[pl.ds(at, count), :], stress[...], preferred_element_type=jnp.float32
        )
        found = (found * norm).astype(jnp.bfloat16)
        for w in range(packs):
            out_ref[d, w] = found[:, w * lanes : (w + 1) * lanes].reshape(groups, rows, lanes)
        return carry

    lax.fori_loop(0, blocks, step, 0)


def stress_kernel(
    norm,
    grid_ref,
    even_ref,
    forward_ref,
    backward_ref,
    viscosity_ref,
    out_ref,
    difference_ref,
    field_ref,
    sum_ref,
):
    packs = grid_ref.shape[1]
    points = forward_ref.shape[0]
    lay_field(grid_ref, field_ref)

    def step(i, carry):
        at = pl.multiple_of(i * TILE, TILE)
        rows = pl.ds(at, TILE)
        even = even_ref[0, rows, :]
        odd = jnp.dot(forward_ref[rows, :], field_ref[...], preferred_element_type=jnp.float32)
        near = jnp.concatenate([viscosity_ref[rows, :]] * packs, axis=1)
        far = jnp.concatenate([viscosity_ref[pl.ds(points + at, TILE), :]] * packs, axis=1)
        near = (near * (even + odd)).astype(jnp.bfloat16).astype(jnp.float32)
        far = (far * (even - odd)).astype(jnp.bfloat16).astype(jnp.float32)
        sum_ref[rows, :] = (near + far).astype(jnp.bfloat16)
        difference_ref[0, rows, :] = (near - far).astype(jnp.bfloat16)
        return carry

    lax.fori_loop(0, points // TILE, step, 0)
    lay_spectrum(norm, backward_ref, sum_ref, out_ref)


def odd_spectrum_kernel(norm, difference_ref, backward_ref, out_ref):
    lay_spectrum(norm, backward_ref, difference_ref.at[0], out_ref)


def whole(shape):
    return pl.BlockSpec(shape, lambda *_: (0,) * len(shape))


def params(flops, nbytes):
    return dict(
        compiler_params=pltpu.CompilerParams(vmem_limit_bytes=VMEM_LIMIT),
        cost_estimate=pl.CostEstimate(flops=flops, bytes_accessed=nbytes, transcendentals=0),
    )


def run_synth(first, spectra, place, orders, starts, degree_table, geometry, chunks, sign):
    comps, slots, degrees = spectra.shape
    groups = orders.shape[0]
    half_cycles = geometry.shape[1]
    blocks = 2 * half_cycles // LANES
    rows = 2 * ORD
    half = CHUNK * ORD // 2
    smem = pl.BlockSpec(memory_space=pltpu.SMEM)
    vmem = pl.BlockSpec(memory_space=pltpu.VMEM)
    return pl.pallas_call(
        functools.partial(synth_kernel, comps, groups, chunks, sign),
        out_shape=(
            jax.ShapeDtypeStruct((blocks, comps, groups, rows, LANES), jnp.bfloat16),
            jax.ShapeDtypeStruct((groups * chunks, 2, half, half_cycles), jnp.bfloat16),
            jax.ShapeDtypeStruct((groups, ORD, degrees), jnp.float32),
        ),
        in_specs=[smem] + [vmem] * 6,
        out_specs=(vmem, pl.BlockSpec(memory_space=pl.ANY), vmem),
        scratch_shapes=[
            pltpu.VMEM((comps, groups * rows, degrees), jnp.bfloat16),
            pltpu.VMEM((comps * rows, half_cycles), jnp.float32),
            pltpu.VMEM((comps * rows, half_cycles), jnp.float32),
            pltpu.VMEM((ORD, half_cycles), jnp.float32),
            pltpu.VMEM((ORD, half_cycles), jnp.float32),
            pltpu.VMEM((ORD, half_cycles), jnp.float32),
            pltpu.VMEM((groups, degrees // BLOCK, ORD, LANES), jnp.float32),
            pltpu.VMEM((comps * rows, CHUNK * ORD), jnp.bfloat16),
            pltpu.VMEM((SLOTS // 2, 2, half, half_cycles), jnp.bfloat16),
            pltpu.VMEM((SLOTS // 2, 2, half, half_cycles), jnp.bfloat16),
            pltpu.SemaphoreType.DMA((SLOTS, 2)),
        ],
        name="synthesis",
        **params(groups * chunks * 2 * comps * rows * 2 * half * half_cycles, 40 << 20),
    )(first, spectra, place, orders, starts, degree_table, geometry)


def run_analysis(first, radial_weight, gridded, table, kappa, gather, weights, shells, sign):
    blocks, comps, groups, rows, _ = gridded.shape
    half_cycles = weights.shape[1]
    half = CHUNK * ORD // 2
    degrees = kappa.shape[2]
    chunks = degrees // CHUNK
    width = -(-comps * rows // LANES) * LANES
    smem = pl.BlockSpec(memory_space=pltpu.SMEM)
    vmem = pl.BlockSpec(memory_space=pltpu.VMEM)
    return pl.pallas_call(
        functools.partial(analysis_kernel, comps, groups, chunks, sign),
        out_shape=(
            jax.ShapeDtypeStruct((comps, groups * rows, degrees), jnp.bfloat16),
            jax.ShapeDtypeStruct((shells, comps, groups * rows, degrees // shells), jnp.bfloat16),
        ),
        in_specs=[smem, smem, vmem, pl.BlockSpec(memory_space=pl.ANY)] + [vmem] * 3,
        out_specs=(vmem, vmem),
        scratch_shapes=[
            pltpu.VMEM((2, half_cycles, width), jnp.bfloat16),
            pltpu.VMEM((2 * half, width), jnp.bfloat16),
            pltpu.VMEM((degrees + CHUNK, width), jnp.bfloat16),
            pltpu.VMEM((SLOTS, 2, half, half_cycles), jnp.bfloat16),
            pltpu.SemaphoreType.DMA((SLOTS, 2)),
        ],
        name="analysis",
        **params(groups * chunks * 2 * comps * rows * 2 * half * half_cycles, 40 << 20),
    )(first, radial_weight, gridded, table, kappa, gather, weights)


def run_grid(received, forward, backward, viscosity, norm):
    blocks, comps, groups, rows, lanes = received[0].shape
    packs = 2 if comps % 2 == 0 else 1
    steps = comps // packs
    _, half_points, depth = forward.shape
    width = packs * lanes
    part = pl.BlockSpec((blocks, packs, groups, rows, lanes), lambda i: (0, i, 0, 0, 0))
    field = pl.BlockSpec((1, half_points, width), lambda i: (i, 0, 0))

    def wave(p, shape):
        return pl.BlockSpec((None,) + shape, lambda i: (p, 0, 0))

    forward_shape, backward_shape = (half_points, depth), (depth, half_points)
    spectrum_type = jax.ShapeDtypeStruct(received[0].shape, jnp.bfloat16)
    one_product = 2 * steps * width * depth * half_points
    even = pl.pallas_call(
        even_field_kernel,
        out_shape=jax.ShapeDtypeStruct((steps, half_points, width), jnp.float32),
        grid=(steps,),
        in_specs=[part, wave(0, forward_shape)],
        out_specs=field,
        scratch_shapes=[pltpu.VMEM((depth, width), jnp.bfloat16)],
        name="even_field",
        **params(one_product, 8 << 20),
    )(received[0], forward)
    first, difference = pl.pallas_call(
        functools.partial(stress_kernel, norm),
        out_shape=(
            spectrum_type,
            jax.ShapeDtypeStruct((steps, half_points, width), jnp.bfloat16),
        ),
        grid=(steps,),
        in_specs=[
            part,
            field,
            wave(1, forward_shape),
            wave(0, backward_shape),
            whole(viscosity.shape),
        ],
        out_specs=(part, field),
        scratch_shapes=[
            pltpu.VMEM((depth, width), jnp.bfloat16),
            pltpu.VMEM((half_points, width), jnp.bfloat16),
        ],
        name="stress",
        **params(2 * one_product, 16 << 20),
    )(received[1], even, forward, backward, viscosity)
    second = pl.pallas_call(
        functools.partial(odd_spectrum_kernel, norm),
        out_shape=spectrum_type,
        grid=(steps,),
        in_specs=[field, wave(1, backward_shape)],
        out_specs=part,
        name="odd_spectrum",
        **params(one_product, 6 << 20),
    )(difference, backward)
    return [first, second]


def run_place(kernel, place, pieces, out_shape, counts):
    vmem = pl.BlockSpec(memory_space=pltpu.VMEM)
    return pl.pallas_call(
        functools.partial(kernel, counts),
        out_shape=out_shape,
        in_specs=[vmem] * (1 + len(pieces)),
        out_specs=vmem,
        name="natural_order",
        **params(2 * place.shape[1] * math.prod(out_shape.shape), 8 << 20),
    )(place, *pieces)


def wave_tables(sorted_all, point_count, groups):
    blocks = sorted_all.shape[0]
    half_points = point_count // 2
    orders = sorted_all.reshape(blocks, 2, groups // 2, 1, ORD).transpose(1, 0, 2, 3, 4)
    shape = (2, blocks, groups // 2, 2, ORD)
    depth = math.prod(shape[1:])
    shift = jnp.arange(2, dtype=jnp.int32)[:, None] * (point_count // 4)
    lane_orders = jnp.broadcast_to(orders, shape).reshape(2, 1, depth)
    lane_shift = jnp.broadcast_to(shift, shape).reshape(2, 1, depth)

    def angle(phase):
        return (phase % point_count).astype(jnp.float32) * (2.0 * math.pi / point_count)

    def both(phase):
        return jnp.stack([jnp.cos(angle(phase)), jnp.sin(angle(phase))])

    rows = jnp.arange(ORD, dtype=jnp.int32)[None, :, None]
    forward_base = both(lane_orders * rows + lane_shift)
    forward_turn = both(lane_orders * ORD)
    row_orders = orders.reshape(2, depth // (2 * ORD), ORD, 1)
    longitudes = jnp.arange(LANES, dtype=jnp.int32)
    angles = angle(row_orders * longitudes)
    backward_base = jnp.stack([jnp.cos(angles), -jnp.sin(angles)])
    turn_shape = (2, 2, depth // (2 * ORD), ORD, LANES)
    backward_turn = jnp.broadcast_to(both(row_orders * LANES), turn_shape)
    vmem = pl.BlockSpec(memory_space=pltpu.VMEM)
    return pl.pallas_call(
        wave_kernel,
        out_shape=(
            jax.ShapeDtypeStruct((2, half_points, depth), jnp.bfloat16),
            jax.ShapeDtypeStruct((2, depth, half_points), jnp.bfloat16),
        ),
        in_specs=[vmem] * 4,
        out_specs=(vmem, vmem),
        name="waves",
        **params(8 * depth * half_points, 12 << 20),
    )(forward_base, forward_turn, backward_base, backward_turn)


def to_blocks(gridded, cycle_local):
    blocks, comps, groups, rows, _ = gridded.shape
    share = LANES // cycle_local
    if share == 1:
        return gridded
    cut = gridded.reshape(2, blocks // 2, comps, groups, rows, share, cycle_local)
    cut = cut.transpose(0, 1, 5, 2, 3, 4, 6)
    cut = jnp.stack([cut[0], jnp.flip(cut[1], axis=1)])
    return cut.reshape(blocks * share, comps, groups, rows, cycle_local)


def from_blocks(gridded, cycle_local):
    blocks, comps, groups, rows, _ = gridded.shape
    share = LANES // cycle_local
    if share == 1:
        return gridded
    cut = gridded.reshape(2, blocks // share // 2, share, comps, groups, rows, cycle_local)
    cut = jnp.stack([cut[0], jnp.flip(cut[1], axis=1)])
    cut = cut.transpose(0, 1, 3, 4, 5, 2, 6)
    return cut.reshape(blocks // share, comps, groups, rows, LANES)


def pack_comps(gridded):
    blocks, comps, groups, rows, cycle_local = gridded.shape
    if cycle_local == LANES:
        return gridded
    side = gridded.transpose(0, 2, 3, 1, 4).reshape(blocks, 1, groups, rows, comps * cycle_local)
    extra = -(comps * cycle_local) % LANES
    return jnp.pad(side, ((0, 0),) * 4 + ((0, extra),))


def unpack_comps(gridded, comps, cycle_local):
    if cycle_local == LANES:
        return gridded
    blocks, _, groups, rows, _ = gridded.shape
    side = gridded[..., : comps * cycle_local]
    side = side.reshape(blocks, groups, rows, comps, cycle_local)
    return side.transpose(0, 3, 1, 2, 4)


def shards(strain_spec, order_map, viscosity, radial_weight):
    comps, shells, slots, parts, degrees = strain_spec.shape
    block_count = lax.axis_size("blk")
    block = lax.axis_index("blk")
    cycle_local = viscosity.shape[1]
    cycle_count = cycle_local * block_count
    half_cycles = cycle_count // 2
    points = viscosity.shape[2]
    groups = slots // ORD
    chunks = degrees // CHUNK

    rank_all = rank_orders(order_map.reshape(block_count, slots))
    sorted_all = apply_rank(order_map.reshape(block_count, slots), rank_all)
    rank = lax.dynamic_index_in_dim(rank_all, block, 0, keepdims=False)
    sorted_orders = lax.dynamic_index_in_dim(sorted_all, block, 0, keepdims=False)
    by_group = sorted_orders.reshape(groups, ORD)
    first = by_group[:, 0] // CHUNK
    order = sorted_orders.astype(jnp.float32)
    counter = jnp.arange(1, degrees, dtype=jnp.float32)
    logs = jnp.where(counter <= order[:, None], jnp.log(1.0 - 0.5 / counter), 0.0)
    starts = 0.5 * jnp.log((2.0 * order + 1.0) / (4.0 * math.pi)) + 0.5 * jnp.sum(logs, axis=1)
    order_lanes = lane_fill(order)

    cycle_index = jnp.arange(half_cycles, dtype=jnp.float32)
    colatitude = math.pi * (2.0 * cycle_index + 1.0) / (2.0 * cycle_count)
    geometry = jnp.stack([2.0 * jnp.cos(colatitude), jnp.log(jnp.sin(colatitude))])

    row_rank = rank // ORD * (2 * ORD) + rank % ORD
    row_rank = (row_rank[:, None] + ORD * jnp.arange(2, dtype=jnp.int32)).reshape(-1)
    place = jnp.arange(slots * 2, dtype=jnp.int32)
    hit = row_rank[None, :] == place[:, None]
    my_orders = lax.dynamic_index_in_dim(
        order_map.reshape(block_count, slots), block, 0, keepdims=False
    )
    doubling = jnp.repeat(jnp.where(my_orders == 0, 1.0, 2.0), 2)
    place_in = jnp.where(hit, doubling[None, :], 0.0).astype(jnp.bfloat16)
    place_out = hit.T.astype(jnp.bfloat16)

    spectra = strain_spec.reshape(comps, slots * parts, degrees)
    part_count = 2
    part_groups = groups // part_count
    part_rows = part_groups * 2 * ORD
    sections = [slice(i * part_groups, (i + 1) * part_groups) for i in range(part_count)]
    signs = [1.0 if i < part_count // 2 else -1.0 for i in range(part_count)]
    start_lanes, degree_table = lane_fill(starts), degree_rows(degrees)
    received, tables = [], []
    for i, part in enumerate(sections):
        gridded, table, kappa = run_synth(
            first[part],
            spectra,
            place_in[i * part_rows : (i + 1) * part_rows],
            order_lanes[part],
            start_lanes[part],
            degree_table,
            geometry,
            chunks,
            signs[i],
        )
        tables.append((table, kappa))
        arrived = lax.all_to_all(to_blocks(gridded, cycle_local), "blk", 0, 0, tiled=True)
        received.append(pack_comps(arrived))

    forward, backward = wave_tables(sorted_all, points, groups)
    weights = fejer_weights(cycle_count)[None, :]
    gather = gather_matrix()
    forward, weights, gather = lax.optimization_barrier((forward, weights, gather))
    mirror = jnp.arange(cycle_local, dtype=jnp.int32)
    mirror = jnp.where(block * 2 < block_count, mirror, cycle_local - 1 - mirror)
    turn = (mirror[None, :] == jnp.arange(cycle_local, dtype=jnp.int32)[:, None]).astype(jnp.float32)
    local = jnp.einsum("jk,ji->ki", viscosity[0], turn, precision=lax.Precision.HIGHEST)
    if cycle_local < LANES:
        local = jnp.concatenate([local] * comps, axis=1)
        local = jnp.pad(local, ((0, 0), (0, -local.shape[1] % LANES)))
    spectrum = run_grid(received, forward, backward, local, 2.0 * math.pi / points)
    returned = [
        lax.all_to_all(unpack_comps(piece, comps, cycle_local), "blk", 0, 0, tiled=True)
        for piece in spectrum
    ]

    shell_count = lax.axis_size("shell")
    ordered, shared = [], []
    for i, part in enumerate(sections):
        table, kappa = tables[i]
        coefs, weighted = run_analysis(
            first[part],
            radial_weight,
            from_blocks(returned[i], cycle_local),
            table,
            kappa,
            gather,
            weights,
            shell_count,
            signs[i],
        )
        ordered.append(coefs)
        shared.append(lax.all_to_all(weighted, "shell", 0, 0, tiled=True))
    stress = run_place(
        unsort_kernel,
        place_out,
        ordered,
        jax.ShapeDtypeStruct((comps, slots * parts, degrees), jnp.bfloat16),
        part_rows,
    )
    integrated = run_place(
        shell_sum_kernel,
        place_out,
        shared,
        jax.ShapeDtypeStruct((comps, slots * parts, degrees // shell_count), jnp.float32),
        part_rows,
    )
    stress_spec = stress.reshape(strain_spec.shape)
    return (stress_spec, integrated.reshape(comps, slots, parts, degrees // shell_count))


def solution(mesh):
    return jax.shard_map(
        shards,
        mesh=mesh,
        in_specs=(P(None, "shell", "blk", None, None), P(), P("shell", "blk", None), P("shell")),
        out_specs=(P(None, "shell", "blk", None, None), P(None, "blk", None, "shell")),
        check_vma=False,
    )
```

```python
import functools
import math

import jax
import jax.numpy as jnp
from jax import lax
from jax.experimental import pallas as pl
from jax.experimental.pallas import tpu as pltpu
from jax.sharding import PartitionSpec as P

two_power = 1099511627776.0
inverse_power = 1.0 / 1099511627776.0
log_jump = 40.0 * math.log(2.0)

ORD = 8
CHUNK = 128
BLOCK = 16
LANES = 128
TILE = 256
SLOTS = 4
VMEM_LIMIT = 56 * 1024 * 1024


def fejer_weights(cycle_count):
    half_count = cycle_count // 2
    cycle_index = jnp.arange(half_count, dtype=jnp.int32)
    wave_number = jnp.arange(1, half_count + 1, dtype=jnp.int32)
    phase_index = wave_number[:, None] * (2 * cycle_index[None, :] + 1) % (2 * cycle_count)
    angles = phase_index.astype(jnp.float32) * (math.pi / cycle_count)
    wave_float = wave_number.astype(jnp.float32)
    divisor = 4.0 * wave_float * wave_float - 1.0
    series = jnp.sum(jnp.cos(angles) / divisor[:, None], axis=0)
    return 2.0 / cycle_count * (1.0 - 2.0 * series)


def late_share(groups):
    return groups // 4


def rank_orders(orders):
    groups = orders.shape[-1] // ORD
    half, late = groups // 2, late_share(groups)
    key = orders + (orders % 2) * (1 << 20)
    rank = jnp.sum((key[..., None, :] < key[..., :, None]).astype(jnp.int32), axis=-1)
    parity = (rank >= half * ORD).astype(jnp.int32)
    group = rank // ORD - parity * half
    early = 2 * late + parity * (half - late) + group - late
    return jnp.where(group < late, parity * late + group, early) * ORD + rank % ORD


def apply_rank(values, rank):
    count = rank.shape[-1]
    place = jnp.arange(count, dtype=jnp.int32)
    hit = rank[..., :, None] == place
    return jnp.sum(jnp.where(hit, values[..., :, None], 0), axis=-2)


def gather_matrix():
    place = jnp.arange(CHUNK * ORD, dtype=jnp.int32)
    parity = place // (CHUNK * ORD // 2)
    degree = 2 * (place % (CHUNK * ORD // 2) // ORD) + parity
    row = jnp.arange(CHUNK, dtype=jnp.int32)
    return (row[:, None] == degree[None, :]).astype(jnp.bfloat16)


def fill_degrees(degree_ref):
    row = lax.broadcasted_iota(jnp.int32, degree_ref.shape[1:], 0)
    below = row.astype(jnp.float32) - 1.0
    square = 4.0 * below * below
    degree_ref[0] = square / (square - 1.0)
    degree_ref[1] = 4.0 / (square - 1.0)


def kappa_lanes(order):
    lane = lax.broadcasted_iota(jnp.int32, order.shape, 1)
    degree = lane.astype(jnp.float32)
    square = degree * degree
    gap = jnp.maximum(square - order * order, 1.0)
    kappa = jnp.where(degree > order, jnp.sqrt((square - 0.25) / gap), 1.0)
    step = 1
    while step < BLOCK:
        moved = pltpu.roll(kappa, step, 1)
        kappa = kappa * jnp.where(lane % BLOCK >= step, moved, 1.0)
        step *= 2
    return kappa


def synth_kernel(
    comps,
    groups,
    chunks,
    base,
    first_ref,
    spec_ref,
    place_ref,
    lanes_ref,
    geometry_ref,
    out_ref,
    table_ref,
    kappa_ref,
    degree_ref,
    sorted_ref,
    even_ref,
    odd_ref,
    prev_ref,
    last_row_ref,
    log_ref,
    end_ref,
    wide_ref,
    buffer_ref,
    second_ref,
    sems,
):
    rows = 2 * ORD
    half = CHUNK * ORD // 2
    lane_blocks = geometry_ref.shape[1] // LANES
    own = place_ref[base * rows : (base + groups) * rows, :]
    fill_degrees(degree_ref)
    for c in range(comps):
        moved = jnp.dot(own, spec_ref[c], preferred_element_type=jnp.float32)
        sorted_ref[c] = moved.astype(jnp.bfloat16)
    degrees = chunks * CHUNK
    batch = next(n for n in (4, 3, 2, 1) if groups % n == 0)

    def fill_kappa(i, carry):
        order = lanes_ref[0, pl.ds(base + i * batch, batch)].reshape(batch * ORD, LANES)
        kappa = kappa_lanes(jnp.concatenate([order] * (degrees // LANES), axis=1))
        kappa = kappa.reshape(batch, ORD, degrees)
        kappa_ref[pl.ds(i * batch, batch)] = kappa
        for b in range(degrees // BLOCK):
            end = kappa[:, :, (b + 1) * BLOCK - 1 : (b + 1) * BLOCK]
            end_ref[pl.ds(i * batch, batch), b] = jnp.broadcast_to(end, (batch, ORD, LANES))
        return carry

    lax.fori_loop(0, groups // batch, fill_kappa, 0)
    shape = (rows, CHUNK * ORD)
    row_order = lax.broadcasted_iota(jnp.int32, shape, 0) % ORD
    lane_order = lax.broadcasted_iota(jnp.int32, shape, 1) % ORD
    mask = jnp.where(row_order == lane_order, 1.0, 0.0)
    count = lax.fori_loop(0, groups, lambda g, n: n + chunks - first_ref[base + g], jnp.int32(0))
    even_ref[...] = jnp.zeros_like(even_ref)
    odd_ref[...] = jnp.zeros_like(odd_ref)
    wide_ref[...] = jnp.zeros_like(wide_ref)
    second_ref[SLOTS // 2 - 1] = jnp.zeros_like(second_ref[SLOTS // 2 - 1])

    def table_copies(item, slot, which):
        offset = 0 if which is buffer_ref else SLOTS // 2
        return [
            pltpu.make_async_copy(
                which.at[slot, p], table_ref.at[item, p], sems.at[slot + offset, p]
            )
            for p in range(2)
        ]

    def products(other, before):
        even_ref[...] += jnp.dot(
            wide_ref[:, :half], other[before, 0], preferred_element_type=jnp.float32
        )
        odd_ref[...] += jnp.dot(
            wide_ref[:, half:], other[before, 1], preferred_element_type=jnp.float32
        )

    def recursion(group, chunk, slot, mine):
        order = lanes_ref[0, base + group]
        begin = chunk * CHUNK
        odd_chunk = lax.rem(chunk, LANES // CHUNK)
        lane = pl.multiple_of((chunk - odd_chunk) * CHUNK, LANES)
        kappa = kappa_ref[group, :, pl.ds(lane, LANES)]
        square = order * order
        seed_at = jnp.concatenate([order - begin.astype(jnp.float32)] * lane_blocks, axis=1)
        twice = geometry_ref[0:1, :]
        prev = prev_ref[...]
        last = last_row_ref[...]
        logs = log_ref[...]
        for b in range(CHUNK // BLOCK):
            scale = jnp.exp(logs)
            held = []
            for i in range(BLOCK):
                step = b * BLOCK + i
                one = degree_ref[0, pl.ds(begin + step, 1), :]
                two = degree_ref[1, pl.ds(begin + step, 1), :]
                coef = jnp.concatenate([one - two * square] * lane_blocks, axis=1)
                now = twice * last - coef * prev
                now = jnp.where(seed_at == float(step), 1.0, now)
                held.append(now * scale)
                prev, last = last, now
            for p in range(2):
                for i in range(p, BLOCK, 4):
                    pair = jnp.concatenate([held[i], held[i + 2]], axis=0).astype(jnp.bfloat16)
                    at = (b * BLOCK + i - p) // 2 * ORD
                    mine[slot, p, at : at + 2 * ORD, :] = pair
            end = end_ref[group, chunk * (CHUNK // BLOCK) + b]
            end = jnp.concatenate([end] * lane_blocks, axis=1)
            last = last * end
            prev = prev * end
            large = jnp.abs(last) > two_power
            factor = jnp.where(large, inverse_power, 1.0)
            last = last * factor
            prev = prev * factor
            logs = logs + jnp.where(large, log_jump, 0.0)
        prev_ref[...] = prev
        last_row_ref[...] = last
        log_ref[...] = logs
        at = pl.multiple_of(group * rows, rows)
        factors = jnp.concatenate([kappa, kappa], axis=0)
        piece = jnp.concatenate(
            [
                (sorted_ref[c, pl.ds(at, rows), pl.ds(lane, LANES)] * factors).astype(jnp.bfloat16)
                for c in range(comps)
            ],
            axis=0,
        )
        lane_at = lax.broadcasted_iota(jnp.int32, (rows, LANES), 1)
        for c in range(comps):
            source = piece[c * rows : (c + 1) * rows].astype(jnp.float32)
            for q in range(CHUNK * ORD // LANES):
                p, t = q // (CHUNK * ORD // LANES // 2), q % (CHUNK * ORD // LANES // 2)
                index = 2 * (lane_at // ORD + t * (LANES // ORD)) + p + odd_chunk * CHUNK
                moved = jnp.take_along_axis(source, index, axis=1)
                lanes = slice(q * LANES, (q + 1) * LANES)
                wide_ref[c * rows : (c + 1) * rows, lanes] = (moved * mask[:, lanes]).astype(jnp.bfloat16)

    def finish(group):
        sign = jnp.where(group < groups // 2, 1.0, -1.0)
        for c in range(comps):
            even = even_ref[c * rows : (c + 1) * rows, :]
            odd = odd_ref[c * rows : (c + 1) * rows, :]
            north = (even + odd).astype(jnp.bfloat16)
            south = (sign * (even - odd)).astype(jnp.bfloat16)
            for b in range(lane_blocks):
                lanes = slice(b * LANES, (b + 1) * LANES)
                out_ref[b, c, group] = north[:, lanes]
                out_ref[2 * lane_blocks - 1 - b, c, group] = south[:, lanes]
        even_ref[...] = jnp.zeros_like(even_ref)
        odd_ref[...] = jnp.zeros_like(odd_ref)

    def body(item, carry):
        before_group, before_chunk, group, chunk = carry
        for parity in range(2):

            @pl.when(jnp.logical_and(item >= SLOTS, lax.rem(item, 2) == parity))
            def _(parity=parity):
                which = second_ref if parity else buffer_ref
                for copy in table_copies(item - SLOTS, lax.rem(item // 2, SLOTS // 2), which):
                    copy.wait()

        @pl.when(chunk == first_ref[base + group])
        def _():
            prev_ref[...] = jnp.zeros_like(prev_ref)
            last_row_ref[...] = jnp.zeros_like(last_row_ref)
            wide_order = jnp.concatenate([lanes_ref[0, base + group]] * lane_blocks, axis=1)
            wide_start = jnp.concatenate([lanes_ref[1, base + group]] * lane_blocks, axis=1)
            log_ref[...] = wide_start + wide_order * geometry_ref[1:2, :]

        for parity in range(2):

            @pl.when(lax.rem(item, 2) == parity)
            def _(parity=parity):
                mine, other = (buffer_ref, second_ref) if parity == 0 else (second_ref, buffer_ref)
                place = lax.rem(item // 2, SLOTS // 2)
                before = lax.rem((item + SLOTS - 1) // 2, SLOTS // 2)
                products(other, before)
                recursion(group, chunk, place, mine)
                for copy in table_copies(item, place, mine):
                    copy.start()

        @pl.when(jnp.logical_and(before_chunk == chunks - 1, item > 0))
        def _():
            finish(before_group)

        done = chunk == chunks - 1
        next_group = jnp.minimum(group + done.astype(jnp.int32), groups - 1)
        next_chunk = jnp.where(done, first_ref[base + next_group], chunk + 1)
        return group, chunk, next_group, next_chunk

    zero = jnp.int32(0)
    lax.fori_loop(0, count, body, (zero, zero, zero, first_ref[base]))
    for parity in range(2):
        which = second_ref if parity else buffer_ref

        @pl.when(lax.rem(count - 1, 2) == parity)
        def _(which=which):
            products(which, lax.rem((count - 1) // 2, SLOTS // 2))

        for back in range(SLOTS, 0, -1):
            item = count - back

            @pl.when(jnp.logical_and(item >= 0, lax.rem(item + SLOTS, 2) == parity))
            def _(item=item, which=which):
                for copy in table_copies(item, lax.rem(item // 2, SLOTS // 2), which):
                    copy.wait()

    finish(jnp.int32(groups - 1))


def analysis_kernel(
    comps,
    groups,
    chunks,
    base,
    first_ref,
    radial_ref,
    grid_ref,
    table_ref,
    kappa_ref,
    gather_ref,
    weight_ref,
    sorted_ref,
    shared_ref,
    side_ref,
    wide_ref,
    found_ref,
    buffer_ref,
    sems,
):
    rows = 2 * ORD
    half = CHUNK * ORD // 2
    half_cycles = weight_ref.shape[1]
    degrees = chunks * CHUNK
    lane_blocks = half_cycles // LANES
    width = found_ref.shape[1]
    count = lax.fori_loop(0, groups, lambda g, n: n + chunks - first_ref[base + g], jnp.int32(0))
    shape = (ORD, width)
    lane = lax.broadcasted_iota(jnp.int32, shape, 1)
    own = lax.broadcasted_iota(jnp.int32, shape, 0) == lane % ORD
    mask = jnp.where(own, 1.0, 0.0)
    mask = jnp.concatenate([mask] * (half // ORD), axis=0)
    wide_ref[...] = jnp.zeros_like(wide_ref)
    radial = radial_ref[0]
    shells, share = shared_ref.shape[0], shared_ref.shape[3]

    def table_copies(item, slot):
        return [
            pltpu.make_async_copy(
                table_ref.at[item, p], buffer_ref.at[slot, p], sems.at[slot, p]
            )
            for p in range(2)
        ]

    for ahead in range(SLOTS - 1):

        @pl.when(ahead < count)
        def _():
            for copy in table_copies(ahead, ahead):
                copy.start()

    def narrow(chunk):
        found = jnp.dot(gather_ref[...], wide_ref[...], preferred_element_type=jnp.float32)
        found_ref[pl.ds(pl.multiple_of(chunk * CHUNK, CHUNK), CHUNK), :] = found.astype(
            jnp.bfloat16
        )

    def advance(group, chunk, carry):
        item, before = carry
        slot = lax.rem(item, SLOTS)
        ahead = item + SLOTS - 1

        @pl.when(ahead < count)
        def _():
            for copy in table_copies(ahead, lax.rem(ahead, SLOTS)):
                copy.start()

        for copy in table_copies(item, slot):
            copy.wait()
        narrow(before)
        for p in range(2):
            wide = jnp.dot(buffer_ref[slot, p], side_ref[p], preferred_element_type=jnp.float32)
            wide_ref[p * half : (p + 1) * half, :] = (wide * mask).astype(jnp.bfloat16)
        return item + 1, chunk

    def group_body(group, item):
        sign = jnp.where(group < groups // 2, 1.0, -1.0)
        for b in range(lane_blocks):
            lanes = slice(b * LANES, (b + 1) * LANES)
            weight = weight_ref[:, lanes]
            norths, souths = [], []
            for c in range(comps):
                norths.append(grid_ref[b, c, group].astype(jnp.float32))
                souths.append(sign * grid_ref[2 * lane_blocks - 1 - b, c, group].astype(jnp.float32))
            fill = jnp.zeros((width - comps * rows, LANES), jnp.float32)
            north = jnp.concatenate(norths + [fill], axis=0)
            south = jnp.concatenate(souths + [fill], axis=0)
            side_ref[0, lanes, :] = (weight * (north + south)).astype(jnp.bfloat16).T
            side_ref[1, lanes, :] = (weight * (north - south)).astype(jnp.bfloat16).T
        found_ref[...] = jnp.zeros_like(found_ref)
        item, before = lax.fori_loop(
            first_ref[base + group], chunks, functools.partial(advance, group), (item, jnp.int32(chunks))
        )
        narrow(before)
        turned = found_ref[:degrees].T.astype(jnp.float32)
        kappa = kappa_ref[group]
        at = pl.multiple_of(group * rows, rows)
        factors = jnp.concatenate([kappa, kappa], axis=0)
        for c in range(comps):
            piece = turned[c * rows : (c + 1) * rows] * factors
            sorted_ref[c, pl.ds(at, rows), :] = piece.astype(jnp.bfloat16)
            piece = (piece * radial).astype(jnp.bfloat16)
            for n in range(shells):
                shared_ref[n, c, pl.ds(at, rows), :] = piece[:, n * share : (n + 1) * share]
        return item

    lax.fori_loop(0, groups, group_body, jnp.int32(0))


def unsort_kernel(offsets, place_ref, *refs):
    out_ref = refs[-1]
    for c in range(out_ref.shape[0]):
        found = 0.0
        for offset, ref in zip(offsets, refs[:-1]):
            place = place_ref[:, offset : offset + ref.shape[1]]
            found += jnp.dot(place, ref[c], preferred_element_type=jnp.float32)
        out_ref[c] = found.astype(jnp.bfloat16)


def shell_sum_kernel(offset, place_ref, shared_ref, *refs):
    out_ref = refs[-1]
    place = place_ref[:, offset : offset + shared_ref.shape[2]]
    for c in range(out_ref.shape[0]):
        found = refs[0][c] if len(refs) > 1 else 0.0
        for n in range(shared_ref.shape[0]):
            found += jnp.dot(place, shared_ref[n, c], preferred_element_type=jnp.float32)
        out_ref[c] = found


def wave_kernel(forward_base, forward_turn, backward_base, backward_turn, forward_ref, backward_ref):
    points = forward_ref.shape[1]
    step = 512
    per = forward_ref.shape[2] // step

    def forward_lanes(i, carry):
        p, block = i // per, i % per
        at = pl.multiple_of(block * step, step)
        turn_cos = forward_turn[0, p, :, pl.ds(at, step)]
        turn_sin = forward_turn[1, p, :, pl.ds(at, step)]

        def turn(n, state):
            cos, sin = state
            later_cos = cos * turn_cos - sin * turn_sin
            later_sin = sin * turn_cos + cos * turn_sin
            rows = pl.ds(pl.multiple_of(n * 2 * ORD, 2 * ORD), 2 * ORD)
            forward_ref[p, rows, pl.ds(at, step)] = jnp.concatenate(
                [cos, later_cos], axis=0
            ).astype(jnp.bfloat16)
            cos = later_cos * turn_cos - later_sin * turn_sin
            sin = later_sin * turn_cos + later_cos * turn_sin
            return cos, sin

        state = (forward_base[0, p, :, pl.ds(at, step)], forward_base[1, p, :, pl.ds(at, step)])
        lax.fori_loop(0, points // (2 * ORD), turn, state)
        return carry

    lax.fori_loop(0, 2 * per, forward_lanes, 0)
    count = backward_base.shape[2]

    def backward_rows(i, carry):
        p, q = i // count, i % count
        real, imaginary = backward_base[0, p, q], backward_base[1, p, q]
        turn_cos, turn_sin = backward_turn[0, p, q], backward_turn[1, p, q]
        rows = pl.ds(pl.multiple_of(q * 2 * ORD, 2 * ORD), 2 * ORD)
        for a in range(points // LANES):
            backward_ref[p, rows, a * LANES : (a + 1) * LANES] = jnp.concatenate(
                [real, imaginary], axis=0
            ).astype(jnp.bfloat16)
            real, imaginary = (
                real * turn_cos + imaginary * turn_sin,
                imaginary * turn_cos - real * turn_sin,
            )
        return carry

    lax.fori_loop(0, 2 * count, backward_rows, 0)


def lay_field(grid_ref, field_ref, begin, end):
    blocks, packs, _, rows, lanes = grid_ref.shape
    count = (end - begin) * rows
    for w in range(packs):
        for d in range(blocks):
            field_ref[d * count : (d + 1) * count, w * lanes : (w + 1) * lanes] = grid_ref[
                d, w, begin:end
            ].reshape(count, lanes)


def early_field_kernel(grid_ref, even_wave_ref, odd_wave_ref, out_ref, field_ref):
    groups = grid_ref.shape[2] // 2
    depth = field_ref.shape[1]
    for p in range(2):
        lay_field(grid_ref, field_ref.at[p], p * groups, (p + 1) * groups)

    def step(i, carry):
        tile = pl.ds(pl.multiple_of(i * TILE, TILE), TILE)
        for p, wave_ref in enumerate((even_wave_ref, odd_wave_ref)):
            out_ref[0, p, tile, :] = jnp.dot(
                wave_ref[tile, :depth], field_ref[p], preferred_element_type=jnp.float32
            )
        return carry

    lax.fori_loop(0, out_ref.shape[2] // TILE, step, 0)


def lay_spectrum(norm, wave_ref, offset, stress, out_ref, begin, end):
    blocks, packs, _, rows, lanes = out_ref.shape
    count = (end - begin) * rows
    batch = math.gcd(blocks, max(1, TILE // count))

    def step(i, carry):
        at = pl.multiple_of(offset + i * (batch * count), 2 * ORD)
        found = jnp.dot(
            wave_ref[pl.ds(at, batch * count), :], stress[...], preferred_element_type=jnp.float32
        )
        found = (found * norm).astype(jnp.bfloat16)
        for n in range(batch):
            piece = found[n * count : (n + 1) * count]
            for w in range(packs):
                out_ref[i * batch + n, w, begin:end] = piece[
                    :, w * lanes : (w + 1) * lanes
                ].reshape(end - begin, rows, lanes)
        return carry

    lax.fori_loop(0, blocks // batch, step, 0)


def stress_kernel(norm, packs, late, early_depth, *refs):
    refs = list(refs)
    grid_ref = refs.pop(0) if late else None
    early_ref, even_wave_ref, odd_wave_ref, even_back_ref, odd_back_ref, viscosity_ref = refs[:6]
    total_ref = refs[6]
    out_ref, field_ref = refs[7:] if late else (None, None)
    points = even_wave_ref.shape[0]
    for p in range(2):
        if late:
            lay_field(grid_ref, field_ref.at[p], p * late, (p + 1) * late)

    def step(i, carry):
        at = pl.multiple_of(i * TILE, TILE)
        tile = pl.ds(at, TILE)
        fields = []
        for p, wave_ref in enumerate((even_wave_ref, odd_wave_ref)):
            field = early_ref[0, p, tile, :]
            if late:
                field += jnp.dot(
                    wave_ref[tile, early_depth:], field_ref[p], preferred_element_type=jnp.float32
                )
            fields.append(field)
        even, odd = fields
        near = jnp.concatenate([viscosity_ref[tile, :]] * packs, axis=1)
        far = jnp.concatenate([viscosity_ref[pl.ds(points + at, TILE), :]] * packs, axis=1)
        near = (near * (even + odd)).astype(jnp.bfloat16).astype(jnp.float32)
        far = (far * (even - odd)).astype(jnp.bfloat16).astype(jnp.float32)
        total_ref[0, 0, tile, :] = (near + far).astype(jnp.bfloat16)
        total_ref[0, 1, tile, :] = (near - far).astype(jnp.bfloat16)
        return carry

    lax.fori_loop(0, points // TILE, step, 0)
    for p, back_ref in enumerate((even_back_ref, odd_back_ref)):
        if late:
            lay_spectrum(
                norm, back_ref, early_depth, total_ref.at[0, p], out_ref, p * late, (p + 1) * late
            )


def early_spectrum_kernel(norm, total_ref, even_back_ref, odd_back_ref, out_ref):
    groups = out_ref.shape[2] // 2
    for p, back_ref in enumerate((even_back_ref, odd_back_ref)):
        lay_spectrum(
            norm, back_ref, 0, total_ref.at[0, p], out_ref, p * groups, (p + 1) * groups
        )


def whole(shape):
    return pl.BlockSpec(shape, lambda *_: (0,) * len(shape))


def params(flops, nbytes):
    return dict(
        compiler_params=pltpu.CompilerParams(vmem_limit_bytes=VMEM_LIMIT),
        cost_estimate=pl.CostEstimate(flops=flops, bytes_accessed=nbytes, transcendentals=0),
    )


def run_synth(first, spectra, place, order_lanes, geometry, chunks, base, groups):
    comps, slots, degrees = spectra.shape
    half_cycles = geometry.shape[1]
    blocks = 2 * half_cycles // LANES
    rows = 2 * ORD
    half = CHUNK * ORD // 2
    smem = pl.BlockSpec(memory_space=pltpu.SMEM)
    vmem = pl.BlockSpec(memory_space=pltpu.VMEM)
    return pl.pallas_call(
        functools.partial(synth_kernel, comps, groups, chunks, base),
        out_shape=(
            jax.ShapeDtypeStruct((blocks, comps, groups, rows, LANES), jnp.bfloat16),
            jax.ShapeDtypeStruct((groups * chunks, 2, half, half_cycles), jnp.bfloat16),
            jax.ShapeDtypeStruct((groups, ORD, degrees), jnp.float32),
        ),
        in_specs=[smem] + [vmem] * 4,
        out_specs=(vmem, pl.BlockSpec(memory_space=pl.ANY), vmem),
        scratch_shapes=[
            pltpu.VMEM((2, degrees, LANES), jnp.float32),
            pltpu.VMEM((comps, groups * rows, degrees), jnp.bfloat16),
            pltpu.VMEM((comps * rows, half_cycles), jnp.float32),
            pltpu.VMEM((comps * rows, half_cycles), jnp.float32),
            pltpu.VMEM((ORD, half_cycles), jnp.float32),
            pltpu.VMEM((ORD, half_cycles), jnp.float32),
            pltpu.VMEM((ORD, half_cycles), jnp.float32),
            pltpu.VMEM((groups, degrees // BLOCK, ORD, LANES), jnp.float32),
            pltpu.VMEM((comps * rows, CHUNK * ORD), jnp.bfloat16),
            pltpu.VMEM((SLOTS // 2, 2, half, half_cycles), jnp.bfloat16),
            pltpu.VMEM((SLOTS // 2, 2, half, half_cycles), jnp.bfloat16),
            pltpu.SemaphoreType.DMA((SLOTS, 2)),
        ],
        name="synthesis",
        **params(groups * chunks * 2 * comps * rows * 2 * half * half_cycles, 40 << 20),
    )(first, spectra, place, order_lanes, geometry)


def run_analysis(first, radial_weight, gridded, table, kappa, gather, weights, shells, base):
    blocks, comps, groups, rows, _ = gridded.shape
    half_cycles = weights.shape[1]
    half = CHUNK * ORD // 2
    degrees = kappa.shape[2]
    chunks = degrees // CHUNK
    width = -(-comps * rows // LANES) * LANES
    smem = pl.BlockSpec(memory_space=pltpu.SMEM)
    vmem = pl.BlockSpec(memory_space=pltpu.VMEM)
    return pl.pallas_call(
        functools.partial(analysis_kernel, comps, groups, chunks, base),
        out_shape=(
            jax.ShapeDtypeStruct((comps, groups * rows, degrees), jnp.bfloat16),
            jax.ShapeDtypeStruct((shells, comps, groups * rows, degrees // shells), jnp.bfloat16),
        ),
        in_specs=[smem, smem, vmem, pl.BlockSpec(memory_space=pl.ANY)] + [vmem] * 3,
        out_specs=(vmem, vmem),
        scratch_shapes=[
            pltpu.VMEM((2, half_cycles, width), jnp.bfloat16),
            pltpu.VMEM((2 * half, width), jnp.bfloat16),
            pltpu.VMEM((degrees + CHUNK, width), jnp.bfloat16),
            pltpu.VMEM((SLOTS, 2, half, half_cycles), jnp.bfloat16),
            pltpu.SemaphoreType.DMA((SLOTS, 2)),
        ],
        name="analysis",
        **params(groups * chunks * 2 * comps * rows * 2 * half * half_cycles, 40 << 20),
    )(first, radial_weight, gridded, table, kappa, gather, weights)


def run_grid(received, forward, backward, viscosity, norm):
    blocks, comps, early_groups, rows, lanes = received[0].shape
    late_groups = received[1].shape[2] if len(received) > 1 else 0
    packs = 2 if comps % 2 == 0 else 1
    steps = comps // packs
    _, half_points, depth = forward.shape
    width = packs * lanes
    early_depth = blocks * early_groups // 2 * rows

    def part(groups):
        return pl.BlockSpec((blocks, packs, groups, rows, lanes), lambda i: (0, i, 0, 0, 0))

    def wave(p, shape):
        return pl.BlockSpec((None,) + shape, lambda i: (p, 0, 0))

    fields = pl.BlockSpec((1, 2, half_points, width), lambda i: (i, 0, 0, 0))
    fields_shape = (steps, 2, half_points, width)
    forward_specs = [wave(p, (half_points, depth)) for p in range(2)]
    backward_specs = [wave(p, (depth, half_points)) for p in range(2)]
    one_product = 2 * steps * width * depth * half_points
    early_field = pl.pallas_call(
        early_field_kernel,
        out_shape=jax.ShapeDtypeStruct(fields_shape, jnp.float32),
        grid=(steps,),
        in_specs=[part(early_groups)] + forward_specs,
        out_specs=fields,
        scratch_shapes=[pltpu.VMEM((2, early_depth, width), jnp.bfloat16)],
        name="early_field",
        **params(one_product, 8 << 20),
    )(received[0], forward, forward)
    total_type = jax.ShapeDtypeStruct(fields_shape, jnp.bfloat16)
    late_type = [jax.ShapeDtypeStruct(piece.shape, jnp.bfloat16) for piece in received[1:]]
    late_scratch = pltpu.VMEM((2, depth - early_depth, width), jnp.bfloat16)
    total, *late = pl.pallas_call(
        functools.partial(stress_kernel, norm, packs, late_groups // 2, early_depth),
        out_shape=[total_type] + late_type,
        grid=(steps,),
        in_specs=[part(late_groups)] * len(late_type)
        + [fields]
        + forward_specs
        + backward_specs
        + [whole(viscosity.shape)],
        out_specs=[fields] + [part(late_groups)] * len(late_type),
        scratch_shapes=[late_scratch] * len(late_type),
        name="stress",
        **params(2 * one_product, 16 << 20),
    )(*received[1:], early_field, forward, forward, backward, backward, viscosity)
    early = pl.pallas_call(
        functools.partial(early_spectrum_kernel, norm),
        out_shape=jax.ShapeDtypeStruct(received[0].shape, jnp.bfloat16),
        grid=(steps,),
        in_specs=[fields] + backward_specs,
        out_specs=part(early_groups),
        name="early_spectrum",
        **params(one_product, 6 << 20),
    )(total, backward, backward)
    return [early] + late


def run_place(kernel, place, pieces, out_shape):
    vmem = pl.BlockSpec(memory_space=pltpu.VMEM)
    return pl.pallas_call(
        kernel,
        out_shape=out_shape,
        in_specs=[vmem] * (1 + len(pieces)),
        out_specs=vmem,
        name="natural_order",
        **params(2 * place.shape[1] * math.prod(out_shape.shape), 8 << 20),
    )(place, *pieces)


def wave_tables(sorted_all, point_count, groups):
    half_points = point_count // 2
    late = late_share(groups)
    early = groups // 2 - late
    by_group = sorted_all.reshape(sorted_all.shape[0], groups, ORD)
    orders = []
    for p in range(2):
        begin = 2 * late + p * early
        first = by_group[:, begin : begin + early].reshape(-1, ORD)
        second = by_group[:, p * late : (p + 1) * late].reshape(-1, ORD)
        orders.append(jnp.concatenate([first, second], axis=0))
    orders = jnp.stack(orders)
    shape = (2, orders.shape[1], 2, ORD)
    depth = math.prod(shape[1:])
    shift = jnp.arange(2, dtype=jnp.int32)[:, None] * (point_count // 4)
    lane_orders = jnp.broadcast_to(orders[:, :, None], shape).reshape(2, 1, depth)
    lane_shift = jnp.broadcast_to(shift, shape).reshape(2, 1, depth)

    def angle(phase):
        return (phase % point_count).astype(jnp.float32) * (2.0 * math.pi / point_count)

    def both(phase):
        return jnp.stack([jnp.cos(angle(phase)), jnp.sin(angle(phase))])

    rows = jnp.arange(ORD, dtype=jnp.int32)[None, :, None]
    forward_base = both(lane_orders * rows + lane_shift)
    forward_turn = both(lane_orders * ORD)
    row_orders = orders.reshape(2, depth // (2 * ORD), ORD, 1)
    longitudes = jnp.arange(LANES, dtype=jnp.int32)
    angles = angle(row_orders * longitudes)
    backward_base = jnp.stack([jnp.cos(angles), -jnp.sin(angles)])
    turn_shape = (2, 2, depth // (2 * ORD), ORD, LANES)
    backward_turn = jnp.broadcast_to(both(row_orders * LANES), turn_shape)
    vmem = pl.BlockSpec(memory_space=pltpu.VMEM)
    return pl.pallas_call(
        wave_kernel,
        out_shape=(
            jax.ShapeDtypeStruct((2, half_points, depth), jnp.bfloat16),
            jax.ShapeDtypeStruct((2, depth, half_points), jnp.bfloat16),
        ),
        in_specs=[vmem] * 4,
        out_specs=(vmem, vmem),
        name="waves",
        **params(8 * depth * half_points, 12 << 20),
    )(forward_base, forward_turn, backward_base, backward_turn)


def to_blocks(gridded, cycle_local):
    blocks, comps, groups, rows, _ = gridded.shape
    share = LANES // cycle_local
    if share == 1:
        return gridded
    cut = gridded.reshape(2, blocks // 2, comps, groups, rows, share, cycle_local)
    cut = cut.transpose(0, 1, 5, 2, 3, 4, 6)
    cut = jnp.stack([cut[0], jnp.flip(cut[1], axis=1)])
    return cut.reshape(blocks * share, comps, groups, rows, cycle_local)


def from_blocks(gridded, cycle_local):
    blocks, comps, groups, rows, _ = gridded.shape
    share = LANES // cycle_local
    if share == 1:
        return gridded
    cut = gridded.reshape(2, blocks // share // 2, share, comps, groups, rows, cycle_local)
    cut = jnp.stack([cut[0], jnp.flip(cut[1], axis=1)])
    cut = cut.transpose(0, 1, 3, 4, 5, 2, 6)
    return cut.reshape(blocks // share, comps, groups, rows, LANES)


def pack_comps(gridded):
    blocks, comps, groups, rows, cycle_local = gridded.shape
    if cycle_local == LANES:
        return gridded
    side = gridded.transpose(0, 2, 3, 1, 4).reshape(blocks, 1, groups, rows, comps * cycle_local)
    extra = -(comps * cycle_local) % LANES
    return jnp.pad(side, ((0, 0),) * 4 + ((0, extra),))


def unpack_comps(gridded, comps, cycle_local):
    if cycle_local == LANES:
        return gridded
    blocks, _, groups, rows, _ = gridded.shape
    side = gridded[..., : comps * cycle_local]
    side = side.reshape(blocks, groups, rows, comps, cycle_local)
    return side.transpose(0, 3, 1, 2, 4)


def shards(strain_spec, order_map, viscosity, radial_weight):
    comps, shells, slots, parts, degrees = strain_spec.shape
    block_count = lax.axis_size("blk")
    block = lax.axis_index("blk")
    cycle_local = viscosity.shape[1]
    cycle_count = cycle_local * block_count
    half_cycles = cycle_count // 2
    points = viscosity.shape[2]
    groups = slots // ORD
    chunks = degrees // CHUNK

    rank_all = rank_orders(order_map.reshape(block_count, slots))
    sorted_all = apply_rank(order_map.reshape(block_count, slots), rank_all)
    rank = lax.dynamic_index_in_dim(rank_all, block, 0, keepdims=False)
    sorted_orders = lax.dynamic_index_in_dim(sorted_all, block, 0, keepdims=False)
    by_group = sorted_orders.reshape(groups, ORD)
    first = by_group[:, 0] // CHUNK
    order = sorted_orders.astype(jnp.float32)
    counter = jnp.arange(1, degrees, dtype=jnp.float32)
    logs = jnp.where(counter <= order[:, None], jnp.log(1.0 - 0.5 / counter), 0.0)
    starts = 0.5 * jnp.log((2.0 * order + 1.0) / (4.0 * math.pi)) + 0.5 * jnp.sum(logs, axis=1)
    order_lanes = jnp.broadcast_to(
        jnp.stack([order, starts]).reshape(2, groups, ORD, 1), (2, groups, ORD, LANES)
    )

    cycle_index = jnp.arange(half_cycles, dtype=jnp.float32)
    colatitude = math.pi * (2.0 * cycle_index + 1.0) / (2.0 * cycle_count)
    geometry = jnp.stack([2.0 * jnp.cos(colatitude), jnp.log(jnp.sin(colatitude))])

    row_rank = rank // ORD * (2 * ORD) + rank % ORD
    row_rank = (row_rank[:, None] + ORD * jnp.arange(2, dtype=jnp.int32)).reshape(-1)
    place = jnp.arange(slots * 2, dtype=jnp.int32)
    hit = row_rank[None, :] == place[:, None]
    my_orders = lax.dynamic_index_in_dim(
        order_map.reshape(block_count, slots), block, 0, keepdims=False
    )
    doubling = jnp.repeat(jnp.where(my_orders == 0, 1.0, 2.0), 2)
    place_in = jnp.where(hit, doubling[None, :], 0.0).astype(jnp.bfloat16)
    place_out = hit.T.astype(jnp.bfloat16)

    spectra = strain_spec.reshape(comps, slots * parts, degrees)
    late = late_share(groups)
    spans = [(2 * late, groups - 2 * late)] + ([(0, 2 * late)] if late else [])
    received, tables = [], []
    for base, count in spans:
        gridded, table, kappa = run_synth(
            first, spectra, place_in, order_lanes, geometry, chunks, base, count
        )
        tables.append((table, kappa))
        arrived = lax.all_to_all(to_blocks(gridded, cycle_local), "blk", 0, 0, tiled=True)
        received.append(pack_comps(arrived))

    forward, backward = wave_tables(sorted_all, points, groups)
    weights = fejer_weights(cycle_count)[None, :]
    gather = gather_matrix()
    forward, weights, gather = lax.optimization_barrier((forward, weights, gather))
    mirror = jnp.arange(cycle_local, dtype=jnp.int32)
    mirror = jnp.where(block * 2 < block_count, mirror, cycle_local - 1 - mirror)
    turn = (mirror[None, :] == jnp.arange(cycle_local, dtype=jnp.int32)[:, None]).astype(jnp.float32)
    local = jnp.einsum("jk,ji->ki", viscosity[0], turn, precision=lax.Precision.HIGHEST)
    if cycle_local < LANES:
        local = jnp.concatenate([local] * comps, axis=1)
        local = jnp.pad(local, ((0, 0), (0, -local.shape[1] % LANES)))
    spectrum = run_grid(received, forward, backward, local, 2.0 * math.pi / points)
    returned = [
        lax.all_to_all(unpack_comps(piece, comps, cycle_local), "blk", 0, 0, tiled=True)
        for piece in spectrum
    ]

    shell_count = lax.axis_size("shell")
    ordered, offsets, integrated = [], [], []
    sum_type = jax.ShapeDtypeStruct((comps, slots * parts, degrees // shell_count), jnp.float32)
    for i in reversed(range(len(spans))):
        base = spans[i][0]
        table, kappa = tables[i]
        coefs, weighted = run_analysis(
            first,
            radial_weight,
            from_blocks(returned[i], cycle_local),
            table,
            kappa,
            gather,
            weights,
            shell_count,
            base,
        )
        ordered.append(coefs)
        offsets.append(base * 2 * ORD)
        shared = lax.all_to_all(weighted, "shell", 0, 0, tiled=True)
        kernel = functools.partial(shell_sum_kernel, offsets[-1])
        integrated = [run_place(kernel, place_out, [shared] + integrated, sum_type)]
    stress = run_place(
        functools.partial(unsort_kernel, offsets),
        place_out,
        ordered,
        jax.ShapeDtypeStruct((comps, slots * parts, degrees), jnp.bfloat16),
    )
    integrated = integrated[0]
    stress_spec = stress.reshape(strain_spec.shape)
    return (stress_spec, integrated.reshape(comps, slots, parts, degrees // shell_count))


def solution(mesh):
    return jax.shard_map(
        shards,
        mesh=mesh,
        in_specs=(P(None, "shell", "blk", None, None), P(), P("shell", "blk", None), P("shell")),
        out_specs=(P(None, "shell", "blk", None, None), P(None, "blk", None, "shell")),
        check_vma=False,
    )
```

```python
import functools
import math

import jax
import jax.numpy as jnp
from jax import lax
from jax.experimental import pallas as pl
from jax.experimental.pallas import tpu as pltpu
from jax.sharding import PartitionSpec as P

two_power = 1099511627776.0
inverse_power = 1.0 / 1099511627776.0
log_jump = 40.0 * math.log(2.0)

ORD = 8
CHUNK = 128
BLOCK = 16
LANES = 128
TILE = 256
SLOTS = 4
VMEM_LIMIT = 63 * 1024 * 1024


def fejer_weights(cycle_count):
    half_count = cycle_count // 2
    cycle_index = jnp.arange(half_count, dtype=jnp.int32)
    wave_number = jnp.arange(1, half_count + 1, dtype=jnp.int32)
    phase_index = wave_number[:, None] * (2 * cycle_index[None, :] + 1) % (2 * cycle_count)
    angles = phase_index.astype(jnp.float32) * (math.pi / cycle_count)
    wave_float = wave_number.astype(jnp.float32)
    divisor = 4.0 * wave_float * wave_float - 1.0
    series = jnp.sum(jnp.cos(angles) / divisor[:, None], axis=0)
    return 2.0 / cycle_count * (1.0 - 2.0 * series)


def late_share(groups):
    return groups // 4


def rank_orders(orders):
    groups = orders.shape[-1] // ORD
    half, late = groups // 2, late_share(groups)
    key = orders + (orders % 2) * (1 << 20)
    rank = jnp.sum((key[..., None, :] < key[..., :, None]).astype(jnp.int32), axis=-1)
    parity = (rank >= half * ORD).astype(jnp.int32)
    group = rank // ORD - parity * half
    early = 2 * late + parity * (half - late) + group - late
    return jnp.where(group < late, parity * late + group, early) * ORD + rank % ORD


def apply_rank(values, rank):
    count = rank.shape[-1]
    place = jnp.arange(count, dtype=jnp.int32)
    hit = rank[..., :, None] == place
    return jnp.sum(jnp.where(hit, values[..., :, None], 0), axis=-2)


def gather_matrix():
    place = jnp.arange(CHUNK * ORD, dtype=jnp.int32)
    parity = place // (CHUNK * ORD // 2)
    degree = 2 * (place % (CHUNK * ORD // 2) // ORD) + parity
    row = jnp.arange(CHUNK, dtype=jnp.int32)
    return (row[:, None] == degree[None, :]).astype(jnp.bfloat16)


def fill_degrees(degree_ref):
    row = lax.broadcasted_iota(jnp.int32, degree_ref.shape[1:], 0)
    below = row.astype(jnp.float32) - 1.0
    square = 4.0 * below * below
    degree_ref[0] = square / (square - 1.0)
    degree_ref[1] = 4.0 / (square - 1.0)


def kappa_lanes(order):
    lane = lax.broadcasted_iota(jnp.int32, order.shape, 1)
    degree = lane.astype(jnp.float32)
    square = degree * degree
    gap = jnp.maximum(square - order * order, 1.0)
    kappa = jnp.where(degree > order, jnp.sqrt((square - 0.25) / gap), 1.0)
    step = 1
    while step < BLOCK:
        moved = pltpu.roll(kappa, step, 1)
        kappa = kappa * jnp.where(lane % BLOCK >= step, moved, 1.0)
        step *= 2
    return kappa


def synth_kernel(
    comps,
    groups,
    chunks,
    base,
    first_ref,
    spec_ref,
    place_ref,
    lanes_ref,
    geometry_ref,
    out_ref,
    table_ref,
    kappa_ref,
    degree_ref,
    sorted_ref,
    even_ref,
    odd_ref,
    prev_ref,
    last_row_ref,
    log_ref,
    end_ref,
    wide_ref,
    buffer_ref,
    second_ref,
    sems,
):
    rows = 2 * ORD
    half = CHUNK * ORD // 2
    lane_blocks = geometry_ref.shape[1] // LANES
    own = place_ref[base * rows : (base + groups) * rows, :]
    fill_degrees(degree_ref)
    for c in range(comps):
        moved = jnp.dot(own, spec_ref[c], preferred_element_type=jnp.float32)
        sorted_ref[c] = moved.astype(jnp.bfloat16)
    degrees = chunks * CHUNK
    batch = next(n for n in (4, 3, 2, 1) if groups % n == 0)

    def fill_kappa(i, carry):
        order = lanes_ref[0, pl.ds(base + i * batch, batch)].reshape(batch * ORD, LANES)
        kappa = kappa_lanes(jnp.concatenate([order] * (degrees // LANES), axis=1))
        kappa = kappa.reshape(batch, ORD, degrees)
        kappa_ref[pl.ds(i * batch, batch)] = kappa
        for b in range(degrees // BLOCK):
            end = kappa[:, :, (b + 1) * BLOCK - 1 : (b + 1) * BLOCK]
            end_ref[pl.ds(i * batch, batch), b] = jnp.broadcast_to(end, (batch, ORD, LANES))
        return carry

    lax.fori_loop(0, groups // batch, fill_kappa, 0)
    shape = (rows, CHUNK * ORD)
    row_order = lax.broadcasted_iota(jnp.int32, shape, 0) % ORD
    lane_order = lax.broadcasted_iota(jnp.int32, shape, 1) % ORD
    mask = jnp.where(row_order == lane_order, 1.0, 0.0)
    count = lax.fori_loop(0, groups, lambda g, n: n + chunks - first_ref[base + g], jnp.int32(0))
    even_ref[...] = jnp.zeros_like(even_ref)
    odd_ref[...] = jnp.zeros_like(odd_ref)
    wide_ref[...] = jnp.zeros_like(wide_ref)
    second_ref[SLOTS // 2 - 1] = jnp.zeros_like(second_ref[SLOTS // 2 - 1])

    def table_copies(item, slot, which):
        offset = 0 if which is buffer_ref else SLOTS // 2
        return [
            pltpu.make_async_copy(
                which.at[slot, p], table_ref.at[item, p], sems.at[slot + offset, p]
            )
            for p in range(2)
        ]

    def products(other, before):
        even_ref[...] += jnp.dot(
            wide_ref[:, :half], other[before, 0], preferred_element_type=jnp.float32
        )
        odd_ref[...] += jnp.dot(
            wide_ref[:, half:], other[before, 1], preferred_element_type=jnp.float32
        )

    def recursion(seeded, group, chunk, slot, mine):
        order = lanes_ref[0, base + group]
        begin = chunk * CHUNK
        odd_chunk = lax.rem(chunk, LANES // CHUNK)
        lane = pl.multiple_of((chunk - odd_chunk) * CHUNK, LANES)
        kappa = kappa_ref[group, :, pl.ds(lane, LANES)]
        square = order * order
        seed_at = jnp.concatenate([order - begin.astype(jnp.float32)] * lane_blocks, axis=1)
        twice = geometry_ref[0:1, :]
        prev = prev_ref[...]
        last = last_row_ref[...]
        logs = log_ref[...]
        for b in range(CHUNK // BLOCK):
            scale = jnp.exp(logs)
            held = []
            for i in range(BLOCK):
                step = b * BLOCK + i
                one = degree_ref[0, pl.ds(begin + step, 1), :]
                two = degree_ref[1, pl.ds(begin + step, 1), :]
                coef = jnp.concatenate([one - two * square] * lane_blocks, axis=1)
                now = twice * last - coef * prev
                if seeded:
                    now = jnp.where(seed_at == float(step), 1.0, now)
                held.append(now * scale)
                prev, last = last, now
            for p in range(2):
                for i in range(p, BLOCK, 4):
                    pair = jnp.concatenate([held[i], held[i + 2]], axis=0).astype(jnp.bfloat16)
                    at = (b * BLOCK + i - p) // 2 * ORD
                    mine[slot, p, at : at + 2 * ORD, :] = pair
            end = end_ref[group, chunk * (CHUNK // BLOCK) + b]
            end = jnp.concatenate([end] * lane_blocks, axis=1)
            last = last * end
            prev = prev * end
            large = jnp.abs(last) > two_power
            factor = jnp.where(large, inverse_power, 1.0)
            last = last * factor
            prev = prev * factor
            logs = logs + jnp.where(large, log_jump, 0.0)
        prev_ref[...] = prev
        last_row_ref[...] = last
        log_ref[...] = logs
        at = pl.multiple_of(group * rows, rows)
        factors = jnp.concatenate([kappa, kappa], axis=0)
        piece = jnp.concatenate(
            [
                (sorted_ref[c, pl.ds(at, rows), pl.ds(lane, LANES)] * factors).astype(jnp.bfloat16)
                for c in range(comps)
            ],
            axis=0,
        )
        lane_at = lax.broadcasted_iota(jnp.int32, (rows, LANES), 1)
        for c in range(comps):
            source = piece[c * rows : (c + 1) * rows].astype(jnp.float32)
            for q in range(CHUNK * ORD // LANES):
                p, t = q // (CHUNK * ORD // LANES // 2), q % (CHUNK * ORD // LANES // 2)
                index = 2 * (lane_at // ORD + t * (LANES // ORD)) + p + odd_chunk * CHUNK
                moved = jnp.take_along_axis(source, index, axis=1)
                lanes = slice(q * LANES, (q + 1) * LANES)
                wide_ref[c * rows : (c + 1) * rows, lanes] = (moved * mask[:, lanes]).astype(jnp.bfloat16)

    def finish(group):
        sign = jnp.where(group < groups // 2, 1.0, -1.0)
        for c in range(comps):
            even = even_ref[c * rows : (c + 1) * rows, :]
            odd = odd_ref[c * rows : (c + 1) * rows, :]
            north = (even + odd).astype(jnp.bfloat16)
            south = (sign * (even - odd)).astype(jnp.bfloat16)
            for b in range(lane_blocks):
                lanes = slice(b * LANES, (b + 1) * LANES)
                out_ref[b, c, group] = north[:, lanes]
                out_ref[2 * lane_blocks - 1 - b, c, group] = south[:, lanes]
        even_ref[...] = jnp.zeros_like(even_ref)
        odd_ref[...] = jnp.zeros_like(odd_ref)

    def body(item, carry):
        before_group, before_chunk, group, chunk = carry
        for parity in range(2):

            @pl.when(jnp.logical_and(item >= SLOTS, lax.rem(item, 2) == parity))
            def _(parity=parity):
                which = second_ref if parity else buffer_ref
                for copy in table_copies(item - SLOTS, lax.rem(item // 2, SLOTS // 2), which):
                    copy.wait()

        @pl.when(chunk == first_ref[base + group])
        def _():
            prev_ref[...] = jnp.zeros_like(prev_ref)
            last_row_ref[...] = jnp.zeros_like(last_row_ref)
            wide_order = jnp.concatenate([lanes_ref[0, base + group]] * lane_blocks, axis=1)
            wide_start = jnp.concatenate([lanes_ref[1, base + group]] * lane_blocks, axis=1)
            log_ref[...] = wide_start + wide_order * geometry_ref[1:2, :]

        seeded = chunk <= first_ref[first_ref.shape[0] // 2 + base + group]
        for parity in range(2):
            mine, other = (buffer_ref, second_ref) if parity == 0 else (second_ref, buffer_ref)
            place = lax.rem(item // 2, SLOTS // 2)
            before = lax.rem((item + SLOTS - 1) // 2, SLOTS // 2)
            turn = lax.rem(item, 2) == parity
            for want in (True, False):

                @pl.when(jnp.logical_and(turn, seeded if want else jnp.logical_not(seeded)))
                def _(mine=mine, other=other, want=want):
                    products(other, before)
                    recursion(want, group, chunk, place, mine)
                    for copy in table_copies(item, place, mine):
                        copy.start()

        @pl.when(jnp.logical_and(before_chunk == chunks - 1, item > 0))
        def _():
            finish(before_group)

        done = chunk == chunks - 1
        next_group = jnp.minimum(group + done.astype(jnp.int32), groups - 1)
        next_chunk = jnp.where(done, first_ref[base + next_group], chunk + 1)
        return group, chunk, next_group, next_chunk

    zero = jnp.int32(0)
    lax.fori_loop(0, count, body, (zero, zero, zero, first_ref[base]))
    for parity in range(2):
        which = second_ref if parity else buffer_ref

        @pl.when(lax.rem(count - 1, 2) == parity)
        def _(which=which):
            products(which, lax.rem((count - 1) // 2, SLOTS // 2))

        for back in range(SLOTS, 0, -1):
            item = count - back

            @pl.when(jnp.logical_and(item >= 0, lax.rem(item + SLOTS, 2) == parity))
            def _(item=item, which=which):
                for copy in table_copies(item, lax.rem(item // 2, SLOTS // 2), which):
                    copy.wait()

    finish(jnp.int32(groups - 1))


def analysis_kernel(
    comps,
    groups,
    chunks,
    base,
    first_ref,
    radial_ref,
    grid_ref,
    table_ref,
    kappa_ref,
    gather_ref,
    weight_ref,
    sorted_ref,
    shared_ref,
    side_ref,
    wide_ref,
    found_ref,
    buffer_ref,
    sems,
):
    rows = 2 * ORD
    half = CHUNK * ORD // 2
    half_cycles = weight_ref.shape[1]
    degrees = chunks * CHUNK
    lane_blocks = half_cycles // LANES
    width = found_ref.shape[1]
    count = lax.fori_loop(0, groups, lambda g, n: n + chunks - first_ref[base + g], jnp.int32(0))
    shape = (ORD, width)
    lane = lax.broadcasted_iota(jnp.int32, shape, 1)
    own = lax.broadcasted_iota(jnp.int32, shape, 0) == lane % ORD
    mask = jnp.where(own, 1.0, 0.0)
    mask = jnp.concatenate([mask] * (half // ORD), axis=0)
    wide_ref[...] = jnp.zeros_like(wide_ref)
    radial = radial_ref[0]
    shells, share = shared_ref.shape[0], shared_ref.shape[3]

    def table_copies(item, slot):
        return [
            pltpu.make_async_copy(
                table_ref.at[item, p], buffer_ref.at[slot, p], sems.at[slot, p]
            )
            for p in range(2)
        ]

    for ahead in range(SLOTS - 1):

        @pl.when(ahead < count)
        def _():
            for copy in table_copies(ahead, ahead):
                copy.start()

    def narrow(chunk):
        found = jnp.dot(gather_ref[...], wide_ref[...], preferred_element_type=jnp.float32)
        found_ref[pl.ds(pl.multiple_of(chunk * CHUNK, CHUNK), CHUNK), :] = found.astype(
            jnp.bfloat16
        )

    def advance(group, chunk, carry):
        item, before = carry
        slot = lax.rem(item, SLOTS)
        ahead = item + SLOTS - 1

        @pl.when(ahead < count)
        def _():
            for copy in table_copies(ahead, lax.rem(ahead, SLOTS)):
                copy.start()

        for copy in table_copies(item, slot):
            copy.wait()
        narrow(before)
        for p in range(2):
            wide = jnp.dot(buffer_ref[slot, p], side_ref[p], preferred_element_type=jnp.float32)
            wide_ref[p * half : (p + 1) * half, :] = (wide * mask).astype(jnp.bfloat16)
        return item + 1, chunk

    def group_body(group, item):
        sign = jnp.where(group < groups // 2, 1.0, -1.0)
        for b in range(lane_blocks):
            lanes = slice(b * LANES, (b + 1) * LANES)
            weight = weight_ref[:, lanes]
            norths, souths = [], []
            for c in range(comps):
                norths.append(grid_ref[b, c, group].astype(jnp.float32))
                souths.append(sign * grid_ref[2 * lane_blocks - 1 - b, c, group].astype(jnp.float32))
            fill = jnp.zeros((width - comps * rows, LANES), jnp.float32)
            north = jnp.concatenate(norths + [fill], axis=0)
            south = jnp.concatenate(souths + [fill], axis=0)
            side_ref[0, lanes, :] = (weight * (north + south)).astype(jnp.bfloat16).T
            side_ref[1, lanes, :] = (weight * (north - south)).astype(jnp.bfloat16).T
        found_ref[...] = jnp.zeros_like(found_ref)
        item, before = lax.fori_loop(
            first_ref[base + group], chunks, functools.partial(advance, group), (item, jnp.int32(chunks))
        )
        narrow(before)
        turned = found_ref[:degrees].T.astype(jnp.float32)
        kappa = kappa_ref[group]
        at = pl.multiple_of(group * rows, rows)
        factors = jnp.concatenate([kappa, kappa], axis=0)
        for c in range(comps):
            piece = turned[c * rows : (c + 1) * rows] * factors
            sorted_ref[c, pl.ds(at, rows), :] = piece.astype(jnp.bfloat16)
            piece = (piece * radial).astype(jnp.bfloat16)
            for n in range(shells):
                shared_ref[n, c, pl.ds(at, rows), :] = piece[:, n * share : (n + 1) * share]
        return item

    lax.fori_loop(0, groups, group_body, jnp.int32(0))


def unsort_kernel(offsets, place_ref, *refs):
    out_ref = refs[-1]
    for c in range(out_ref.shape[0]):
        found = 0.0
        for offset, ref in zip(offsets, refs[:-1]):
            place = place_ref[:, offset : offset + ref.shape[1]]
            found += jnp.dot(place, ref[c], preferred_element_type=jnp.float32)
        out_ref[c] = found.astype(jnp.bfloat16)


def shell_sum_kernel(offset, place_ref, shared_ref, *refs):
    out_ref = refs[-1]
    place = place_ref[:, offset : offset + shared_ref.shape[2]]
    for c in range(out_ref.shape[0]):
        found = refs[0][c] if len(refs) > 1 else 0.0
        for n in range(shared_ref.shape[0]):
            found += jnp.dot(place, shared_ref[n, c], preferred_element_type=jnp.float32)
        out_ref[c] = found


def wave_kernel(forward_base, forward_turn, backward_base, backward_turn, forward_ref, backward_ref):
    points = forward_ref.shape[1]
    step = 512
    per = forward_ref.shape[2] // step

    def forward_lanes(i, carry):
        p, block = i // per, i % per
        at = pl.multiple_of(block * step, step)
        turn_cos = forward_turn[0, p, :, pl.ds(at, step)]
        turn_sin = forward_turn[1, p, :, pl.ds(at, step)]

        def turn(n, state):
            cos, sin = state
            later_cos = cos * turn_cos - sin * turn_sin
            later_sin = sin * turn_cos + cos * turn_sin
            rows = pl.ds(pl.multiple_of(n * 2 * ORD, 2 * ORD), 2 * ORD)
            forward_ref[p, rows, pl.ds(at, step)] = jnp.concatenate(
                [cos, later_cos], axis=0
            ).astype(jnp.bfloat16)
            cos = later_cos * turn_cos - later_sin * turn_sin
            sin = later_sin * turn_cos + later_cos * turn_sin
            return cos, sin

        state = (forward_base[0, p, :, pl.ds(at, step)], forward_base[1, p, :, pl.ds(at, step)])
        lax.fori_loop(0, points // (2 * ORD), turn, state)
        return carry

    lax.fori_loop(0, 2 * per, forward_lanes, 0)
    count = backward_base.shape[2]

    def backward_rows(i, carry):
        p, q = i // count, i % count
        real, imaginary = backward_base[0, p, q], backward_base[1, p, q]
        turn_cos, turn_sin = backward_turn[0, p, q], backward_turn[1, p, q]
        rows = pl.ds(pl.multiple_of(q * 2 * ORD, 2 * ORD), 2 * ORD)
        for a in range(points // LANES):
            backward_ref[p, rows, a * LANES : (a + 1) * LANES] = jnp.concatenate(
                [real, imaginary], axis=0
            ).astype(jnp.bfloat16)
            real, imaginary = (
                real * turn_cos + imaginary * turn_sin,
                imaginary * turn_cos - real * turn_sin,
            )
        return carry

    lax.fori_loop(0, 2 * count, backward_rows, 0)


def lay_field(grid_ref, field_ref, begin, end):
    blocks, packs, _, rows, lanes = grid_ref.shape
    count = (end - begin) * rows
    for w in range(packs):
        for d in range(blocks):
            field_ref[d * count : (d + 1) * count, w * lanes : (w + 1) * lanes] = grid_ref[
                d, w, begin:end
            ].reshape(count, lanes)


def early_field_kernel(grid_ref, even_wave_ref, odd_wave_ref, out_ref, field_ref):
    groups = grid_ref.shape[2] // 2
    depth = field_ref.shape[1]
    for p in range(2):
        lay_field(grid_ref, field_ref.at[p], p * groups, (p + 1) * groups)

    def step(i, carry):
        tile = pl.ds(pl.multiple_of(i * TILE, TILE), TILE)
        for p, wave_ref in enumerate((even_wave_ref, odd_wave_ref)):
            out_ref[0, p, tile, :] = jnp.dot(
                wave_ref[tile, :depth], field_ref[p], preferred_element_type=jnp.float32
            )
        return carry

    lax.fori_loop(0, out_ref.shape[2] // TILE, step, 0)


def lay_spectrum(norm, wave_ref, offset, stress, out_ref, begin, end):
    blocks, packs, _, rows, lanes = out_ref.shape
    count = (end - begin) * rows
    batch = math.gcd(blocks, max(1, TILE // count))

    def step(i, carry):
        at = pl.multiple_of(offset + i * (batch * count), 2 * ORD)
        found = jnp.dot(
            wave_ref[pl.ds(at, batch * count), :], stress[...], preferred_element_type=jnp.float32
        )
        found = (found * norm).astype(jnp.bfloat16)
        for n in range(batch):
            piece = found[n * count : (n + 1) * count]
            for w in range(packs):
                out_ref[i * batch + n, w, begin:end] = piece[
                    :, w * lanes : (w + 1) * lanes
                ].reshape(end - begin, rows, lanes)
        return carry

    lax.fori_loop(0, blocks // batch, step, 0)


def stress_kernel(norm, packs, late, early_depth, *refs):
    refs = list(refs)
    grid_ref = refs.pop(0) if late else None
    early_ref, even_wave_ref, odd_wave_ref, even_back_ref, odd_back_ref, viscosity_ref = refs[:6]
    total_ref = refs[6]
    out_ref, field_ref = refs[7:] if late else (None, None)
    points = even_wave_ref.shape[0]
    for p in range(2):
        if late:
            lay_field(grid_ref, field_ref.at[p], p * late, (p + 1) * late)

    def step(i, carry):
        at = pl.multiple_of(i * TILE, TILE)
        tile = pl.ds(at, TILE)
        fields = []
        for p, wave_ref in enumerate((even_wave_ref, odd_wave_ref)):
            field = early_ref[0, p, tile, :]
            if late:
                field += jnp.dot(
                    wave_ref[tile, early_depth:], field_ref[p], preferred_element_type=jnp.float32
                )
            fields.append(field)
        even, odd = fields
        near = jnp.concatenate([viscosity_ref[tile, :]] * packs, axis=1)
        far = jnp.concatenate([viscosity_ref[pl.ds(points + at, TILE), :]] * packs, axis=1)
        near = (near * (even + odd)).astype(jnp.bfloat16).astype(jnp.float32)
        far = (far * (even - odd)).astype(jnp.bfloat16).astype(jnp.float32)
        total_ref[0, 0, tile, :] = (near + far).astype(jnp.bfloat16)
        total_ref[0, 1, tile, :] = (near - far).astype(jnp.bfloat16)
        return carry

    lax.fori_loop(0, points // TILE, step, 0)
    for p, back_ref in enumerate((even_back_ref, odd_back_ref)):
        if late:
            lay_spectrum(
                norm, back_ref, early_depth, total_ref.at[0, p], out_ref, p * late, (p + 1) * late
            )


def early_spectrum_kernel(norm, total_ref, even_back_ref, odd_back_ref, out_ref):
    groups = out_ref.shape[2] // 2
    for p, back_ref in enumerate((even_back_ref, odd_back_ref)):
        lay_spectrum(
            norm, back_ref, 0, total_ref.at[0, p], out_ref, p * groups, (p + 1) * groups
        )


def whole(shape):
    return pl.BlockSpec(shape, lambda *_: (0,) * len(shape))


def params(flops, nbytes):
    return dict(
        compiler_params=pltpu.CompilerParams(vmem_limit_bytes=VMEM_LIMIT),
        cost_estimate=pl.CostEstimate(flops=flops, bytes_accessed=nbytes, transcendentals=0),
    )


def run_synth(first, spectra, place, order_lanes, geometry, chunks, base, groups):
    comps, slots, degrees = spectra.shape
    half_cycles = geometry.shape[1]
    blocks = 2 * half_cycles // LANES
    rows = 2 * ORD
    half = CHUNK * ORD // 2
    smem = pl.BlockSpec(memory_space=pltpu.SMEM)
    vmem = pl.BlockSpec(memory_space=pltpu.VMEM)
    return pl.pallas_call(
        functools.partial(synth_kernel, comps, groups, chunks, base),
        out_shape=(
            jax.ShapeDtypeStruct((blocks, comps, groups, rows, LANES), jnp.bfloat16),
            jax.ShapeDtypeStruct((groups * chunks, 2, half, half_cycles), jnp.bfloat16),
            jax.ShapeDtypeStruct((groups, ORD, degrees), jnp.float32),
        ),
        in_specs=[smem] + [vmem] * 4,
        out_specs=(vmem, pl.BlockSpec(memory_space=pl.ANY), vmem),
        scratch_shapes=[
            pltpu.VMEM((2, degrees, LANES), jnp.float32),
            pltpu.VMEM((comps, groups * rows, degrees), jnp.bfloat16),
            pltpu.VMEM((comps * rows, half_cycles), jnp.float32),
            pltpu.VMEM((comps * rows, half_cycles), jnp.float32),
            pltpu.VMEM((ORD, half_cycles), jnp.float32),
            pltpu.VMEM((ORD, half_cycles), jnp.float32),
            pltpu.VMEM((ORD, half_cycles), jnp.float32),
            pltpu.VMEM((groups, degrees // BLOCK, ORD, LANES), jnp.float32),
            pltpu.VMEM((comps * rows, CHUNK * ORD), jnp.bfloat16),
            pltpu.VMEM((SLOTS // 2, 2, half, half_cycles), jnp.bfloat16),
            pltpu.VMEM((SLOTS // 2, 2, half, half_cycles), jnp.bfloat16),
            pltpu.SemaphoreType.DMA((SLOTS, 2)),
        ],
        name="synthesis",
        **params(groups * chunks * 2 * comps * rows * 2 * half * half_cycles, 40 << 20),
    )(first, spectra, place, order_lanes, geometry)


def run_analysis(first, radial_weight, gridded, table, kappa, gather, weights, shells, base):
    blocks, comps, groups, rows, _ = gridded.shape
    half_cycles = weights.shape[1]
    half = CHUNK * ORD // 2
    degrees = kappa.shape[2]
    chunks = degrees // CHUNK
    width = -(-comps * rows // LANES) * LANES
    smem = pl.BlockSpec(memory_space=pltpu.SMEM)
    vmem = pl.BlockSpec(memory_space=pltpu.VMEM)
    return pl.pallas_call(
        functools.partial(analysis_kernel, comps, groups, chunks, base),
        out_shape=(
            jax.ShapeDtypeStruct((comps, groups * rows, degrees), jnp.bfloat16),
            jax.ShapeDtypeStruct((shells, comps, groups * rows, degrees // shells), jnp.bfloat16),
        ),
        in_specs=[smem, smem, vmem, pl.BlockSpec(memory_space=pl.ANY)] + [vmem] * 3,
        out_specs=(vmem, vmem),
        scratch_shapes=[
            pltpu.VMEM((2, half_cycles, width), jnp.bfloat16),
            pltpu.VMEM((2 * half, width), jnp.bfloat16),
            pltpu.VMEM((degrees + CHUNK, width), jnp.bfloat16),
            pltpu.VMEM((SLOTS, 2, half, half_cycles), jnp.bfloat16),
            pltpu.SemaphoreType.DMA((SLOTS, 2)),
        ],
        name="analysis",
        **params(groups * chunks * 2 * comps * rows * 2 * half * half_cycles, 40 << 20),
    )(first, radial_weight, gridded, table, kappa, gather, weights)


def run_grid(received, forward, backward, viscosity, norm):
    blocks, comps, early_groups, rows, lanes = received[0].shape
    late_groups = received[1].shape[2] if len(received) > 1 else 0
    packs = 2 if comps % 2 == 0 else 1
    steps = comps // packs
    _, half_points, depth = forward.shape
    width = packs * lanes
    early_depth = blocks * early_groups // 2 * rows

    def part(groups):
        return pl.BlockSpec((blocks, packs, groups, rows, lanes), lambda i: (0, i, 0, 0, 0))

    def wave(p, shape):
        return pl.BlockSpec((None,) + shape, lambda i: (p, 0, 0))

    fields = pl.BlockSpec((1, 2, half_points, width), lambda i: (i, 0, 0, 0))
    fields_shape = (steps, 2, half_points, width)
    forward_specs = [wave(p, (half_points, depth)) for p in range(2)]
    backward_specs = [wave(p, (depth, half_points)) for p in range(2)]
    one_product = 2 * steps * width * depth * half_points
    early_field = pl.pallas_call(
        early_field_kernel,
        out_shape=jax.ShapeDtypeStruct(fields_shape, jnp.float32),
        grid=(steps,),
        in_specs=[part(early_groups)] + forward_specs,
        out_specs=fields,
        scratch_shapes=[pltpu.VMEM((2, early_depth, width), jnp.bfloat16)],
        name="early_field",
        **params(one_product, 8 << 20),
    )(received[0], forward, forward)
    total_type = jax.ShapeDtypeStruct(fields_shape, jnp.bfloat16)
    late_type = [jax.ShapeDtypeStruct(piece.shape, jnp.bfloat16) for piece in received[1:]]
    late_scratch = pltpu.VMEM((2, depth - early_depth, width), jnp.bfloat16)
    total, *late = pl.pallas_call(
        functools.partial(stress_kernel, norm, packs, late_groups // 2, early_depth),
        out_shape=[total_type] + late_type,
        grid=(steps,),
        in_specs=[part(late_groups)] * len(late_type)
        + [fields]
        + forward_specs
        + backward_specs
        + [whole(viscosity.shape)],
        out_specs=[fields] + [part(late_groups)] * len(late_type),
        scratch_shapes=[late_scratch] * len(late_type),
        name="stress",
        **params(2 * one_product, 16 << 20),
    )(*received[1:], early_field, forward, forward, backward, backward, viscosity)
    early = pl.pallas_call(
        functools.partial(early_spectrum_kernel, norm),
        out_shape=jax.ShapeDtypeStruct(received[0].shape, jnp.bfloat16),
        grid=(steps,),
        in_specs=[fields] + backward_specs,
        out_specs=part(early_groups),
        name="early_spectrum",
        **params(one_product, 6 << 20),
    )(total, backward, backward)
    return [early] + late


def run_place(kernel, place, pieces, out_shape):
    vmem = pl.BlockSpec(memory_space=pltpu.VMEM)
    return pl.pallas_call(
        kernel,
        out_shape=out_shape,
        in_specs=[vmem] * (1 + len(pieces)),
        out_specs=vmem,
        name="natural_order",
        **params(2 * place.shape[1] * math.prod(out_shape.shape), 8 << 20),
    )(place, *pieces)


def wave_tables(sorted_all, point_count, groups):
    half_points = point_count // 2
    late = late_share(groups)
    early = groups // 2 - late
    by_group = sorted_all.reshape(sorted_all.shape[0], groups, ORD)
    orders = []
    for p in range(2):
        begin = 2 * late + p * early
        first = by_group[:, begin : begin + early].reshape(-1, ORD)
        second = by_group[:, p * late : (p + 1) * late].reshape(-1, ORD)
        orders.append(jnp.concatenate([first, second], axis=0))
    orders = jnp.stack(orders)
    shape = (2, orders.shape[1], 2, ORD)
    depth = math.prod(shape[1:])
    shift = jnp.arange(2, dtype=jnp.int32)[:, None] * (point_count // 4)
    lane_orders = jnp.broadcast_to(orders[:, :, None], shape).reshape(2, 1, depth)
    lane_shift = jnp.broadcast_to(shift, shape).reshape(2, 1, depth)

    def angle(phase):
        return (phase % point_count).astype(jnp.float32) * (2.0 * math.pi / point_count)

    def both(phase):
        return jnp.stack([jnp.cos(angle(phase)), jnp.sin(angle(phase))])

    rows = jnp.arange(ORD, dtype=jnp.int32)[None, :, None]
    forward_base = both(lane_orders * rows + lane_shift)
    forward_turn = both(lane_orders * ORD)
    row_orders = orders.reshape(2, depth // (2 * ORD), ORD, 1)
    longitudes = jnp.arange(LANES, dtype=jnp.int32)
    angles = angle(row_orders * longitudes)
    backward_base = jnp.stack([jnp.cos(angles), -jnp.sin(angles)])
    turn_shape = (2, 2, depth // (2 * ORD), ORD, LANES)
    backward_turn = jnp.broadcast_to(both(row_orders * LANES), turn_shape)
    vmem = pl.BlockSpec(memory_space=pltpu.VMEM)
    return pl.pallas_call(
        wave_kernel,
        out_shape=(
            jax.ShapeDtypeStruct((2, half_points, depth), jnp.bfloat16),
            jax.ShapeDtypeStruct((2, depth, half_points), jnp.bfloat16),
        ),
        in_specs=[vmem] * 4,
        out_specs=(vmem, vmem),
        name="waves",
        **params(8 * depth * half_points, 12 << 20),
    )(forward_base, forward_turn, backward_base, backward_turn)


def to_blocks(gridded, cycle_local):
    blocks, comps, groups, rows, _ = gridded.shape
    share = LANES // cycle_local
    if share == 1:
        return gridded
    cut = gridded.reshape(2, blocks // 2, comps, groups, rows, share, cycle_local)
    cut = cut.transpose(0, 1, 5, 2, 3, 4, 6)
    cut = jnp.stack([cut[0], jnp.flip(cut[1], axis=1)])
    return cut.reshape(blocks * share, comps, groups, rows, cycle_local)


def from_blocks(gridded, cycle_local):
    blocks, comps, groups, rows, _ = gridded.shape
    share = LANES // cycle_local
    if share == 1:
        return gridded
    cut = gridded.reshape(2, blocks // share // 2, share, comps, groups, rows, cycle_local)
    cut = jnp.stack([cut[0], jnp.flip(cut[1], axis=1)])
    cut = cut.transpose(0, 1, 3, 4, 5, 2, 6)
    return cut.reshape(blocks // share, comps, groups, rows, LANES)


def pack_comps(gridded):
    blocks, comps, groups, rows, cycle_local = gridded.shape
    if cycle_local == LANES:
        return gridded
    side = gridded.transpose(0, 2, 3, 1, 4).reshape(blocks, 1, groups, rows, comps * cycle_local)
    extra = -(comps * cycle_local) % LANES
    return jnp.pad(side, ((0, 0),) * 4 + ((0, extra),))


def unpack_comps(gridded, comps, cycle_local):
    if cycle_local == LANES:
        return gridded
    blocks, _, groups, rows, _ = gridded.shape
    side = gridded[..., : comps * cycle_local]
    side = side.reshape(blocks, groups, rows, comps, cycle_local)
    return side.transpose(0, 3, 1, 2, 4)


def shards(strain_spec, order_map, viscosity, radial_weight):
    comps, shells, slots, parts, degrees = strain_spec.shape
    block_count = lax.axis_size("blk")
    block = lax.axis_index("blk")
    cycle_local = viscosity.shape[1]
    cycle_count = cycle_local * block_count
    half_cycles = cycle_count // 2
    points = viscosity.shape[2]
    groups = slots // ORD
    chunks = degrees // CHUNK

    rank_all = rank_orders(order_map.reshape(block_count, slots))
    sorted_all = apply_rank(order_map.reshape(block_count, slots), rank_all)
    rank = lax.dynamic_index_in_dim(rank_all, block, 0, keepdims=False)
    sorted_orders = lax.dynamic_index_in_dim(sorted_all, block, 0, keepdims=False)
    by_group = sorted_orders.reshape(groups, ORD)
    first = jnp.concatenate([by_group[:, 0], by_group[:, -1]]) // CHUNK
    order = sorted_orders.astype(jnp.float32)
    counter = jnp.arange(1, degrees, dtype=jnp.float32)
    logs = jnp.where(counter <= order[:, None], jnp.log(1.0 - 0.5 / counter), 0.0)
    starts = 0.5 * jnp.log((2.0 * order + 1.0) / (4.0 * math.pi)) + 0.5 * jnp.sum(logs, axis=1)
    order_lanes = jnp.broadcast_to(
        jnp.stack([order, starts]).reshape(2, groups, ORD, 1), (2, groups, ORD, LANES)
    )

    cycle_index = jnp.arange(half_cycles, dtype=jnp.float32)
    colatitude = math.pi * (2.0 * cycle_index + 1.0) / (2.0 * cycle_count)
    geometry = jnp.stack([2.0 * jnp.cos(colatitude), jnp.log(jnp.sin(colatitude))])

    row_rank = rank // ORD * (2 * ORD) + rank % ORD
    row_rank = (row_rank[:, None] + ORD * jnp.arange(2, dtype=jnp.int32)).reshape(-1)
    place = jnp.arange(slots * 2, dtype=jnp.int32)
    hit = row_rank[None, :] == place[:, None]
    my_orders = lax.dynamic_index_in_dim(
        order_map.reshape(block_count, slots), block, 0, keepdims=False
    )
    doubling = jnp.repeat(jnp.where(my_orders == 0, 1.0, 2.0), 2)
    place_in = jnp.where(hit, doubling[None, :], 0.0).astype(jnp.bfloat16)
    place_out = hit.T.astype(jnp.bfloat16)

    spectra = strain_spec.reshape(comps, slots * parts, degrees)
    late = late_share(groups)
    spans = [(2 * late, groups - 2 * late)] + ([(0, 2 * late)] if late else [])
    received, tables = [], []
    for base, count in spans:
        gridded, table, kappa = run_synth(
            first, spectra, place_in, order_lanes, geometry, chunks, base, count
        )
        tables.append((table, kappa))
        arrived = lax.all_to_all(to_blocks(gridded, cycle_local), "blk", 0, 0, tiled=True)
        received.append(pack_comps(arrived))

    forward, backward = wave_tables(sorted_all, points, groups)
    weights = fejer_weights(cycle_count)[None, :]
    gather = gather_matrix()
    forward, weights, gather = lax.optimization_barrier((forward, weights, gather))
    mirror = jnp.arange(cycle_local, dtype=jnp.int32)
    mirror = jnp.where(block * 2 < block_count, mirror, cycle_local - 1 - mirror)
    turn = (mirror[None, :] == jnp.arange(cycle_local, dtype=jnp.int32)[:, None]).astype(jnp.float32)
    local = jnp.einsum("jk,ji->ki", viscosity[0], turn, precision=lax.Precision.HIGHEST)
    if cycle_local < LANES:
        local = jnp.concatenate([local] * comps, axis=1)
        local = jnp.pad(local, ((0, 0), (0, -local.shape[1] % LANES)))
    spectrum = run_grid(received, forward, backward, local, 2.0 * math.pi / points)
    returned = [
        lax.all_to_all(unpack_comps(piece, comps, cycle_local), "blk", 0, 0, tiled=True)
        for piece in spectrum
    ]

    shell_count = lax.axis_size("shell")
    ordered, offsets, integrated = [], [], []
    sum_type = jax.ShapeDtypeStruct((comps, slots * parts, degrees // shell_count), jnp.float32)
    for i in reversed(range(len(spans))):
        base = spans[i][0]
        table, kappa = tables[i]
        coefs, weighted = run_analysis(
            first,
            radial_weight,
            from_blocks(returned[i], cycle_local),
            table,
            kappa,
            gather,
            weights,
            shell_count,
            base,
        )
        ordered.append(coefs)
        offsets.append(base * 2 * ORD)
        shared = lax.all_to_all(weighted, "shell", 0, 0, tiled=True)
        kernel = functools.partial(shell_sum_kernel, offsets[-1])
        integrated = [run_place(kernel, place_out, [shared] + integrated, sum_type)]
    stress = run_place(
        functools.partial(unsort_kernel, offsets),
        place_out,
        ordered,
        jax.ShapeDtypeStruct((comps, slots * parts, degrees), jnp.bfloat16),
    )
    integrated = integrated[0]
    stress_spec = stress.reshape(strain_spec.shape)
    return (stress_spec, integrated.reshape(comps, slots, parts, degrees // shell_count))


def solution(mesh):
    return jax.shard_map(
        shards,
        mesh=mesh,
        in_specs=(P(None, "shell", "blk", None, None), P(), P("shell", "blk", None), P("shell")),
        out_specs=(P(None, "shell", "blk", None, None), P(None, "blk", None, "shell")),
        check_vma=False,
    )
```

```python
import functools
import math

import jax
import jax.numpy as jnp
from jax import lax
from jax.experimental import pallas as pl
from jax.experimental.pallas import tpu as pltpu
from jax.sharding import PartitionSpec as P

two_power = 1099511627776.0
inverse_power = 1.0 / 1099511627776.0
log_jump = 40.0 * math.log(2.0)

ORD = 8
CHUNK = 128
BLOCK = 16
LANES = 128
TILE = 512
SLOTS = 4
VMEM_LIMIT = 63 * 1024 * 1024


def fejer_weights(cycle_count):
    half_count = cycle_count // 2
    cycle_index = jnp.arange(half_count, dtype=jnp.int32)
    wave_number = jnp.arange(1, half_count + 1, dtype=jnp.int32)
    phase_index = wave_number[:, None] * (2 * cycle_index[None, :] + 1) % (2 * cycle_count)
    angles = phase_index.astype(jnp.float32) * (math.pi / cycle_count)
    wave_float = wave_number.astype(jnp.float32)
    divisor = 4.0 * wave_float * wave_float - 1.0
    series = jnp.sum(jnp.cos(angles) / divisor[:, None], axis=0)
    return 2.0 / cycle_count * (1.0 - 2.0 * series)


def late_share(groups):
    return groups // 4


def rank_orders(orders):
    groups = orders.shape[-1] // ORD
    half, late = groups // 2, late_share(groups)
    key = orders + (orders % 2) * (1 << 20)
    rank = jnp.sum((key[..., None, :] < key[..., :, None]).astype(jnp.int32), axis=-1)
    parity = (rank >= half * ORD).astype(jnp.int32)
    group = rank // ORD - parity * half
    early = 2 * late + parity * (half - late) + group - late
    return jnp.where(group < late, parity * late + group, early) * ORD + rank % ORD


def apply_rank(values, rank):
    count = rank.shape[-1]
    place = jnp.arange(count, dtype=jnp.int32)
    hit = rank[..., :, None] == place
    return jnp.sum(jnp.where(hit, values[..., :, None], 0), axis=-2)


def gather_matrix():
    place = jnp.arange(CHUNK * ORD, dtype=jnp.int32)
    parity = place // (CHUNK * ORD // 2)
    degree = 2 * (place % (CHUNK * ORD // 2) // ORD) + parity
    row = jnp.arange(CHUNK, dtype=jnp.int32)
    return (row[:, None] == degree[None, :]).astype(jnp.bfloat16)


def fill_degrees(degree_ref):
    row = lax.broadcasted_iota(jnp.int32, degree_ref.shape[1:], 0)
    below = row.astype(jnp.float32) - 1.0
    square = 4.0 * below * below
    degree_ref[0] = square / (square - 1.0)
    degree_ref[1] = 4.0 / (square - 1.0)


def kappa_lanes(order):
    lane = lax.broadcasted_iota(jnp.int32, order.shape, 1)
    degree = lane.astype(jnp.float32)
    square = degree * degree
    gap = jnp.maximum(square - order * order, 1.0)
    kappa = jnp.where(degree > order, jnp.sqrt((square - 0.25) / gap), 1.0)
    step = 1
    while step < BLOCK:
        moved = pltpu.roll(kappa, step, 1)
        kappa = kappa * jnp.where(lane % BLOCK >= step, moved, 1.0)
        step *= 2
    return kappa


def synth_kernel(
    comps,
    groups,
    chunks,
    base,
    first_ref,
    spec_ref,
    place_ref,
    lanes_ref,
    geometry_ref,
    out_ref,
    table_ref,
    kappa_ref,
    degree_ref,
    sorted_ref,
    even_ref,
    odd_ref,
    prev_ref,
    last_row_ref,
    log_ref,
    end_ref,
    wide_ref,
    buffer_ref,
    second_ref,
    sems,
):
    rows = 2 * ORD
    half = CHUNK * ORD // 2
    lane_blocks = geometry_ref.shape[1] // LANES
    own = place_ref[base * rows : (base + groups) * rows, :]
    fill_degrees(degree_ref)
    for c in range(comps):
        moved = jnp.dot(own, spec_ref[c], preferred_element_type=jnp.float32)
        sorted_ref[c] = moved.astype(jnp.bfloat16)
    degrees = chunks * CHUNK
    batch = next(n for n in (4, 3, 2, 1) if groups % n == 0)

    def fill_kappa(i, carry):
        order = lanes_ref[0, pl.ds(base + i * batch, batch)].reshape(batch * ORD, LANES)
        kappa = kappa_lanes(jnp.concatenate([order] * (degrees // LANES), axis=1))
        kappa = kappa.reshape(batch, ORD, degrees)
        kappa_ref[pl.ds(i * batch, batch)] = kappa
        for b in range(degrees // BLOCK):
            end = kappa[:, :, (b + 1) * BLOCK - 1 : (b + 1) * BLOCK]
            end_ref[pl.ds(i * batch, batch), b] = jnp.broadcast_to(end, (batch, ORD, LANES))
        return carry

    lax.fori_loop(0, groups // batch, fill_kappa, 0)
    shape = (rows, CHUNK * ORD)
    row_order = lax.broadcasted_iota(jnp.int32, shape, 0) % ORD
    lane_order = lax.broadcasted_iota(jnp.int32, shape, 1) % ORD
    mask = jnp.where(row_order == lane_order, 1.0, 0.0)
    count = lax.fori_loop(0, groups, lambda g, n: n + chunks - first_ref[base + g], jnp.int32(0))
    even_ref[...] = jnp.zeros_like(even_ref)
    odd_ref[...] = jnp.zeros_like(odd_ref)
    wide_ref[...] = jnp.zeros_like(wide_ref)
    second_ref[SLOTS // 2 - 1] = jnp.zeros_like(second_ref[SLOTS // 2 - 1])

    def table_copies(item, slot, which):
        offset = 0 if which is buffer_ref else SLOTS // 2
        return [
            pltpu.make_async_copy(
                which.at[slot, p], table_ref.at[item, p], sems.at[slot + offset, p]
            )
            for p in range(2)
        ]

    def products(other, before):
        even_ref[...] += jnp.dot(
            wide_ref[:, :half], other[before, 0], preferred_element_type=jnp.float32
        )
        odd_ref[...] += jnp.dot(
            wide_ref[:, half:], other[before, 1], preferred_element_type=jnp.float32
        )

    def recursion(seeded, group, chunk, slot, mine):
        order = lanes_ref[0, base + group]
        begin = chunk * CHUNK
        odd_chunk = lax.rem(chunk, LANES // CHUNK)
        lane = pl.multiple_of((chunk - odd_chunk) * CHUNK, LANES)
        kappa = kappa_ref[group, :, pl.ds(lane, LANES)]
        square = order * order
        seed_at = jnp.concatenate([order - begin.astype(jnp.float32)] * lane_blocks, axis=1)
        twice = geometry_ref[0:1, :]
        prev = prev_ref[...]
        last = last_row_ref[...]
        logs = log_ref[...]
        for b in range(CHUNK // BLOCK):
            scale = jnp.exp(logs)
            held = []
            for i in range(BLOCK):
                step = b * BLOCK + i
                one = degree_ref[0, pl.ds(begin + step, 1), :]
                two = degree_ref[1, pl.ds(begin + step, 1), :]
                coef = jnp.concatenate([one - two * square] * lane_blocks, axis=1)
                now = twice * last - coef * prev
                if seeded:
                    now = jnp.where(seed_at == float(step), 1.0, now)
                held.append(now * scale)
                prev, last = last, now
            for p in range(2):
                for i in range(p, BLOCK, 4):
                    pair = jnp.concatenate([held[i], held[i + 2]], axis=0).astype(jnp.bfloat16)
                    at = (b * BLOCK + i - p) // 2 * ORD
                    mine[slot, p, at : at + 2 * ORD, :] = pair
            end = end_ref[group, chunk * (CHUNK // BLOCK) + b]
            end = jnp.concatenate([end] * lane_blocks, axis=1)
            last = last * end
            prev = prev * end
            large = jnp.abs(last) > two_power
            factor = jnp.where(large, inverse_power, 1.0)
            last = last * factor
            prev = prev * factor
            logs = logs + jnp.where(large, log_jump, 0.0)
        prev_ref[...] = prev
        last_row_ref[...] = last
        log_ref[...] = logs
        at = pl.multiple_of(group * rows, rows)
        factors = jnp.concatenate([kappa, kappa], axis=0)
        piece = jnp.concatenate(
            [
                (sorted_ref[c, pl.ds(at, rows), pl.ds(lane, LANES)] * factors).astype(jnp.bfloat16)
                for c in range(comps)
            ],
            axis=0,
        )
        lane_at = lax.broadcasted_iota(jnp.int32, (rows, LANES), 1)
        for c in range(comps):
            source = piece[c * rows : (c + 1) * rows].astype(jnp.float32)
            for q in range(CHUNK * ORD // LANES):
                p, t = q // (CHUNK * ORD // LANES // 2), q % (CHUNK * ORD // LANES // 2)
                index = 2 * (lane_at // ORD + t * (LANES // ORD)) + p + odd_chunk * CHUNK
                moved = jnp.take_along_axis(source, index, axis=1)
                lanes = slice(q * LANES, (q + 1) * LANES)
                wide_ref[c * rows : (c + 1) * rows, lanes] = (moved * mask[:, lanes]).astype(jnp.bfloat16)

    def finish(group):
        sign = jnp.where(group < groups // 2, 1.0, -1.0)
        for c in range(comps):
            even = even_ref[c * rows : (c + 1) * rows, :]
            odd = odd_ref[c * rows : (c + 1) * rows, :]
            north = (even + odd).astype(jnp.bfloat16)
            south = (sign * (even - odd)).astype(jnp.bfloat16)
            for b in range(lane_blocks):
                lanes = slice(b * LANES, (b + 1) * LANES)
                out_ref[b, c, group] = north[:, lanes]
                out_ref[2 * lane_blocks - 1 - b, c, group] = south[:, lanes]
        even_ref[...] = jnp.zeros_like(even_ref)
        odd_ref[...] = jnp.zeros_like(odd_ref)

    def body(item, carry):
        before_group, before_chunk, group, chunk = carry
        for parity in range(2):

            @pl.when(jnp.logical_and(item >= SLOTS, lax.rem(item, 2) == parity))
            def _(parity=parity):
                which = second_ref if parity else buffer_ref
                for copy in table_copies(item - SLOTS, lax.rem(item // 2, SLOTS // 2), which):
                    copy.wait()

        @pl.when(chunk == first_ref[base + group])
        def _():
            prev_ref[...] = jnp.zeros_like(prev_ref)
            last_row_ref[...] = jnp.zeros_like(last_row_ref)
            wide_order = jnp.concatenate([lanes_ref[0, base + group]] * lane_blocks, axis=1)
            wide_start = jnp.concatenate([lanes_ref[1, base + group]] * lane_blocks, axis=1)
            log_ref[...] = wide_start + wide_order * geometry_ref[1:2, :]

        seeded = chunk <= first_ref[first_ref.shape[0] // 2 + base + group]
        for parity in range(2):
            mine, other = (buffer_ref, second_ref) if parity == 0 else (second_ref, buffer_ref)
            place = lax.rem(item // 2, SLOTS // 2)
            before = lax.rem((item + SLOTS - 1) // 2, SLOTS // 2)
            turn = lax.rem(item, 2) == parity
            for want in (True, False):

                @pl.when(jnp.logical_and(turn, seeded if want else jnp.logical_not(seeded)))
                def _(mine=mine, other=other, want=want):
                    products(other, before)
                    recursion(want, group, chunk, place, mine)
                    for copy in table_copies(item, place, mine):
                        copy.start()

        @pl.when(jnp.logical_and(before_chunk == chunks - 1, item > 0))
        def _():
            finish(before_group)

        done = chunk == chunks - 1
        next_group = jnp.minimum(group + done.astype(jnp.int32), groups - 1)
        next_chunk = jnp.where(done, first_ref[base + next_group], chunk + 1)
        return group, chunk, next_group, next_chunk

    zero = jnp.int32(0)
    lax.fori_loop(0, count, body, (zero, zero, zero, first_ref[base]))
    for parity in range(2):
        which = second_ref if parity else buffer_ref

        @pl.when(lax.rem(count - 1, 2) == parity)
        def _(which=which):
            products(which, lax.rem((count - 1) // 2, SLOTS // 2))

        for back in range(SLOTS, 0, -1):
            item = count - back

            @pl.when(jnp.logical_and(item >= 0, lax.rem(item + SLOTS, 2) == parity))
            def _(item=item, which=which):
                for copy in table_copies(item, lax.rem(item // 2, SLOTS // 2), which):
                    copy.wait()

    finish(jnp.int32(groups - 1))


def analysis_kernel(
    comps,
    groups,
    chunks,
    base,
    first_ref,
    radial_ref,
    grid_ref,
    table_ref,
    kappa_ref,
    gather_ref,
    weight_ref,
    sorted_ref,
    shared_ref,
    side_ref,
    wide_ref,
    found_ref,
    buffer_ref,
    sems,
):
    rows = 2 * ORD
    half = CHUNK * ORD // 2
    half_cycles = weight_ref.shape[1]
    degrees = chunks * CHUNK
    lane_blocks = half_cycles // LANES
    width = found_ref.shape[1]
    count = lax.fori_loop(0, groups, lambda g, n: n + chunks - first_ref[base + g], jnp.int32(0))
    shape = (ORD, width)
    lane = lax.broadcasted_iota(jnp.int32, shape, 1)
    own = lax.broadcasted_iota(jnp.int32, shape, 0) == lane % ORD
    mask = jnp.where(own, 1.0, 0.0)
    mask = jnp.concatenate([mask] * (half // ORD), axis=0)
    wide_ref[...] = jnp.zeros_like(wide_ref)
    radial = radial_ref[0]
    shells, share = shared_ref.shape[0], shared_ref.shape[3]

    def table_copies(item, slot):
        return [
            pltpu.make_async_copy(
                table_ref.at[item, p], buffer_ref.at[slot, p], sems.at[slot, p]
            )
            for p in range(2)
        ]

    for ahead in range(SLOTS - 1):

        @pl.when(ahead < count)
        def _():
            for copy in table_copies(ahead, ahead):
                copy.start()

    def narrow(chunk):
        found = jnp.dot(gather_ref[...], wide_ref[...], preferred_element_type=jnp.float32)
        found_ref[pl.ds(pl.multiple_of(chunk * CHUNK, CHUNK), CHUNK), :] = found.astype(
            jnp.bfloat16
        )

    def advance(group, chunk, carry):
        item, before = carry
        slot = lax.rem(item, SLOTS)
        ahead = item + SLOTS - 1

        @pl.when(ahead < count)
        def _():
            for copy in table_copies(ahead, lax.rem(ahead, SLOTS)):
                copy.start()

        for copy in table_copies(item, slot):
            copy.wait()
        narrow(before)
        for p in range(2):
            wide = jnp.dot(buffer_ref[slot, p], side_ref[p], preferred_element_type=jnp.float32)
            wide_ref[p * half : (p + 1) * half, :] = (wide * mask).astype(jnp.bfloat16)
        return item + 1, chunk

    def group_body(group, item):
        sign = jnp.where(group < groups // 2, 1.0, -1.0)
        for b in range(lane_blocks):
            lanes = slice(b * LANES, (b + 1) * LANES)
            weight = weight_ref[:, lanes]
            norths, souths = [], []
            for c in range(comps):
                norths.append(grid_ref[b, c, group].astype(jnp.float32))
                souths.append(sign * grid_ref[2 * lane_blocks - 1 - b, c, group].astype(jnp.float32))
            fill = jnp.zeros((width - comps * rows, LANES), jnp.float32)
            north = jnp.concatenate(norths + [fill], axis=0)
            south = jnp.concatenate(souths + [fill], axis=0)
            side_ref[0, lanes, :] = (weight * (north + south)).astype(jnp.bfloat16).T
            side_ref[1, lanes, :] = (weight * (north - south)).astype(jnp.bfloat16).T
        found_ref[...] = jnp.zeros_like(found_ref)
        item, before = lax.fori_loop(
            first_ref[base + group], chunks, functools.partial(advance, group), (item, jnp.int32(chunks))
        )
        narrow(before)
        turned = found_ref[:degrees].T.astype(jnp.float32)
        kappa = kappa_ref[group]
        at = pl.multiple_of(group * rows, rows)
        factors = jnp.concatenate([kappa, kappa], axis=0)
        for c in range(comps):
            piece = turned[c * rows : (c + 1) * rows] * factors
            sorted_ref[c, pl.ds(at, rows), :] = piece.astype(jnp.bfloat16)
            piece = (piece * radial).astype(jnp.bfloat16)
            for n in range(shells):
                shared_ref[n, c, pl.ds(at, rows), :] = piece[:, n * share : (n + 1) * share]
        return item

    lax.fori_loop(0, groups, group_body, jnp.int32(0))


def unsort_kernel(offsets, place_ref, *refs):
    out_ref = refs[-1]
    for c in range(out_ref.shape[0]):
        found = 0.0
        for offset, ref in zip(offsets, refs[:-1]):
            place = place_ref[:, offset : offset + ref.shape[1]]
            found += jnp.dot(place, ref[c], preferred_element_type=jnp.float32)
        out_ref[c] = found.astype(jnp.bfloat16)


def shell_sum_kernel(offset, place_ref, shared_ref, *refs):
    out_ref = refs[-1]
    place = place_ref[:, offset : offset + shared_ref.shape[2]]
    for c in range(out_ref.shape[0]):
        found = refs[0][c] if len(refs) > 1 else 0.0
        for n in range(shared_ref.shape[0]):
            found += jnp.dot(place, shared_ref[n, c], preferred_element_type=jnp.float32)
        out_ref[c] = found


def wave_kernel(forward_base, forward_turn, backward_base, backward_turn, forward_ref, backward_ref):
    points = forward_ref.shape[1]
    step = 512
    per = forward_ref.shape[2] // step

    def forward_lanes(i, carry):
        p, block = i // per, i % per
        at = pl.multiple_of(block * step, step)
        turn_cos = forward_turn[0, p, :, pl.ds(at, step)]
        turn_sin = forward_turn[1, p, :, pl.ds(at, step)]

        def turn(n, state):
            cos, sin = state
            later_cos = cos * turn_cos - sin * turn_sin
            later_sin = sin * turn_cos + cos * turn_sin
            rows = pl.ds(pl.multiple_of(n * 2 * ORD, 2 * ORD), 2 * ORD)
            forward_ref[p, rows, pl.ds(at, step)] = jnp.concatenate(
                [cos, later_cos], axis=0
            ).astype(jnp.bfloat16)
            cos = later_cos * turn_cos - later_sin * turn_sin
            sin = later_sin * turn_cos + later_cos * turn_sin
            return cos, sin

        state = (forward_base[0, p, :, pl.ds(at, step)], forward_base[1, p, :, pl.ds(at, step)])
        lax.fori_loop(0, points // (2 * ORD), turn, state)
        return carry

    lax.fori_loop(0, 2 * per, forward_lanes, 0)
    count = backward_base.shape[2]

    def backward_rows(i, carry):
        p, q = i // count, i % count
        real, imaginary = backward_base[0, p, q], backward_base[1, p, q]
        turn_cos, turn_sin = backward_turn[0, p, q], backward_turn[1, p, q]
        rows = pl.ds(pl.multiple_of(q * 2 * ORD, 2 * ORD), 2 * ORD)
        for a in range(points // LANES):
            backward_ref[p, rows, a * LANES : (a + 1) * LANES] = jnp.concatenate(
                [real, imaginary], axis=0
            ).astype(jnp.bfloat16)
            real, imaginary = (
                real * turn_cos + imaginary * turn_sin,
                imaginary * turn_cos - real * turn_sin,
            )
        return carry

    lax.fori_loop(0, 2 * count, backward_rows, 0)


def lay_field(grid_ref, field_ref, begin, end):
    blocks, packs, _, rows, lanes = grid_ref.shape
    count = (end - begin) * rows
    for w in range(packs):
        for d in range(blocks):
            field_ref[d * count : (d + 1) * count, w * lanes : (w + 1) * lanes] = grid_ref[
                d, w, begin:end
            ].reshape(count, lanes)


def early_field_kernel(grid_ref, even_wave_ref, odd_wave_ref, out_ref, field_ref):
    groups = grid_ref.shape[2] // 2
    depth = field_ref.shape[1]
    for p in range(2):
        lay_field(grid_ref, field_ref.at[p], p * groups, (p + 1) * groups)

    def step(i, carry):
        tile = pl.ds(pl.multiple_of(i * TILE, TILE), TILE)
        for p, wave_ref in enumerate((even_wave_ref, odd_wave_ref)):
            out_ref[0, p, tile, :] = jnp.dot(
                wave_ref[tile, :depth], field_ref[p], preferred_element_type=jnp.float32
            )
        return carry

    lax.fori_loop(0, out_ref.shape[2] // TILE, step, 0)


def lay_spectrum(norm, wave_ref, offset, stress, out_ref, begin, end):
    blocks, packs, _, rows, lanes = out_ref.shape
    count = (end - begin) * rows
    batch = math.gcd(blocks, max(1, TILE // count))

    def step(i, carry):
        at = pl.multiple_of(offset + i * (batch * count), 2 * ORD)
        found = jnp.dot(
            wave_ref[pl.ds(at, batch * count), :], stress[...], preferred_element_type=jnp.float32
        )
        found = (found * norm).astype(jnp.bfloat16)
        for n in range(batch):
            piece = found[n * count : (n + 1) * count]
            for w in range(packs):
                out_ref[i * batch + n, w, begin:end] = piece[
                    :, w * lanes : (w + 1) * lanes
                ].reshape(end - begin, rows, lanes)
        return carry

    lax.fori_loop(0, blocks // batch, step, 0)


def stress_kernel(norm, packs, late, early_depth, *refs):
    refs = list(refs)
    grid_ref = refs.pop(0) if late else None
    early_ref, even_wave_ref, odd_wave_ref, even_back_ref, odd_back_ref, viscosity_ref = refs[:6]
    total_ref = refs[6]
    out_ref, field_ref = refs[7:] if late else (None, None)
    points = even_wave_ref.shape[0]
    for p in range(2):
        if late:
            lay_field(grid_ref, field_ref.at[p], p * late, (p + 1) * late)

    def step(i, carry):
        at = pl.multiple_of(i * TILE, TILE)
        tile = pl.ds(at, TILE)
        fields = []
        for p, wave_ref in enumerate((even_wave_ref, odd_wave_ref)):
            field = early_ref[0, p, tile, :]
            if late:
                field += jnp.dot(
                    wave_ref[tile, early_depth:], field_ref[p], preferred_element_type=jnp.float32
                )
            fields.append(field)
        even, odd = fields
        near = jnp.concatenate([viscosity_ref[tile, :]] * packs, axis=1)
        far = jnp.concatenate([viscosity_ref[pl.ds(points + at, TILE), :]] * packs, axis=1)
        near = (near * (even + odd)).astype(jnp.bfloat16).astype(jnp.float32)
        far = (far * (even - odd)).astype(jnp.bfloat16).astype(jnp.float32)
        total_ref[0, 0, tile, :] = (near + far).astype(jnp.bfloat16)
        total_ref[0, 1, tile, :] = (near - far).astype(jnp.bfloat16)
        return carry

    lax.fori_loop(0, points // TILE, step, 0)
    for p, back_ref in enumerate((even_back_ref, odd_back_ref)):
        if late:
            lay_spectrum(
                norm, back_ref, early_depth, total_ref.at[0, p], out_ref, p * late, (p + 1) * late
            )


def early_spectrum_kernel(norm, total_ref, even_back_ref, odd_back_ref, out_ref):
    groups = out_ref.shape[2] // 2
    for p, back_ref in enumerate((even_back_ref, odd_back_ref)):
        lay_spectrum(
            norm, back_ref, 0, total_ref.at[0, p], out_ref, p * groups, (p + 1) * groups
        )


def whole(shape):
    return pl.BlockSpec(shape, lambda *_: (0,) * len(shape))


def params(flops, nbytes):
    return dict(
        compiler_params=pltpu.CompilerParams(vmem_limit_bytes=VMEM_LIMIT),
        cost_estimate=pl.CostEstimate(flops=flops, bytes_accessed=nbytes, transcendentals=0),
    )


def run_synth(first, spectra, place, order_lanes, geometry, chunks, base, groups):
    comps, slots, degrees = spectra.shape
    half_cycles = geometry.shape[1]
    blocks = 2 * half_cycles // LANES
    rows = 2 * ORD
    half = CHUNK * ORD // 2
    smem = pl.BlockSpec(memory_space=pltpu.SMEM)
    vmem = pl.BlockSpec(memory_space=pltpu.VMEM)
    return pl.pallas_call(
        functools.partial(synth_kernel, comps, groups, chunks, base),
        out_shape=(
            jax.ShapeDtypeStruct((blocks, comps, groups, rows, LANES), jnp.bfloat16),
            jax.ShapeDtypeStruct((groups * chunks, 2, half, half_cycles), jnp.bfloat16),
            jax.ShapeDtypeStruct((groups, ORD, degrees), jnp.float32),
        ),
        in_specs=[smem] + [vmem] * 4,
        out_specs=(vmem, pl.BlockSpec(memory_space=pl.ANY), vmem),
        scratch_shapes=[
            pltpu.VMEM((2, degrees, LANES), jnp.float32),
            pltpu.VMEM((comps, groups * rows, degrees), jnp.bfloat16),
            pltpu.VMEM((comps * rows, half_cycles), jnp.float32),
            pltpu.VMEM((comps * rows, half_cycles), jnp.float32),
            pltpu.VMEM((ORD, half_cycles), jnp.float32),
            pltpu.VMEM((ORD, half_cycles), jnp.float32),
            pltpu.VMEM((ORD, half_cycles), jnp.float32),
            pltpu.VMEM((groups, degrees // BLOCK, ORD, LANES), jnp.float32),
            pltpu.VMEM((comps * rows, CHUNK * ORD), jnp.bfloat16),
            pltpu.VMEM((SLOTS // 2, 2, half, half_cycles), jnp.bfloat16),
            pltpu.VMEM((SLOTS // 2, 2, half, half_cycles), jnp.bfloat16),
            pltpu.SemaphoreType.DMA((SLOTS, 2)),
        ],
        name="synthesis",
        **params(groups * chunks * 2 * comps * rows * 2 * half * half_cycles, 40 << 20),
    )(first, spectra, place, order_lanes, geometry)


def run_analysis(first, radial_weight, gridded, table, kappa, gather, weights, shells, base):
    blocks, comps, groups, rows, _ = gridded.shape
    half_cycles = weights.shape[1]
    half = CHUNK * ORD // 2
    degrees = kappa.shape[2]
    chunks = degrees // CHUNK
    width = -(-comps * rows // LANES) * LANES
    smem = pl.BlockSpec(memory_space=pltpu.SMEM)
    vmem = pl.BlockSpec(memory_space=pltpu.VMEM)
    return pl.pallas_call(
        functools.partial(analysis_kernel, comps, groups, chunks, base),
        out_shape=(
            jax.ShapeDtypeStruct((comps, groups * rows, degrees), jnp.bfloat16),
            jax.ShapeDtypeStruct((shells, comps, groups * rows, degrees // shells), jnp.bfloat16),
        ),
        in_specs=[smem, smem, vmem, pl.BlockSpec(memory_space=pl.ANY)] + [vmem] * 3,
        out_specs=(vmem, vmem),
        scratch_shapes=[
            pltpu.VMEM((2, half_cycles, width), jnp.bfloat16),
            pltpu.VMEM((2 * half, width), jnp.bfloat16),
            pltpu.VMEM((degrees + CHUNK, width), jnp.bfloat16),
            pltpu.VMEM((SLOTS, 2, half, half_cycles), jnp.bfloat16),
            pltpu.SemaphoreType.DMA((SLOTS, 2)),
        ],
        name="analysis",
        **params(groups * chunks * 2 * comps * rows * 2 * half * half_cycles, 40 << 20),
    )(first, radial_weight, gridded, table, kappa, gather, weights)


def run_grid(received, forward, backward, viscosity, norm):
    blocks, comps, early_groups, rows, lanes = received[0].shape
    late_groups = received[1].shape[2] if len(received) > 1 else 0
    packs = 2 if comps % 2 == 0 else 1
    steps = comps // packs
    _, half_points, depth = forward.shape
    width = packs * lanes
    early_depth = blocks * early_groups // 2 * rows

    def part(groups):
        return pl.BlockSpec((blocks, packs, groups, rows, lanes), lambda i: (0, i, 0, 0, 0))

    def wave(p, shape):
        return pl.BlockSpec((None,) + shape, lambda i: (p, 0, 0))

    fields = pl.BlockSpec((1, 2, half_points, width), lambda i: (i, 0, 0, 0))
    fields_shape = (steps, 2, half_points, width)
    forward_specs = [wave(p, (half_points, depth)) for p in range(2)]
    backward_specs = [wave(p, (depth, half_points)) for p in range(2)]
    one_product = 2 * steps * width * depth * half_points
    early_field = pl.pallas_call(
        early_field_kernel,
        out_shape=jax.ShapeDtypeStruct(fields_shape, jnp.float32),
        grid=(steps,),
        in_specs=[part(early_groups)] + forward_specs,
        out_specs=fields,
        scratch_shapes=[pltpu.VMEM((2, early_depth, width), jnp.bfloat16)],
        name="early_field",
        **params(one_product, 8 << 20),
    )(received[0], forward, forward)
    total_type = jax.ShapeDtypeStruct(fields_shape, jnp.bfloat16)
    late_type = [jax.ShapeDtypeStruct(piece.shape, jnp.bfloat16) for piece in received[1:]]
    late_scratch = pltpu.VMEM((2, depth - early_depth, width), jnp.bfloat16)
    total, *late = pl.pallas_call(
        functools.partial(stress_kernel, norm, packs, late_groups // 2, early_depth),
        out_shape=[total_type] + late_type,
        grid=(steps,),
        in_specs=[part(late_groups)] * len(late_type)
        + [fields]
        + forward_specs
        + backward_specs
        + [whole(viscosity.shape)],
        out_specs=[fields] + [part(late_groups)] * len(late_type),
        scratch_shapes=[late_scratch] * len(late_type),
        name="stress",
        **params(2 * one_product, 16 << 20),
    )(*received[1:], early_field, forward, forward, backward, backward, viscosity)
    early = pl.pallas_call(
        functools.partial(early_spectrum_kernel, norm),
        out_shape=jax.ShapeDtypeStruct(received[0].shape, jnp.bfloat16),
        grid=(steps,),
        in_specs=[fields] + backward_specs,
        out_specs=part(early_groups),
        name="early_spectrum",
        **params(one_product, 6 << 20),
    )(total, backward, backward)
    return [early] + late


def run_place(kernel, place, pieces, out_shape):
    vmem = pl.BlockSpec(memory_space=pltpu.VMEM)
    return pl.pallas_call(
        kernel,
        out_shape=out_shape,
        in_specs=[vmem] * (1 + len(pieces)),
        out_specs=vmem,
        name="natural_order",
        **params(2 * place.shape[1] * math.prod(out_shape.shape), 8 << 20),
    )(place, *pieces)


def wave_tables(sorted_all, point_count, groups):
    half_points = point_count // 2
    late = late_share(groups)
    early = groups // 2 - late
    by_group = sorted_all.reshape(sorted_all.shape[0], groups, ORD)
    orders = []
    for p in range(2):
        begin = 2 * late + p * early
        first = by_group[:, begin : begin + early].reshape(-1, ORD)
        second = by_group[:, p * late : (p + 1) * late].reshape(-1, ORD)
        orders.append(jnp.concatenate([first, second], axis=0))
    orders = jnp.stack(orders)
    shape = (2, orders.shape[1], 2, ORD)
    depth = math.prod(shape[1:])
    shift = jnp.arange(2, dtype=jnp.int32)[:, None] * (point_count // 4)
    lane_orders = jnp.broadcast_to(orders[:, :, None], shape).reshape(2, 1, depth)
    lane_shift = jnp.broadcast_to(shift, shape).reshape(2, 1, depth)

    def angle(phase):
        return (phase % point_count).astype(jnp.float32) * (2.0 * math.pi / point_count)

    def both(phase):
        return jnp.stack([jnp.cos(angle(phase)), jnp.sin(angle(phase))])

    rows = jnp.arange(ORD, dtype=jnp.int32)[None, :, None]
    forward_base = both(lane_orders * rows + lane_shift)
    forward_turn = both(lane_orders * ORD)
    row_orders = orders.reshape(2, depth // (2 * ORD), ORD, 1)
    longitudes = jnp.arange(LANES, dtype=jnp.int32)
    angles = angle(row_orders * longitudes)
    backward_base = jnp.stack([jnp.cos(angles), -jnp.sin(angles)])
    turn_shape = (2, 2, depth // (2 * ORD), ORD, LANES)
    backward_turn = jnp.broadcast_to(both(row_orders * LANES), turn_shape)
    vmem = pl.BlockSpec(memory_space=pltpu.VMEM)
    return pl.pallas_call(
        wave_kernel,
        out_shape=(
            jax.ShapeDtypeStruct((2, half_points, depth), jnp.bfloat16),
            jax.ShapeDtypeStruct((2, depth, half_points), jnp.bfloat16),
        ),
        in_specs=[vmem] * 4,
        out_specs=(vmem, vmem),
        name="waves",
        **params(8 * depth * half_points, 12 << 20),
    )(forward_base, forward_turn, backward_base, backward_turn)


def to_blocks(gridded, cycle_local):
    blocks, comps, groups, rows, _ = gridded.shape
    share = LANES // cycle_local
    if share == 1:
        return gridded
    cut = gridded.reshape(2, blocks // 2, comps, groups, rows, share, cycle_local)
    cut = cut.transpose(0, 1, 5, 2, 3, 4, 6)
    cut = jnp.stack([cut[0], jnp.flip(cut[1], axis=1)])
    return cut.reshape(blocks * share, comps, groups, rows, cycle_local)


def from_blocks(gridded, cycle_local):
    blocks, comps, groups, rows, _ = gridded.shape
    share = LANES // cycle_local
    if share == 1:
        return gridded
    cut = gridded.reshape(2, blocks // share // 2, share, comps, groups, rows, cycle_local)
    cut = jnp.stack([cut[0], jnp.flip(cut[1], axis=1)])
    cut = cut.transpose(0, 1, 3, 4, 5, 2, 6)
    return cut.reshape(blocks // share, comps, groups, rows, LANES)


def pack_comps(gridded):
    blocks, comps, groups, rows, cycle_local = gridded.shape
    if cycle_local == LANES:
        return gridded
    side = gridded.transpose(0, 2, 3, 1, 4).reshape(blocks, 1, groups, rows, comps * cycle_local)
    extra = -(comps * cycle_local) % LANES
    return jnp.pad(side, ((0, 0),) * 4 + ((0, extra),))


def unpack_comps(gridded, comps, cycle_local):
    if cycle_local == LANES:
        return gridded
    blocks, _, groups, rows, _ = gridded.shape
    side = gridded[..., : comps * cycle_local]
    side = side.reshape(blocks, groups, rows, comps, cycle_local)
    return side.transpose(0, 3, 1, 2, 4)


def shards(strain_spec, order_map, viscosity, radial_weight):
    comps, shells, slots, parts, degrees = strain_spec.shape
    block_count = lax.axis_size("blk")
    block = lax.axis_index("blk")
    cycle_local = viscosity.shape[1]
    cycle_count = cycle_local * block_count
    half_cycles = cycle_count // 2
    points = viscosity.shape[2]
    groups = slots // ORD
    chunks = degrees // CHUNK

    rank_all = rank_orders(order_map.reshape(block_count, slots))
    sorted_all = apply_rank(order_map.reshape(block_count, slots), rank_all)
    rank = lax.dynamic_index_in_dim(rank_all, block, 0, keepdims=False)
    sorted_orders = lax.dynamic_index_in_dim(sorted_all, block, 0, keepdims=False)
    by_group = sorted_orders.reshape(groups, ORD)
    first = jnp.concatenate([by_group[:, 0], by_group[:, -1]]) // CHUNK
    order = sorted_orders.astype(jnp.float32)
    counter = jnp.arange(1, degrees, dtype=jnp.float32)
    logs = jnp.where(counter <= order[:, None], jnp.log(1.0 - 0.5 / counter), 0.0)
    starts = 0.5 * jnp.log((2.0 * order + 1.0) / (4.0 * math.pi)) + 0.5 * jnp.sum(logs, axis=1)
    order_lanes = jnp.broadcast_to(
        jnp.stack([order, starts]).reshape(2, groups, ORD, 1), (2, groups, ORD, LANES)
    )

    cycle_index = jnp.arange(half_cycles, dtype=jnp.float32)
    colatitude = math.pi * (2.0 * cycle_index + 1.0) / (2.0 * cycle_count)
    geometry = jnp.stack([2.0 * jnp.cos(colatitude), jnp.log(jnp.sin(colatitude))])

    row_rank = rank // ORD * (2 * ORD) + rank % ORD
    row_rank = (row_rank[:, None] + ORD * jnp.arange(2, dtype=jnp.int32)).reshape(-1)
    place = jnp.arange(slots * 2, dtype=jnp.int32)
    hit = row_rank[None, :] == place[:, None]
    my_orders = lax.dynamic_index_in_dim(
        order_map.reshape(block_count, slots), block, 0, keepdims=False
    )
    doubling = jnp.repeat(jnp.where(my_orders == 0, 1.0, 2.0), 2)
    place_in = jnp.where(hit, doubling[None, :], 0.0).astype(jnp.bfloat16)
    place_out = hit.T.astype(jnp.bfloat16)

    spectra = strain_spec.reshape(comps, slots * parts, degrees)
    late = late_share(groups)
    spans = [(2 * late, groups - 2 * late)] + ([(0, 2 * late)] if late else [])
    received, tables = [], []
    for base, count in spans:
        gridded, table, kappa = run_synth(
            first, spectra, place_in, order_lanes, geometry, chunks, base, count
        )
        tables.append((table, kappa))
        arrived = lax.all_to_all(to_blocks(gridded, cycle_local), "blk", 0, 0, tiled=True)
        received.append(pack_comps(arrived))

    forward, backward = wave_tables(sorted_all, points, groups)
    weights = fejer_weights(cycle_count)[None, :]
    gather = gather_matrix()
    forward, weights, gather = lax.optimization_barrier((forward, weights, gather))
    mirror = jnp.arange(cycle_local, dtype=jnp.int32)
    mirror = jnp.where(block * 2 < block_count, mirror, cycle_local - 1 - mirror)
    turn = (mirror[None, :] == jnp.arange(cycle_local, dtype=jnp.int32)[:, None]).astype(jnp.float32)
    local = jnp.einsum("jk,ji->ki", viscosity[0], turn, precision=lax.Precision.HIGHEST)
    if cycle_local < LANES:
        local = jnp.concatenate([local] * comps, axis=1)
        local = jnp.pad(local, ((0, 0), (0, -local.shape[1] % LANES)))
    spectrum = run_grid(received, forward, backward, local, 2.0 * math.pi / points)
    returned = [
        lax.all_to_all(unpack_comps(piece, comps, cycle_local), "blk", 0, 0, tiled=True)
        for piece in spectrum
    ]

    shell_count = lax.axis_size("shell")
    ordered, offsets, integrated = [], [], []
    sum_type = jax.ShapeDtypeStruct((comps, slots * parts, degrees // shell_count), jnp.float32)
    for i in reversed(range(len(spans))):
        base = spans[i][0]
        table, kappa = tables[i]
        coefs, weighted = run_analysis(
            first,
            radial_weight,
            from_blocks(returned[i], cycle_local),
            table,
            kappa,
            gather,
            weights,
            shell_count,
            base,
        )
        ordered.append(coefs)
        offsets.append(base * 2 * ORD)
        shared = lax.all_to_all(weighted, "shell", 0, 0, tiled=True)
        kernel = functools.partial(shell_sum_kernel, offsets[-1])
        integrated = [run_place(kernel, place_out, [shared] + integrated, sum_type)]
    stress = run_place(
        functools.partial(unsort_kernel, offsets),
        place_out,
        ordered,
        jax.ShapeDtypeStruct((comps, slots * parts, degrees), jnp.bfloat16),
    )
    integrated = integrated[0]
    stress_spec = stress.reshape(strain_spec.shape)
    return (stress_spec, integrated.reshape(comps, slots, parts, degrees // shell_count))


def solution(mesh):
    return jax.shard_map(
        shards,
        mesh=mesh,
        in_specs=(P(None, "shell", "blk", None, None), P(), P("shell", "blk", None), P("shell")),
        out_specs=(P(None, "shell", "blk", None, None), P(None, "blk", None, "shell")),
        check_vma=False,
    )
```
